256 devices in a mesh: tok: 32 (over z, y), voc: 8 (over x, core).
Axes of the slice: x: 4, y: 4, z: 8, core: 2. Of those that a mesh axis runs over, the one named last changes fastest.
Arguments:
- student_hidden: bfloat16 [2048, 2048], P('tok'), may hold values from -7.5 to 7.5
- learner_projection_weights: bfloat16 [2048, 131072], P(None, ('voc', 'tok')), may hold values from -0.41984465 to 0.41984465
- mentor_unscaled_scores: bfloat16 [2048, 131072], P('tok', 'voc'), may hold values from -20 to 480
- token_teacher_row: int32 [2048], replicated, may hold values from 0 to 2047, as said below
- sequence_length_list: int32 [8], replicated, may hold values from 1 to 512, 2048 in all
Outputs:
- distill_objective: float32 [], replicated
- grad_hidden: bfloat16 [2048, 2048], P(('tok', 'voc'))
- grad_weight: bfloat16 [2048, 131072], P(None, ('voc', 'tok'))
The draws below stay inside these ranges and needn't reach their ends.
Inputs may be any that keep to these rules, and one draw needn't show every extreme that they name: student token s takes the teacher's row token_teacher_row[s]; every row is taken once. `sequence_length_list`: the 8 sequences fill all 2048 tokens.
All inputs are finite; a program needn't handle non-finite values.
Results may differ from the reference program's by a relative error of at most 0.007.
Values may be sent and summed in bfloat16 or wider, within the bound.
A program may use at most 128 MiB of HBM per device.

```python
import math
import jax
import jax.numpy as jnp
import numpy as np
from jax import lax

D = 2048
BUNDLED_TEXTS = 8
SPAN_POSITIONS = 2048
VOCAB = 131072
MOST_LEN = 512


aligned_count = 6


def drawn_pairs(key):
    base = jax.random.fold_in(key, 7)
    key_cols, key_signs, key_rows, key_order = jax.random.split(base, 4)
    columns = jax.random.permutation(key_cols, VOCAB)[:2 * aligned_count].reshape(aligned_count, 2)
    signs = (2 * jax.random.randint(key_signs, (aligned_count, D), 0, 2) - 1).astype(jnp.float32)
    picked = jax.random.permutation(key_rows, SPAN_POSITIONS)[:aligned_count]
    order = jax.random.permutation(key_order, SPAN_POSITIONS)
    return (columns, signs, picked, order)


def peak_levels():
    return jnp.array([120.0, 180.0, 240.0, 120.0, 180.0, 240.0], jnp.float32)


def alternating_signs():
    return jnp.where(jnp.arange(D) % 2 == 0, 1.0, -1.0).astype(jnp.float32)


def draw_token_teacher_row(key, part):
    columns, signs, picked, order = drawn_pairs(key)
    return order.astype(jnp.int32)


def draw_learner_projection_weights(key, part):
    columns, signs, picked, order = drawn_pairs(key)
    key = jax.random.fold_in(key, 11)
    spread = 3.0 / math.sqrt(D)
    values = jax.random.truncated_normal(key, -6.0, 6.0, (D, VOCAB), jnp.float32) * spread
    tip = 128.0 / D
    first = (signs * tip).T
    second = (signs * alternating_signs()[None, :] * tip).T
    values = values.at[:, columns[:, 0]].set(first)
    values = values.at[:, columns[:, 1]].set(second)
    return values.astype(jnp.bfloat16)


def draw_student_hidden(key, part):
    columns, signs, picked, order = drawn_pairs(key)
    key = jax.random.fold_in(key, 13)
    key_base = jax.random.fold_in(key, 0)
    values = jax.random.truncated_normal(key_base, -6.0, 6.0, (SPAN_POSITIONS, D), jnp.float32)
    levels = peak_levels()
    beta_one = levels / 64.0
    beta_two = (levels - 2.0) / 64.0
    aligned = signs * (beta_one[:, None] + beta_two[:, None] * alternating_signs()[None, :])
    values = values.at[picked].set(aligned)
    return values.astype(jnp.bfloat16)


def draw_mentor_unscaled_scores(key, part):
    columns, signs, picked, order = drawn_pairs(key)
    key = jax.random.fold_in(key, 17)
    key_base = jax.random.fold_in(key, 0)
    values = jax.random.truncated_normal(key_base, -6.0, 6.0, (SPAN_POSITIONS, VOCAB), jnp.float32) * 3.0
    teacher_rows = order[picked]
    highest = 2.0 * peak_levels()
    values = values.at[teacher_rows, columns[:, 0]].set(highest)
    values = values.at[teacher_rows, columns[:, 1]].set(highest - 4.0)
    return values.astype(jnp.bfloat16)


def length_profile(count, total, bound, skew):
    loads = [(1 << 20) // math.isqrt(grade ** skew) + 1 for grade in range(2, count + 1)]
    rest, holding = total - bound - (count - 1), [1] * (count - 1)
    while rest > 0:
        free = [i for i in range(count - 1) if holding[i] < bound]
        pool, left = sum([loads[i] for i in free]), rest
        for i in free:
            extra = min(bound - holding[i], max(1, left * loads[i] // pool), rest)
            holding[i] = holding[i] + extra
            rest = rest - extra
    return np.array([bound] + holding)


def uneven_parts(rng, amount, total, limit, lean):
    if amount == 2:
        one = jax.random.randint(rng, (), max(1, total - limit), min(limit, total - 1) + 1)
        return jnp.stack([one, total - one])
    sizes = jnp.asarray(length_profile(amount, total, limit, lean), jnp.int32)
    pairs = (amount - 1) // 2
    giver, taker = sizes[1:1 + 2 * pairs:2], sizes[2:2 + 2 * pairs:2]
    room = jnp.minimum(giver - 1, limit - taker)
    passed = jax.random.randint(jax.random.fold_in(rng, 1), (pairs,), 0, 1 << 20) % (room + 1)
    sizes = sizes.at[1:1 + 2 * pairs:2].set(giver - passed).at[2:2 + 2 * pairs:2].set(taker + passed)
    return sizes[jax.random.permutation(jax.random.fold_in(rng, 2), amount)]


def setup_inputs(seed: int = 0) -> dict:
    streams_of = jax.random.split(jax.random.key(seed), 6)
    student_hidden = draw_student_hidden(jax.random.fold_in(streams_of[5], 71), 0)
    learner_projection_weights = draw_learner_projection_weights(jax.random.fold_in(streams_of[5], 71), 0)
    mentor_unscaled_scores = draw_mentor_unscaled_scores(jax.random.fold_in(streams_of[5], 71), 0)
    token_teacher_row = draw_token_teacher_row(jax.random.fold_in(streams_of[5], 71), 0)
    sequence_length_list = uneven_parts(streams_of[4], BUNDLED_TEXTS, SPAN_POSITIONS, MOST_LEN, 1).astype(jnp.int32)
    return dict(student_hidden=student_hidden, learner_projection_weights=learner_projection_weights, mentor_unscaled_scores=mentor_unscaled_scores, token_teacher_row=token_teacher_row, sequence_length_list=sequence_length_list)


smoothing_divisor = 2.0
objective_scaling = 512.0


def token_valid(sequence_length_list, total):
    ends = jnp.cumsum(sequence_length_list).astype(jnp.int32) - 1
    places = jnp.arange(total, dtype=jnp.int32)
    hits = jnp.sum((places[:, None] == ends[None, :]).astype(jnp.float32), axis=1)
    return 1.0 - hits


def reference(student_hidden, learner_projection_weights, mentor_unscaled_scores, token_teacher_row, sequence_length_list):
    usable_indicator = token_valid(sequence_length_list, SPAN_POSITIONS)
    block = math.gcd(SPAN_POSITIONS, 256)
    hidden_blocks = student_hidden.reshape(SPAN_POSITIONS // block, block, D)
    perm_blocks = token_teacher_row.reshape(SPAN_POSITIONS // block, block)
    valid_blocks = usable_indicator.reshape(SPAN_POSITIONS // block, block)

    def one_block(items):
        shard_activation_entries, selected_positions, retention_indicator = items
        learner_scores = jnp.dot(shard_activation_entries, learner_projection_weights, preferred_element_type=jnp.float32) / smoothing_divisor
        mentor_reordered_scores = jnp.take(mentor_unscaled_scores, selected_positions, axis=0).astype(jnp.float32) / smoothing_divisor
        learner_logarithmic_likelihoods = jax.nn.log_softmax(learner_scores, axis=-1)
        log_teacher = jax.nn.log_softmax(mentor_reordered_scores, axis=-1)
        mentor_distribution = jnp.exp(log_teacher)
        kullback_leibler_term = jnp.sum(mentor_distribution * (log_teacher - learner_logarithmic_likelihoods), axis=-1)
        derivative_routine = objective_scaling * smoothing_divisor * retention_indicator[:, None] * (jnp.exp(learner_logarithmic_likelihoods) - mentor_distribution)
        return kullback_leibler_term, derivative_routine.astype(jnp.bfloat16)

    kullback_leibler_term, grad_logits = lax.map(one_block, (hidden_blocks, perm_blocks, valid_blocks))
    kullback_leibler_term = kullback_leibler_term.reshape(SPAN_POSITIONS)
    grad_logits = grad_logits.reshape(SPAN_POSITIONS, VOCAB)
    distill_objective = smoothing_divisor * smoothing_divisor * jnp.sum(usable_indicator * kullback_leibler_term) / (SPAN_POSITIONS - BUNDLED_TEXTS)
    grad_weight = jnp.dot(student_hidden.T, grad_logits, preferred_element_type=jnp.float32).astype(jnp.bfloat16)
    grad_hidden = jnp.dot(grad_logits, learner_projection_weights.T, preferred_element_type=jnp.float32).astype(jnp.bfloat16)
    return (distill_objective, grad_hidden, grad_weight)
```

```python
import functools

import jax
import jax.numpy as jnp
from jax import lax
from jax.experimental import pallas as pl
from jax.experimental.pallas import tpu as pltpu
from jax.sharding import PartitionSpec as P

MESH = pl.DeviceIdType.MESH
F32 = jnp.float32
BF16 = jnp.bfloat16
TEMPERATURE = 2.0
SCALE = 512.0
LANES = 128


def mod(a, n):
    return lax.rem(a, n)


def kernel(
    dims,
    hidden,
    weights,
    mentor,
    rows,
    lengths,
    loss_out,
    grad_hidden,
    grad_weight,
    gathered,
    teacher,
    picks,
    scores,
    slope,
    mate_send,
    mate_recv,
    own_half,
    folded,
    first_a,
    first_b,
    second_a,
    second_b,
    got_a,
    got_b,
    last,
    final,
    final_recv,
    stat_voc,
    stat_y,
    stat_z,
    loss_voc,
    loss_y,
    loss_z,
    local_sem,
    s1_sem,
    t_sem,
    s2a_sem,
    s2b_sem,
    s3a_sem,
    s3b_sem,
    ca_sem,
    cb_sem,
    stat_voc_sem,
    stat_y_sem,
    stat_z_sem,
    loss_voc_sem,
    loss_y_sem,
    loss_z_sem,
    mate_sem,
    r1a_sem,
    r1b_sem,
    r2a_sem,
    r2b_sem,
    r3_sem,
    final_sem,
):
    Z, Y, X, R, V, D = dims
    tok, voc = lax.axis_index("tok"), lax.axis_index("voc")
    z, y = tok // Y, mod(tok, Y)
    x, core = voc // 2, mod(voc, 2)
    NT, NV = Z * Y, X * 2
    CH = Y * R
    N = Z * CH
    HALF = D // 2
    QUARTER = D // 4
    CS = D // NV
    CP = CS // 2
    nb = max(1, CH // LANES)
    q = CH // nb

    def at(dz=0, dy=0, dx=0, dc=0):
        return (
            mod(z + dz, Z) * Y + mod(y + dy, Y),
            mod(x + dx, X) * 2 + mod(core + dc, 2),
        )

    def copy(src, dst, sems, index, device):
        return pltpu.make_async_remote_copy(
            src_ref=src,
            dst_ref=dst,
            send_sem=sems.at[0, index],
            recv_sem=sems.at[1, index],
            device_id=device,
            device_id_type=MESH,
        )

    def each(n, body, start=0):
        def step(i, carry):
            body(i)
            return carry

        lax.fori_loop(start, n, step, 0)

    barrier = pltpu.get_barrier_semaphore()

    def greet_tok(i):
        pl.semaphore_signal(barrier, inc=1, device_id=at(dz=i // Y, dy=mod(i, Y)), device_id_type=MESH)

    def greet_voc(i):
        pl.semaphore_signal(barrier, inc=1, device_id=at(dx=i // 2, dc=mod(i, 2)), device_id_type=MESH)

    each(NT, greet_tok, 1)
    each(NV, greet_voc, 1)
    pl.semaphore_wait(barrier, NT - 1 + NV - 1)

    def s1(i):
        return copy(
            hidden.at[:, pl.ds(pl.multiple_of(voc * CS, CS), CS)],
            gathered.at[x, core, z, y],
            s1_sem,
            i,
            at(dz=i),
        )

    each(Z, lambda i: s1(i).start(), 1)
    own_columns = pltpu.make_async_copy(
        hidden.at[:, pl.ds(pl.multiple_of(voc * CS, CS), CS)],
        gathered.at[x, core, z, y],
        local_sem.at[0],
    )
    own_columns.start()

    def t_copy(i):
        device = at(dz=i // Y, dy=mod(i, Y))
        return copy(
            mentor.at[:, pl.ds(pl.multiple_of(device[0] * V, V), V)],
            teacher.at[pl.ds(pl.multiple_of(tok * R, R), R), :],
            t_sem,
            i,
            device,
        )

    each(NT, lambda i: t_copy(i).start(), 1)
    own_block = pltpu.make_async_copy(
        mentor.at[:, pl.ds(pl.multiple_of(tok * V, V), V)],
        teacher.at[pl.ds(pl.multiple_of(tok * R, R), R), :],
        local_sem.at[1],
    )
    own_block.start()

    eye = lax.broadcasted_iota(jnp.int32, (q, LANES), 0) == lax.broadcasted_iota(
        jnp.int32, (q, LANES), 1
    )
    eye_rows = lax.broadcasted_iota(jnp.int32, (R, LANES), 0) == lax.broadcasted_iota(
        jnp.int32, (R, LANES), 1
    )

    def columns_of(i):
        return mentor[:, pl.ds(pl.multiple_of(i * V, V), V)].astype(F32) / TEMPERATURE

    def fold(op, value):
        total = value[:, :LANES]
        for j in range(1, V // LANES):
            total = op(total, value[:, j * LANES : (j + 1) * LANES])
        return total

    top_t = lax.fori_loop(
        0,
        NT,
        lambda i, m: jnp.maximum(m, fold(jnp.maximum, columns_of(i))),
        jnp.full((R, LANES), -jnp.inf, F32),
    )
    top_t = jnp.max(top_t, axis=1, keepdims=True)
    sum_t = lax.fori_loop(
        0,
        NT,
        lambda i, s: s + fold(jnp.add, jnp.exp(columns_of(i) - top_t)),
        jnp.zeros((R, LANES), F32),
    )
    sum_t = jnp.sum(sum_t, axis=1, keepdims=True)

    def to_lanes(column, mask):
        return jnp.sum(jnp.where(mask, column, 0.0), axis=0, keepdims=True)

    stat_voc[voc, Z] = jnp.concatenate(
        [to_lanes(top_t, eye_rows), to_lanes(sum_t, eye_rows), jnp.zeros((6, LANES), F32)], axis=0
    )

    def fill_picks(k):
        here = pl.ds(pl.multiple_of(k * CH, CH), CH)
        wanted = rows[here, :]
        places = lax.broadcasted_iota(jnp.int32, (CH, N), 1)
        picks[here, :] = jnp.where(places == wanted, 1.0, 0.0).astype(BF16)

    each(Z, fill_picks)

    own_columns.wait()
    each(Z, lambda i: s1(i).wait(), 1)
    first, second = pl.ds(0, CP), pl.ds(CP, CP)

    def s2a(i):
        block = gathered.at[x, core, :, y, :, first]
        return copy(block, block, s2a_sem, i, at(dy=i))

    def s2b(i):
        block = gathered.at[x, core, :, y, :, second]
        return copy(block, block, s2b_sem, i, at(dx=i))

    each(Y, lambda i: s2a(i).start(), 1)
    each(X, lambda i: s2b(i).start(), 1)

    def s3a(i):
        block = gathered.at[x, core, :, :, :, first]
        return copy(block, block, s3a_sem, i, at(dx=i))

    def s3b(i):
        block = gathered.at[:, core, :, y, :, second]
        return copy(block, block, s3b_sem, i, at(dy=i))

    def ca(i):
        block = gathered.at[mod(x + X - i, X), core, :, :, :, first]
        return copy(block, block, ca_sem, i, at(dc=1))

    def cb(i):
        block = gathered.at[:, core, :, mod(y + Y - i, Y), :, second]
        return copy(block, block, cb_sem, i, at(dc=1))

    each(Y, lambda i: s2a(i).wait(), 1)
    each(X, lambda i: s3a(i).start(), 1)
    each(X, lambda i: s2b(i).wait(), 1)
    each(Y, lambda i: s3b(i).start(), 1)
    ca(0).start()
    cb(0).start()

    def on_x(i):
        s3a(i).wait()
        ca(i).start()

    def on_y(i):
        s3b(i).wait()
        cb(i).start()

    each(X, on_x, 1)
    each(Y, on_y, 1)
    each(X, lambda i: ca(i).wait())
    each(Y, lambda i: cb(i).wait())

    def hidden_of(b, k):
        return gathered[b // 2, b % 2, k].reshape(CH, CS)

    def score(k):
        here = pl.ds(pl.multiple_of(k * CH, CH), CH)
        wide = jnp.concatenate([hidden_of(b, k) for b in range(NV)], axis=1)
        value = jnp.dot(wide, weights[...], preferred_element_type=F32) / TEMPERATURE
        scores[here, :] = value
        top = jnp.max(value, axis=1, keepdims=True)
        total = jnp.sum(jnp.exp(value - top), axis=1, keepdims=True)
        parts = [to_lanes(top[j * q : (j + 1) * q], eye) for j in range(nb)]
        parts += [to_lanes(total[j * q : (j + 1) * q], eye) for j in range(nb)]
        parts.append(jnp.zeros((8 - 2 * nb, LANES), F32))
        stat_voc[voc, k] = jnp.concatenate(parts, axis=0)

    each(Z, score)

    def stage(buf, sems, slot, n, target, count=None):
        def c(i):
            block = buf.at[slot] if count is None else buf.at[slot, pl.ds(0, count)]
            return copy(block, block, sems, i, target(i))

        each(n, lambda i: c(i).start(), 1)
        each(n, lambda i: c(i).wait(), 1)

    def combine(buf, n, first_row, width, count):
        tops = [buf[j, :count, first_row : first_row + width] for j in range(n)]
        sums = [buf[j, :count, first_row + width : first_row + 2 * width] for j in range(n)]
        top = functools.reduce(jnp.maximum, tops)
        total = functools.reduce(jnp.add, [s * jnp.exp(m - top) for s, m in zip(sums, tops)])
        return top, total

    def pack(top, total):
        return jnp.concatenate([top, total, jnp.zeros((Z, 8 - 2 * nb, LANES), F32)], axis=1)

    stage(stat_voc, stat_voc_sem, voc, NV, lambda i: at(dx=i // 2, dc=mod(i, 2)))
    top_s, sum_s = combine(stat_voc, NV, 0, nb, Z)
    stat_y[y, :Z] = pack(top_s, sum_s)
    tops = [stat_voc[j, Z, 0:1] for j in range(NV)]
    sums = [stat_voc[j, Z, 1:2] for j in range(NV)]
    top_t = functools.reduce(jnp.maximum, tops)
    sum_t = functools.reduce(jnp.add, [s * jnp.exp(m - top_t) for s, m in zip(sums, tops)])
    used = lax.broadcasted_iota(jnp.int32, (1, LANES), 1) < R
    sum_t = jnp.where(used, sum_t, 1.0)
    stat_y[y, Z] = jnp.concatenate([top_t, jnp.log(sum_t), jnp.zeros((6, LANES), F32)], axis=0)

    stage(stat_y, stat_y_sem, y, Y, lambda i: at(dy=i))
    top_s, sum_s = combine(stat_y, Y, 0, nb, Z)
    stat_z[z, :Z] = pack(top_s, sum_s)
    for j in range(Y):
        stat_z[z, Z + j] = stat_y[j, Z]

    stage(stat_z, stat_z_sem, z, Z, lambda i: at(dz=i))
    top_s, sum_s = combine(stat_z, Z, 0, nb, Z)
    if q < LANES:
        sum_s = jnp.where(lax.broadcasted_iota(jnp.int32, sum_s.shape, 2) < q, sum_s, 1.0)
    stat_voc[0, :Z] = pack(top_s, jnp.log(sum_s))
    table_top = jnp.concatenate(
        [stat_z[i, Z + j, 0:1] for i in range(Z) for j in range(Y)], axis=0
    ).astype(BF16)
    table_log = jnp.concatenate(
        [stat_z[i, Z + j, 1:2] for i in range(Z) for j in range(Y)], axis=0
    )
    log_hi = table_log.astype(BF16)
    rest = table_log - log_hi.astype(F32)
    log_mid = rest.astype(BF16)
    log_lo = (rest - log_mid.astype(F32)).astype(BF16)

    ends = []
    total = jnp.int32(0)
    for j in range(lengths.shape[0]):
        total = total + lengths[j]
        ends.append(total - 1)

    own_block.wait()
    each(NT, lambda i: t_copy(i).wait(), 1)

    def mate(k):
        return copy(mate_send.at[k], mate_recv.at[k], mate_sem, k, at(dc=1))

    def r1a(k, i):
        return copy(
            folded.at[k, :, mod(x + i, X), :, pl.ds(0, QUARTER)],
            first_a.at[k, i - 1],
            r1a_sem,
            k * X + i,
            at(dx=i),
        )

    def r1b(k, i):
        return copy(
            folded.at[k, mod(y + i, Y), :, :, pl.ds(QUARTER, QUARTER)],
            first_b.at[k, i - 1],
            r1b_sem,
            k * Y + i,
            at(dy=i),
        )

    def gradient(k, acc):
        zc = mod(z + 1 + k, Z)
        here = pl.ds(pl.multiple_of(zc * CH, CH), CH)
        wanted = rows[here, :]
        block = wanted // R
        pick = (lax.broadcasted_iota(jnp.int32, (CH, NT), 1) == block).astype(F32).astype(BF16)
        lane = lax.broadcasted_iota(jnp.int32, (CH, LANES), 1) == (wanted - block * R)

        def take(table):
            return jnp.dot(pick, table, preferred_element_type=F32)

        def one(value):
            return jnp.sum(jnp.where(lane, value, 0.0), axis=1, keepdims=True)

        teacher_top = one(take(table_top))
        teacher_log = one(take(log_hi) + take(log_mid) + take(log_lo))
        stats = stat_voc[0, zc]

        def to_column(row):
            return jnp.sum(jnp.where(eye, row, 0.0), axis=1, keepdims=True)

        student_top = jnp.concatenate([to_column(stats[j : j + 1]) for j in range(nb)], axis=0)
        student_log = jnp.concatenate(
            [to_column(stats[nb + j : nb + j + 1]) for j in range(nb)], axis=0
        )
        place = lax.broadcasted_iota(jnp.int32, (CH, 1), 0) + zc * CH
        valid = jnp.ones((CH, 1), F32)
        for end in ends:
            valid = jnp.where(place == end, 0.0, valid)
        taken = jnp.dot(picks[here, :], teacher[...], preferred_element_type=F32) / TEMPERATURE
        log_teacher = (taken - teacher_top) - teacher_log
        log_student = (scores[here, :] - student_top) - student_log
        p_teacher = jnp.exp(log_teacher)
        p_student = jnp.exp(log_student)
        kl = jnp.sum(p_teacher * (log_teacher - log_student), axis=1, keepdims=True)
        grad = ((SCALE * TEMPERATURE) * valid * (p_student - p_teacher)).astype(BF16)
        slope[here, :] = grad

        def product(c):
            return lax.dot_general(
                grad,
                weights[pl.ds(pl.multiple_of(c * HALF, HALF), HALF), :],
                (((1,), (1,)), ((), ())),
                preferred_element_type=F32,
            )

        mate_send[k] = product(1 - core).astype(BF16)
        mate(k).start()
        own_half[mod(k, 2)] = product(core)
        return acc + jnp.sum(valid * kl, axis=0, keepdims=True)

    def fold_mate(k):
        mate(k).wait()
        value = own_half[mod(k, 2)] + mate_recv[k].astype(F32)
        folded[k] = value.astype(BF16).reshape(Y, X, 16, HALF)
        each(X, lambda i: r1a(k, i).start(), 1)
        each(Y, lambda i: r1b(k, i).start(), 1)

    acc = gradient(0, jnp.zeros((1, 1), F32))

    def forward(k, acc):
        acc = gradient(k, acc)
        fold_mate(k - 1)
        return acc

    acc = lax.fori_loop(1, Z, forward, acc)
    fold_mate(Z - 1)

    loss_voc[voc] = jnp.broadcast_to(acc, (8, LANES))
    stage(loss_voc, loss_voc_sem, voc, NV, lambda i: at(dx=i // 2, dc=mod(i, 2)))
    loss_y[y] = functools.reduce(jnp.add, [loss_voc[j] for j in range(NV)])
    stage(loss_y, loss_y_sem, y, Y, lambda i: at(dy=i))
    loss_z[z] = functools.reduce(jnp.add, [loss_y[j] for j in range(Y)])
    stage(loss_z, loss_z_sem, z, Z, lambda i: at(dz=i))
    loss = functools.reduce(jnp.add, [loss_z[j] for j in range(Z)])
    loss_out[...] = TEMPERATURE * TEMPERATURE * loss / (N - lengths.shape[0])

    def weight_part(b):
        wide = gathered[b // 2, mod(b, 2)].reshape(N, CS)
        value = lax.dot_general(
            wide, slope[...], (((0,), (0,)), ((), ())), preferred_element_type=F32
        )
        grad_weight[pl.ds(pl.multiple_of(b * CS, CS), CS), :] = value.astype(BF16)

    def r2a(k, i):
        return copy(
            second_a.at[k, mod(y + i, Y)], got_a.at[k, i - 1], r2a_sem, k * Y + i, at(dy=i)
        )

    def r2b(k, i):
        return copy(
            second_b.at[k, mod(x + i, X)], got_b.at[k, i - 1], r2b_sem, k * X + i, at(dx=i)
        )

    def fold_first(k):
        each(X, lambda i: r1a(k, i).wait(), 1)
        value = folded[k, :, x, :, :QUARTER].astype(F32)
        for i in range(X - 1):
            value = value + first_a[k, i].astype(F32)
        second_a[k] = value.astype(BF16)
        each(Y, lambda i: r2a(k, i).start(), 1)
        each(Y, lambda i: r1b(k, i).wait(), 1)
        value = folded[k, y, :, :, QUARTER:].astype(F32)
        for i in range(Y - 1):
            value = value + first_b[k, i].astype(F32)
        second_b[k] = value.astype(BF16)
        each(X, lambda i: r2b(k, i).start(), 1)

    def fold_second(k):
        each(Y, lambda i: r2a(k, i).wait(), 1)
        each(X, lambda i: r2b(k, i).wait(), 1)
        left = second_a[k, y].astype(F32)
        for i in range(Y - 1):
            left = left + got_a[k, i].astype(F32)
        right = second_b[k, x].astype(F32)
        for i in range(X - 1):
            right = right + got_b[k, i].astype(F32)
        last[0, k] = jnp.concatenate([left, right], axis=1).astype(BF16)

    def r3(k):
        return copy(last.at[0, k], last.at[1, k], r3_sem, k, at(dz=k + 1))

    weight_part(0)
    fold_first(0)

    def backward(k):
        weight_part(k)
        fold_first(k)
        fold_second(k - 1)
        r3(k - 1).start()

    each(Z, backward, 1)
    fold_second(Z - 1)
    each(Z - 1, lambda k: r3(k).wait())
    value = last[0, Z - 1].astype(F32)
    for k in range(Z - 1):
        value = value + last[1, k].astype(F32)
    final[...] = value
    swap = copy(final.at[pl.ds(pl.multiple_of((1 - core) * 8, 8), 8), :], final_recv, final_sem, 0, at(dc=1))
    swap.start()
    mine = jnp.where(core == 0, value[:8], value[8:])
    swap.wait()
    theirs = final_recv[...]
    grad_hidden[:, :HALF] = jnp.where(core == 0, mine, theirs).astype(BF16)
    grad_hidden[:, HALF:] = jnp.where(core == 0, theirs, mine).astype(BF16)


def body(dims, hidden, weights, mentor, rows, lengths):
    Z, Y, X, R, V, D = dims
    NT, NV, CH = Z * Y, X * 2, Y * R
    N, HALF, QUARTER, CS = Z * CH, D // 2, D // 4, D // NV
    vmem = pl.BlockSpec(memory_space=pltpu.VMEM)
    dma = lambda n: pltpu.SemaphoreType.DMA((2, n))
    loss, grad_hidden, grad_weight = pl.pallas_call(
        functools.partial(kernel, dims),
        out_shape=(
            jax.ShapeDtypeStruct((8, LANES), F32),
            jax.ShapeDtypeStruct((8, D), BF16),
            jax.ShapeDtypeStruct((D, V), BF16),
        ),
        in_specs=[vmem, vmem, vmem, vmem, pl.BlockSpec(memory_space=pltpu.SMEM)],
        out_specs=(vmem, vmem, vmem),
        scratch_shapes=[
            pltpu.VMEM((X, 2, Z, Y, R, CS), BF16),
            pltpu.VMEM((N, V), BF16),
            pltpu.VMEM((N, N), BF16),
            pltpu.VMEM((N, V), F32),
            pltpu.VMEM((N, V), BF16),
            pltpu.VMEM((Z, CH, HALF), BF16),
            pltpu.VMEM((Z, CH, HALF), BF16),
            pltpu.VMEM((2, CH, HALF), F32),
            pltpu.VMEM((Z, Y, X, 16, HALF), BF16),
            pltpu.VMEM((Z, X - 1, Y, 16, QUARTER), BF16),
            pltpu.VMEM((Z, Y - 1, X, 16, QUARTER), BF16),
            pltpu.VMEM((Z, Y, 16, QUARTER), BF16),
            pltpu.VMEM((Z, X, 16, QUARTER), BF16),
            pltpu.VMEM((Z, Y - 1, 16, QUARTER), BF16),
            pltpu.VMEM((Z, X - 1, 16, QUARTER), BF16),
            pltpu.VMEM((2, Z, 16, HALF), BF16),
            pltpu.VMEM((16, HALF), F32),
            pltpu.VMEM((8, HALF), F32),
            pltpu.VMEM((NV, Z + 1, 8, LANES), F32),
            pltpu.VMEM((Y, Z + 1, 8, LANES), F32),
            pltpu.VMEM((Z, Z + Y, 8, LANES), F32),
            pltpu.VMEM((NV, 8, LANES), F32),
            pltpu.VMEM((Y, 8, LANES), F32),
            pltpu.VMEM((Z, 8, LANES), F32),
            pltpu.SemaphoreType.DMA((2,)),
            dma(Z),
            dma(NT),
            dma(Y),
            dma(X),
            dma(X),
            dma(Y),
            dma(X),
            dma(Y),
            dma(NV),
            dma(Y),
            dma(Z),
            dma(NV),
            dma(Y),
            dma(Z),
            dma(Z),
            dma(Z * X),
            dma(Z * Y),
            dma(Z * Y),
            dma(Z * X),
            dma(Z),
            dma(1),
        ],
        compiler_params=pltpu.CompilerParams(
            collective_id=0, has_side_effects=True, vmem_limit_bytes=63 * 2**20
        ),
    )(hidden, weights, mentor, rows[:, None], lengths)
    return loss[0, 0], grad_hidden, grad_weight


def solution(mesh):
    NT, NV = mesh.shape["tok"], mesh.shape["voc"]
    Y = 1 << ((NT.bit_length() - 1) // 2)
    Z, X = NT // Y, NV // 2

    def run(hidden, weights, mentor, rows, lengths):
        N, D = hidden.shape
        dims = (Z, Y, X, N // NT, weights.shape[1] // (NT * NV), D)
        return jax.shard_map(
            functools.partial(body, dims),
            mesh=mesh,
            in_specs=(P("tok", None), P(None, ("voc", "tok")), P("tok", "voc"), P(), P()),
            out_specs=(P(), P(("tok", "voc"), None), P(None, ("voc", "tok"))),
            check_vma=False,
        )(hidden, weights, mentor, rows, lengths)

    return run
```

```python
import functools

import jax
import jax.numpy as jnp
from jax import lax
from jax.experimental import pallas as pl
from jax.experimental.pallas import tpu as pltpu
from jax.sharding import PartitionSpec as P

MESH = pl.DeviceIdType.MESH
F32 = jnp.float32
BF16 = jnp.bfloat16
TEMPERATURE = 2.0
SCALE = 512.0
LANES = 128


def mod(a, n):
    return lax.rem(a, n)


def kernel(
    dims,
    hidden,
    weights_hbm,
    mentor_hbm,
    rows,
    lengths,
    loss_out,
    grad_hidden,
    grad_weight,
    weights,
    mentor,
    wanted_rows,
    gathered,
    teacher,
    picks,
    scores,
    slope,
    mate_send,
    mate_recv,
    own_half,
    folded,
    first_a,
    first_b,
    second_a,
    second_b,
    got_a,
    got_b,
    last,
    final,
    final_recv,
    stat_voc,
    stat_y,
    stat_z,
    mentor_voc,
    mentor_y,
    mentor_z,
    loss_voc,
    loss_y,
    loss_z,
    local_sem,
    s1_sem,
    t_sem,
    s2a_sem,
    s2b_sem,
    s3a_sem,
    s3b_sem,
    c_sem,
    stat_voc_sem,
    stat_y_sem,
    stat_z_sem,
    mentor_voc_sem,
    mentor_y_sem,
    mentor_z_sem,
    loss_voc_sem,
    loss_y_sem,
    loss_z_sem,
    mate_sem,
    r1a_sem,
    r1b_sem,
    r2a_sem,
    r2b_sem,
    r3_sem,
    final_sem,
):
    Z, Y, X, R, V, D = dims
    tok, voc = lax.axis_index("tok"), lax.axis_index("voc")
    z, y = tok // Y, mod(tok, Y)
    x, core = voc // 2, mod(voc, 2)
    NT, NV = Z * Y, X * 2
    CH = Y * R
    N = Z * CH
    HALF = D // 2
    QUARTER = D // 4
    CS = D // NV
    CP = CS // 2
    nb = max(1, CH // LANES)
    q = CH // nb
    per_tile = 8 // nb
    tiles = max(1, Z // per_tile)

    def at(dz=0, dy=0, dx=0, dc=0):
        return (
            mod(z + dz, Z) * Y + mod(y + dy, Y),
            mod(x + dx, X) * 2 + mod(core + dc, 2),
        )

    def copy(src, dst, sems, index, device):
        return pltpu.make_async_remote_copy(
            src_ref=src,
            dst_ref=dst,
            send_sem=sems.at[0, index],
            recv_sem=sems.at[1, index],
            device_id=device,
            device_id_type=MESH,
        )

    def each(n, body, start=0):
        def step(i, carry):
            body(i)
            return carry

        lax.fori_loop(start, n, step, 0)

    load_mentor = pltpu.make_async_copy(mentor_hbm, mentor, local_sem.at[2])
    load_weights = pltpu.make_async_copy(weights_hbm, weights, local_sem.at[3])
    load_mentor.start()
    load_weights.start()

    barrier = pltpu.get_barrier_semaphore()

    def greet_tok(i):
        pl.semaphore_signal(barrier, inc=1, device_id=at(dz=i // Y, dy=mod(i, Y)), device_id_type=MESH)

    def greet_voc(i):
        pl.semaphore_signal(barrier, inc=1, device_id=at(dx=i // 2, dc=mod(i, 2)), device_id_type=MESH)

    each(NT, greet_tok, 1)
    each(NV, greet_voc, 1)
    pl.semaphore_wait(barrier, NT - 1 + NV - 1)

    def s1(i):
        return copy(
            hidden.at[:, pl.ds(pl.multiple_of(voc * CS, CS), CS)],
            gathered.at[x, core, z, y],
            s1_sem,
            i,
            at(dz=i),
        )

    each(Z, lambda i: s1(i).start(), 1)
    own_columns = pltpu.make_async_copy(
        hidden.at[:, pl.ds(pl.multiple_of(voc * CS, CS), CS)],
        gathered.at[x, core, z, y],
        local_sem.at[0],
    )
    own_columns.start()

    def t_copy(i):
        device = at(dz=i // Y, dy=mod(i, Y))
        return copy(
            mentor_hbm.at[:, pl.ds(pl.multiple_of(device[0] * V, V), V)],
            teacher.at[pl.ds(pl.multiple_of(tok * R, R), R), :],
            t_sem,
            i,
            device,
        )

    each(NT, lambda i: t_copy(i).start(), 1)
    own_block = pltpu.make_async_copy(
        mentor_hbm.at[:, pl.ds(pl.multiple_of(tok * V, V), V)],
        teacher.at[pl.ds(pl.multiple_of(tok * R, R), R), :],
        local_sem.at[1],
    )
    own_block.start()

    def stage(buf, sems, slot, n, target):
        def c(i):
            return copy(buf.at[slot], buf.at[slot], sems, i, target(i))

        def start():
            each(n, lambda i: c(i).start(), 1)

        def wait():
            each(n, lambda i: c(i).wait(), 1)

        return start, wait

    def three(voc_buf, y_buf, z_buf, voc_sem, y_sem, z_sem):
        return (
            stage(voc_buf, voc_sem, voc, NV, lambda i: at(dx=i // 2, dc=mod(i, 2))),
            stage(y_buf, y_sem, y, Y, lambda i: at(dy=i)),
            stage(z_buf, z_sem, z, Z, lambda i: at(dz=i)),
        )

    stat_stages = three(stat_voc, stat_y, stat_z, stat_voc_sem, stat_y_sem, stat_z_sem)
    mentor_stages = three(
        mentor_voc, mentor_y, mentor_z, mentor_voc_sem, mentor_y_sem, mentor_z_sem
    )
    loss_stages = three(loss_voc, loss_y, loss_z, loss_voc_sem, loss_y_sem, loss_z_sem)

    load_mentor.wait()
    eye = lax.broadcasted_iota(jnp.int32, (q, LANES), 0) == lax.broadcasted_iota(
        jnp.int32, (q, LANES), 1
    )
    eye_rows = lax.broadcasted_iota(jnp.int32, (R, LANES), 0) == lax.broadcasted_iota(
        jnp.int32, (R, LANES), 1
    )

    def columns_of(i):
        return mentor[:, pl.ds(pl.multiple_of(i * V, V), V)].astype(F32) / TEMPERATURE

    def fold(op, value):
        total = value[:, :LANES]
        for j in range(1, V // LANES):
            total = op(total, value[:, j * LANES : (j + 1) * LANES])
        return total

    top_t = lax.fori_loop(
        0,
        NT,
        lambda i, m: jnp.maximum(m, fold(jnp.maximum, columns_of(i))),
        jnp.full((R, LANES), -jnp.inf, F32),
    )
    top_t = jnp.max(top_t, axis=1, keepdims=True)
    sum_t = lax.fori_loop(
        0,
        NT,
        lambda i, s: s + fold(jnp.add, jnp.exp(columns_of(i) - top_t)),
        jnp.zeros((R, LANES), F32),
    )
    sum_t = jnp.sum(sum_t, axis=1, keepdims=True)

    def to_lanes(column, mask):
        return jnp.sum(jnp.where(mask, column, 0.0), axis=0, keepdims=True)

    mentor_voc[voc] = jnp.concatenate(
        [to_lanes(top_t, eye_rows), to_lanes(sum_t, eye_rows), jnp.zeros((6, LANES), F32)], axis=0
    )
    mentor_stages[0][0]()

    def to_column(row):
        return jnp.sum(jnp.where(eye[:, : row.shape[1]], row, 0.0), axis=1, keepdims=True)

    def fill_picks(k):
        here = pl.ds(pl.multiple_of(k * CH, CH), CH)
        parts = [to_column(rows[pl.ds(k * nb + j, 1), :].astype(F32)) for j in range(nb)]
        wanted = jnp.concatenate(parts, axis=0).astype(jnp.int32)
        wanted_rows[here, :] = wanted
        places = lax.broadcasted_iota(jnp.int32, (CH, N), 1)
        picks[here, :] = jnp.where(places == wanted, 1.0, 0.0).astype(BF16)

    each(Z, fill_picks)

    mentor_stages[0][1]()
    tops = [mentor_voc[j, 0:1] for j in range(NV)]
    sums = [mentor_voc[j, 1:2] for j in range(NV)]
    top_t = functools.reduce(jnp.maximum, tops)
    sum_t = functools.reduce(jnp.add, [s * jnp.exp(m - top_t) for s, m in zip(sums, tops)])
    used = lax.broadcasted_iota(jnp.int32, (1, LANES), 1) < R
    sum_t = jnp.where(used, sum_t, 1.0)
    mentor_y[y] = jnp.concatenate([top_t, jnp.log(sum_t), jnp.zeros((6, LANES), F32)], axis=0)
    mentor_stages[1][0]()

    first, second = pl.ds(0, CP), pl.ds(CP, CP)
    load_weights.wait()
    stat_voc[voc] = jnp.zeros((2 * tiles, 8, LANES), F32)

    def away(j):
        return mod(jnp.where(mod(j, 2) == 1, (j + 1) // 2, Z - j // 2), Z)

    def chunk(j):
        return mod(z + Z - away(j), Z)

    def s2a(j, i):
        block = gathered.at[x, core, chunk(j), y, :, first]
        return copy(block, block, s2a_sem, j * Y + i, at(dy=i))

    def s2b(j, i):
        block = gathered.at[x, core, chunk(j), y, :, second]
        return copy(block, block, s2b_sem, j * X + i, at(dx=i))

    def s3a(j, i):
        block = gathered.at[x, core, chunk(j), :, :, first]
        return copy(block, block, s3a_sem, j * X + i, at(dx=i))

    def s3b(j, i):
        block = gathered.at[:, core, chunk(j), y, :, second]
        return copy(block, block, s3b_sem, j * Y + i, at(dy=i))

    def c(j):
        block = gathered.at[:, core, chunk(j)]
        return copy(block, block, c_sem, j, at(dc=1))

    def hidden_of(b, k):
        return gathered[b // 2, b % 2, k].reshape(CH, CS)

    def score(k):
        here = pl.ds(pl.multiple_of(k * CH, CH), CH)
        wide = jnp.concatenate([hidden_of(b, k) for b in range(NV)], axis=1)
        value = jnp.dot(wide, weights[...], preferred_element_type=F32) / TEMPERATURE
        scores[here, :] = value
        top = jnp.max(value, axis=1, keepdims=True)
        total = jnp.sum(jnp.exp(value - top), axis=1, keepdims=True)
        group = lax.broadcasted_iota(jnp.int32, (8, LANES), 0) // nb == mod(k, per_tile)

        def put(column, tile):
            parts = [to_lanes(column[j * q : (j + 1) * q], eye) for j in range(nb)]
            value = jnp.concatenate(parts * per_tile, axis=0)
            stat_voc[voc, tile] = jnp.where(group, value, stat_voc[voc, tile])

        put(top, k // per_tile)
        put(total, tiles + k // per_tile)

    def gather(j):
        @pl.when(j == 0)
        def _():
            own_columns.wait()

        @pl.when((j > 0) & (j < Z))
        def _():
            s1(away(j)).wait()

        @pl.when(j < Z)
        def _():
            each(Y, lambda i: s2a(j, i).start(), 1)
            each(X, lambda i: s2b(j, i).start(), 1)

        @pl.when((j >= 1) & (j < Z + 1))
        def _():
            each(Y, lambda i: s2a(j - 1, i).wait(), 1)
            each(X, lambda i: s3a(j - 1, i).start(), 1)
            each(X, lambda i: s2b(j - 1, i).wait(), 1)
            each(Y, lambda i: s3b(j - 1, i).start(), 1)

        @pl.when((j >= 2) & (j < Z + 2))
        def _():
            each(X, lambda i: s3a(j - 2, i).wait(), 1)
            each(Y, lambda i: s3b(j - 2, i).wait(), 1)
            c(j - 2).start()

        @pl.when(j >= 3)
        def _():
            c(j - 3).wait()
            score(chunk(j - 3))

    each(Z + 3, gather)

    def combine(buf, n):
        tops = [buf[j, :tiles] for j in range(n)]
        sums = [buf[j, tiles:] for j in range(n)]
        top = functools.reduce(jnp.maximum, tops)
        total = functools.reduce(jnp.add, [s * jnp.exp(m - top) for s, m in zip(sums, tops)])
        return top, total

    stat_stages[0][0]()
    mentor_stages[1][1]()
    for j in range(Y):
        mentor_z[z, j] = mentor_y[j]
    mentor_stages[2][0]()
    stat_stages[0][1]()
    top_s, sum_s = combine(stat_voc, NV)
    stat_y[y, :tiles] = top_s
    stat_y[y, tiles:] = sum_s
    stat_stages[1][0]()
    stat_stages[1][1]()
    top_s, sum_s = combine(stat_y, Y)
    stat_z[z, :tiles] = top_s
    stat_z[z, tiles:] = sum_s
    stat_stages[2][0]()
    mentor_stages[2][1]()
    table_top = jnp.concatenate(
        [mentor_z[i, j, 0:1] for i in range(Z) for j in range(Y)], axis=0
    ).astype(BF16)
    table_log = jnp.concatenate(
        [mentor_z[i, j, 1:2] for i in range(Z) for j in range(Y)], axis=0
    )
    log_hi = table_log.astype(BF16)
    rest = table_log - log_hi.astype(F32)
    log_mid = rest.astype(BF16)
    log_lo = (rest - log_mid.astype(F32)).astype(BF16)
    stat_stages[2][1]()
    top_s, sum_s = combine(stat_z, Z)
    stat_voc[0, :tiles] = top_s
    stat_voc[0, tiles:] = jnp.log(jnp.where(sum_s > 0.0, sum_s, 1.0))

    ends = []
    total = jnp.int32(0)
    for j in range(lengths.shape[0]):
        total = total + lengths[j]
        ends.append(total - 1)

    own_block.wait()
    each(NT, lambda i: t_copy(i).wait(), 1)

    def mate(k):
        return copy(mate_send.at[k], mate_recv.at[k], mate_sem, k, at(dc=1))

    def r1a(k, i):
        return copy(
            folded.at[k, :, mod(x + i, X), :, pl.ds(0, QUARTER)],
            first_a.at[k, i - 1],
            r1a_sem,
            k * X + i,
            at(dx=i),
        )

    def r1b(k, i):
        return copy(
            folded.at[k, mod(y + i, Y), :, :, pl.ds(QUARTER, QUARTER)],
            first_b.at[k, i - 1],
            r1b_sem,
            k * Y + i,
            at(dy=i),
        )

    loss_voc[voc] = jnp.zeros((8, LANES), F32)

    def gradient(k):
        zc = mod(z + 1 + k, Z)
        here = pl.ds(pl.multiple_of(zc * CH, CH), CH)
        wanted = wanted_rows[here, :]
        block = wanted // R
        pick = (lax.broadcasted_iota(jnp.int32, (CH, NT), 1) == block).astype(F32).astype(BF16)
        lane = lax.broadcasted_iota(jnp.int32, (CH, LANES), 1) == (wanted - block * R)

        def take(table):
            return jnp.dot(pick, table, preferred_element_type=F32)

        def one(value):
            return jnp.sum(jnp.where(lane, value, 0.0), axis=1, keepdims=True)

        teacher_top = one(take(table_top))
        teacher_log = one(take(log_hi) + take(log_mid) + take(log_lo))
        row_of = lax.broadcasted_iota(jnp.int32, (8, LANES), 0)

        def student(tile):
            value = stat_voc[0, tile + zc // per_tile]
            first_row = mod(zc, per_tile) * nb
            picked = [
                jnp.sum(jnp.where(row_of == first_row + j, value, 0.0), axis=0, keepdims=True)
                for j in range(nb)
            ]
            return jnp.concatenate([to_column(row) for row in picked], axis=0)

        student_top = student(0)
        student_log = student(tiles)
        place = lax.broadcasted_iota(jnp.int32, (CH, 1), 0) + zc * CH
        valid = jnp.ones((CH, 1), F32)
        for end in ends:
            valid = jnp.where(place == end, 0.0, valid)
        taken = jnp.dot(picks[here, :], teacher[...], preferred_element_type=F32) / TEMPERATURE
        log_teacher = (taken - teacher_top) - teacher_log
        log_student = (scores[here, :] - student_top) - student_log
        p_teacher = jnp.exp(log_teacher)
        p_student = jnp.exp(log_student)
        kl = jnp.sum(p_teacher * (log_teacher - log_student), axis=1, keepdims=True)
        grad = ((SCALE * TEMPERATURE) * valid * (p_student - p_teacher)).astype(BF16)
        slope[here, :] = grad

        def product(c):
            return lax.dot_general(
                grad,
                weights[pl.ds(pl.multiple_of(c * HALF, HALF), HALF), :],
                (((1,), (1,)), ((), ())),
                preferred_element_type=F32,
            )

        mate_send[k] = product(1 - core).astype(BF16)
        mate(k).start()
        own_half[mod(k, 2)] = product(core)
        loss_voc[voc] = loss_voc[voc] + jnp.sum(valid * kl, axis=0, keepdims=True)

    def fold_mate(k):
        mate(k).wait()
        value = own_half[mod(k, 2)] + mate_recv[k].astype(F32)
        folded[k] = value.astype(BF16).reshape(Y, X, 16, HALF)
        each(X, lambda i: r1a(k, i).start(), 1)
        each(Y, lambda i: r1b(k, i).start(), 1)

    def weight_part(b):
        wide = gathered[b // 2, mod(b, 2)].reshape(N, CS)
        value = lax.dot_general(
            wide, slope[...], (((0,), (0,)), ((), ())), preferred_element_type=F32
        )
        grad_weight[pl.ds(pl.multiple_of(b * CS, CS), CS), :] = value.astype(BF16)

    def r2a(k, i):
        return copy(
            second_a.at[k, mod(y + i, Y)], got_a.at[k, i - 1], r2a_sem, k * Y + i, at(dy=i)
        )

    def r2b(k, i):
        return copy(
            second_b.at[k, mod(x + i, X)], got_b.at[k, i - 1], r2b_sem, k * X + i, at(dx=i)
        )

    def fold_first(k):
        each(X, lambda i: r1a(k, i).wait(), 1)
        value = folded[k, :, x, :, :QUARTER].astype(F32)
        for i in range(X - 1):
            value = value + first_a[k, i].astype(F32)
        second_a[k] = value.astype(BF16)
        each(Y, lambda i: r2a(k, i).start(), 1)
        each(Y, lambda i: r1b(k, i).wait(), 1)
        value = folded[k, y, :, :, QUARTER:].astype(F32)
        for i in range(Y - 1):
            value = value + first_b[k, i].astype(F32)
        second_b[k] = value.astype(BF16)
        each(X, lambda i: r2b(k, i).start(), 1)

    def fold_second(k):
        each(Y, lambda i: r2a(k, i).wait(), 1)
        each(X, lambda i: r2b(k, i).wait(), 1)
        left = second_a[k, y].astype(F32)
        for i in range(Y - 1):
            left = left + got_a[k, i].astype(F32)
        right = second_b[k, x].astype(F32)
        for i in range(X - 1):
            right = right + got_b[k, i].astype(F32)
        last[0, k] = jnp.concatenate([left, right], axis=1).astype(BF16)

    def r3(k):
        return copy(last.at[0, k], last.at[1, k], r3_sem, k, at(dz=k + 1))

    LAG1, LAG2 = 3, 5

    def turn(j):
        @pl.when(j < Z)
        def _():
            gradient(j)

        @pl.when((j >= 1) & (j < Z + 1))
        def _():
            fold_mate(j - 1)

        @pl.when((j >= LAG1) & (j < Z + LAG1))
        def _():
            fold_first(j - LAG1)

        @pl.when((j >= LAG2) & (j < Z + LAG2))
        def _():
            fold_second(j - LAG2)

        @pl.when((j >= LAG2) & (j < Z + LAG2 - 1))
        def _():
            r3(j - LAG2).start()

        @pl.when(j == Z)
        def _():
            loss_stages[0][0]()

        @pl.when(j == Z + 1)
        def _():
            loss_stages[0][1]()
            loss_y[y] = functools.reduce(jnp.add, [loss_voc[i] for i in range(NV)])
            loss_stages[1][0]()

        @pl.when(j == Z + 2)
        def _():
            loss_stages[1][1]()
            loss_z[z] = functools.reduce(jnp.add, [loss_y[i] for i in range(Y)])
            loss_stages[2][0]()

        @pl.when((j >= Z) & (j < Z + NV // 2))
        def _():
            weight_part(2 * (j - Z))
            weight_part(2 * (j - Z) + 1)

    each(Z + LAG2, turn)
    loss_stages[2][1]()
    loss = functools.reduce(jnp.add, [loss_z[j] for j in range(Z)])
    loss_out[...] = TEMPERATURE * TEMPERATURE * loss / (N - lengths.shape[0])
    each(Z - 1, lambda k: r3(k).wait())
    value = last[0, Z - 1].astype(F32)
    for k in range(Z - 1):
        value = value + last[1, k].astype(F32)
    final[...] = value
    swap = copy(final.at[pl.ds(pl.multiple_of((1 - core) * 8, 8), 8), :], final_recv, final_sem, 0, at(dc=1))
    swap.start()
    mine = jnp.where(core == 0, value[:8], value[8:])
    swap.wait()
    theirs = final_recv[...]
    grad_hidden[:, :HALF] = jnp.where(core == 0, mine, theirs).astype(BF16)
    grad_hidden[:, HALF:] = jnp.where(core == 0, theirs, mine).astype(BF16)


def body(dims, hidden, weights, mentor, rows, lengths):
    Z, Y, X, R, V, D = dims
    NT, NV, CH = Z * Y, X * 2, Y * R
    N, HALF, QUARTER, CS = Z * CH, D // 2, D // 4, D // NV
    vmem = pl.BlockSpec(memory_space=pltpu.VMEM)
    anywhere = pl.BlockSpec(memory_space=pl.ANY)
    nb = max(1, CH // LANES)
    tiles = max(1, Z * nb // 8)
    dma = lambda n: pltpu.SemaphoreType.DMA((2, n))
    loss, grad_hidden, grad_weight = pl.pallas_call(
        functools.partial(kernel, dims),
        out_shape=(
            jax.ShapeDtypeStruct((8, LANES), F32),
            jax.ShapeDtypeStruct((8, D), BF16),
            jax.ShapeDtypeStruct((D, V), BF16),
        ),
        in_specs=[anywhere, anywhere, anywhere, vmem, pl.BlockSpec(memory_space=pltpu.SMEM)],
        out_specs=(vmem, vmem, vmem),
        scratch_shapes=[
            pltpu.VMEM((D, V), BF16),
            pltpu.VMEM((R, V * NT), BF16),
            pltpu.VMEM((N, 1), jnp.int32),
            pltpu.VMEM((X, 2, Z, Y, R, CS), BF16),
            pltpu.VMEM((N, V), BF16),
            pltpu.VMEM((N, N), BF16),
            pltpu.VMEM((N, V), F32),
            pltpu.VMEM((N, V), BF16),
            pltpu.VMEM((Z, CH, HALF), BF16),
            pltpu.VMEM((Z, CH, HALF), BF16),
            pltpu.VMEM((2, CH, HALF), F32),
            pltpu.VMEM((Z, Y, X, 16, HALF), BF16),
            pltpu.VMEM((Z, X - 1, Y, 16, QUARTER), BF16),
            pltpu.VMEM((Z, Y - 1, X, 16, QUARTER), BF16),
            pltpu.VMEM((Z, Y, 16, QUARTER), BF16),
            pltpu.VMEM((Z, X, 16, QUARTER), BF16),
            pltpu.VMEM((Z, Y - 1, 16, QUARTER), BF16),
            pltpu.VMEM((Z, X - 1, 16, QUARTER), BF16),
            pltpu.VMEM((2, Z, 16, HALF), BF16),
            pltpu.VMEM((16, HALF), F32),
            pltpu.VMEM((8, HALF), F32),
            pltpu.VMEM((NV, 2 * tiles, 8, LANES), F32),
            pltpu.VMEM((Y, 2 * tiles, 8, LANES), F32),
            pltpu.VMEM((Z, 2 * tiles, 8, LANES), F32),
            pltpu.VMEM((NV, 8, LANES), F32),
            pltpu.VMEM((Y, 8, LANES), F32),
            pltpu.VMEM((Z, Y, 8, LANES), F32),
            pltpu.VMEM((NV, 8, LANES), F32),
            pltpu.VMEM((Y, 8, LANES), F32),
            pltpu.VMEM((Z, 8, LANES), F32),
            pltpu.SemaphoreType.DMA((4,)),
            dma(Z),
            dma(NT),
            dma(Z * Y),
            dma(Z * X),
            dma(Z * X),
            dma(Z * Y),
            dma(Z),
            dma(NV),
            dma(Y),
            dma(Z),
            dma(NV),
            dma(Y),
            dma(Z),
            dma(NV),
            dma(Y),
            dma(Z),
            dma(Z),
            dma(Z * X),
            dma(Z * Y),
            dma(Z * Y),
            dma(Z * X),
            dma(Z),
            dma(1),
        ],
        compiler_params=pltpu.CompilerParams(
            collective_id=0, has_side_effects=True, vmem_limit_bytes=63 * 2**20
        ),
    )(hidden, weights, mentor, rows.reshape(Z * nb, CH // nb), lengths)
    return loss[0, 0], grad_hidden, grad_weight


def solution(mesh):
    NT, NV = mesh.shape["tok"], mesh.shape["voc"]
    Y = 1 << ((NT.bit_length() - 1) // 2)
    Z, X = NT // Y, NV // 2

    def run(hidden, weights, mentor, rows, lengths):
        N, D = hidden.shape
        dims = (Z, Y, X, N // NT, weights.shape[1] // (NT * NV), D)
        return jax.shard_map(
            functools.partial(body, dims),
            mesh=mesh,
            in_specs=(P("tok", None), P(None, ("voc", "tok")), P("tok", "voc"), P(), P()),
            out_specs=(P(), P(("tok", "voc"), None), P(None, ("voc", "tok"))),
            check_vma=False,
        )(hidden, weights, mentor, rows, lengths)

    return run
```

```python
import functools

import jax
import jax.numpy as jnp
from jax import lax
from jax.experimental import pallas as pl
from jax.experimental.pallas import tpu as pltpu
from jax.sharding import PartitionSpec as P

MESH = pl.DeviceIdType.MESH
F32 = jnp.float32
BF16 = jnp.bfloat16
TEMPERATURE = 2.0
SCALE = 512.0
LANES = 128


def mod(a, n):
    return lax.rem(a, n)


def kernel(
    dims,
    hidden,
    weights_hbm,
    mentor_hbm,
    rows,
    lengths,
    loss_out,
    grad_hidden,
    grad_weight,
    weights,
    mentor,
    wanted_rows,
    run_top,
    run_sum,
    gathered,
    teacher,
    picks,
    scores,
    slope,
    mate_send,
    mate_recv,
    own_half,
    folded,
    first_a,
    first_b,
    second_a,
    second_b,
    got_a,
    got_b,
    first_c,
    second_c,
    got_c,
    third_c,
    got_d,
    last,
    final,
    final_recv,
    stat_voc,
    stat_y,
    stat_z,
    mentor_voc,
    mentor_y,
    mentor_z,
    loss_voc,
    loss_y,
    loss_z,
    local_sem,
    s1_sem,
    t_sem,
    s2a_sem,
    s2b_sem,
    s3a_sem,
    s3b_sem,
    c_sem,
    stat_voc_sem,
    stat_y_sem,
    stat_z_sem,
    mentor_voc_sem,
    mentor_y_sem,
    mentor_z_sem,
    loss_voc_sem,
    loss_y_sem,
    loss_z_sem,
    mate_sem,
    r1a_sem,
    r1b_sem,
    r2a_sem,
    r2b_sem,
    r1c_sem,
    r2c_sem,
    r3c_sem,
    r3_sem,
    final_sem,
):
    Z, Y, X, R, V, D = dims
    tok, voc = lax.axis_index("tok"), lax.axis_index("voc")
    z, y = tok // Y, mod(tok, Y)
    x, core = voc // 2, mod(voc, 2)
    NT, NV = Z * Y, X * 2
    CH = Y * R
    N = Z * CH
    HALF = D // 2
    PC = HALF // 4
    PA = (HALF - PC) // 2
    CS = D // NV
    CP = CS // 2
    nb = max(1, CH // LANES)
    q = CH // nb
    per_tile = 8 // nb
    tiles = max(1, Z // per_tile)

    def at(dz=0, dy=0, dx=0, dc=0):
        return (
            mod(z + dz, Z) * Y + mod(y + dy, Y),
            mod(x + dx, X) * 2 + mod(core + dc, 2),
        )

    def copy(src, dst, sems, index, device):
        return pltpu.make_async_remote_copy(
            src_ref=src,
            dst_ref=dst,
            send_sem=sems.at[0, index],
            recv_sem=sems.at[1, index],
            device_id=device,
            device_id_type=MESH,
        )

    def join(block, sems, index=0):
        copy(block, block, sems, index, at(dc=1)).wait()

    def each(n, body, start=0):
        def step(i, carry):
            body(i)
            return carry

        lax.fori_loop(start, n, step, 0)

    load_mentor = pltpu.make_async_copy(mentor_hbm, mentor, local_sem.at[2])
    load_weights = pltpu.make_async_copy(weights_hbm, weights, local_sem.at[3])
    load_mentor.start()
    load_weights.start()

    barrier = pltpu.get_barrier_semaphore()

    def greet_tok(i):
        pl.semaphore_signal(barrier, inc=1, device_id=at(dz=i // Y, dy=mod(i, Y)), device_id_type=MESH)

    def greet_voc(i):
        pl.semaphore_signal(barrier, inc=1, device_id=at(dx=i // 2, dc=mod(i, 2)), device_id_type=MESH)

    each(NT, greet_tok, 1)
    each(NV, greet_voc, 1)
    pl.semaphore_wait(barrier, NT - 1 + NV - 1)

    def s1(i):
        return copy(
            hidden.at[:, pl.ds(pl.multiple_of(voc * CS, CS), CS)],
            gathered.at[x, core, z, y],
            s1_sem,
            i,
            at(dz=i),
        )

    each(Z, lambda i: s1(i).start(), 1)
    own_columns = pltpu.make_async_copy(
        hidden.at[:, pl.ds(pl.multiple_of(voc * CS, CS), CS)],
        gathered.at[x, core, z, y],
        local_sem.at[0],
    )
    own_columns.start()

    def t_copy(i):
        device = at(dz=i // Y, dy=mod(i, Y))
        return copy(
            mentor_hbm.at[:, pl.ds(pl.multiple_of(device[0] * V, V), V)],
            teacher.at[pl.ds(pl.multiple_of(tok * R, R), R), :],
            t_sem,
            0,
            device,
        )

    each(NT, lambda i: t_copy(i).start(), 1)
    own_block = pltpu.make_async_copy(
        mentor_hbm.at[:, pl.ds(pl.multiple_of(tok * V, V), V)],
        teacher.at[pl.ds(pl.multiple_of(tok * R, R), R), :],
        local_sem.at[1],
    )
    own_block.start()

    def stage(buf, sems, slot, n, target):
        def c(i):
            return copy(buf.at[slot], buf.at[slot], sems, 0, target(i))

        def start():
            each(n, lambda i: c(i).start(), 1)

        def wait():
            join(buf.at[pl.ds(0, n - 1)], sems)

        return start, wait

    def three(voc_buf, y_buf, z_buf, voc_sem, y_sem, z_sem):
        return (
            stage(voc_buf, voc_sem, voc, NV, lambda i: at(dx=i // 2, dc=mod(i, 2))),
            stage(y_buf, y_sem, y, Y, lambda i: at(dy=i)),
            stage(z_buf, z_sem, z, Z, lambda i: at(dz=i)),
        )

    stat_stages = three(stat_voc, stat_y, stat_z, stat_voc_sem, stat_y_sem, stat_z_sem)
    mentor_stages = three(
        mentor_voc, mentor_y, mentor_z, mentor_voc_sem, mentor_y_sem, mentor_z_sem
    )
    loss_stages = three(loss_voc, loss_y, loss_z, loss_voc_sem, loss_y_sem, loss_z_sem)

    eye = lax.broadcasted_iota(jnp.int32, (q, LANES), 0) == lax.broadcasted_iota(
        jnp.int32, (q, LANES), 1
    )
    eye_rows = lax.broadcasted_iota(jnp.int32, (R, LANES), 0) == lax.broadcasted_iota(
        jnp.int32, (R, LANES), 1
    )

    def columns_of(i):
        return mentor[:, pl.ds(pl.multiple_of(i * V, V), V)].astype(F32) / TEMPERATURE

    def fold(op, value):
        total = value[:, :LANES]
        for j in range(1, V // LANES):
            total = op(total, value[:, j * LANES : (j + 1) * LANES])
        return total

    def to_lanes(column, mask):
        return jnp.sum(jnp.where(mask, column, 0.0), axis=0, keepdims=True)

    run_top[...] = jnp.full((R, LANES), -jnp.inf, F32)
    run_sum[...] = jnp.zeros((R, LANES), F32)

    def mentor_part(j):
        old = run_top[...]
        top = lax.fori_loop(
            j * Y, (j + 1) * Y, lambda i, m: jnp.maximum(m, fold(jnp.maximum, columns_of(i))), old
        )
        wide = jnp.concatenate([top] * (V // LANES), axis=1)
        run_sum[...] = lax.fori_loop(
            j * Y,
            (j + 1) * Y,
            lambda i, s: s + fold(jnp.add, jnp.exp(columns_of(i) - wide)),
            run_sum[...] * jnp.exp(old - top),
        )
        run_top[...] = top

    def mentor_done():
        top_t = jnp.max(run_top[...], axis=1, keepdims=True)
        sum_t = jnp.sum(run_sum[...] * jnp.exp(run_top[...] - top_t), axis=1, keepdims=True)
        mentor_voc[voc] = jnp.concatenate(
            [to_lanes(top_t, eye_rows), to_lanes(sum_t, eye_rows), jnp.zeros((6, LANES), F32)],
            axis=0,
        )
        mentor_stages[0][0]()

    def to_column(row):
        return jnp.sum(jnp.where(eye[:, : row.shape[1]], row, 0.0), axis=1, keepdims=True)

    def fill_picks(k):
        here = pl.ds(pl.multiple_of(k * CH, CH), CH)
        parts = [to_column(rows[pl.ds(k * nb + j, 1), :].astype(F32)) for j in range(nb)]
        wanted = jnp.concatenate(parts, axis=0).astype(jnp.int32)
        wanted_rows[here, :] = wanted
        places = lax.broadcasted_iota(jnp.int32, (CH, N), 1)
        picks[here, :] = jnp.where(places == wanted, 1.0, 0.0).astype(BF16)

    def mentor_second():
        mentor_stages[0][1]()
        tops = [mentor_voc[j, 0:1] for j in range(NV)]
        sums = [mentor_voc[j, 1:2] for j in range(NV)]
        top_t = functools.reduce(jnp.maximum, tops)
        sum_t = functools.reduce(jnp.add, [s * jnp.exp(m - top_t) for s, m in zip(sums, tops)])
        used = lax.broadcasted_iota(jnp.int32, (1, LANES), 1) < R
        sum_t = jnp.where(used, sum_t, 1.0)
        mentor_y[y] = jnp.concatenate([top_t, jnp.log(sum_t), jnp.zeros((6, LANES), F32)], axis=0)
        mentor_stages[1][0]()

    def mentor_third():
        mentor_stages[1][1]()
        for j in range(Y):
            mentor_z[z, j] = mentor_y[j]
        mentor_stages[2][0]()

    first, second = pl.ds(0, CP), pl.ds(CP, CP)
    stat_voc[voc] = jnp.zeros((2 * tiles, 8, LANES), F32)

    def away(j):
        return mod(jnp.where(mod(j, 2) == 1, (j + 1) // 2, Z - j // 2), Z)

    def chunk(j):
        return mod(z + Z - away(j), Z)

    def s2a(j, i):
        block = gathered.at[x, core, chunk(j), y, :, first]
        return copy(block, block, s2a_sem, j, at(dy=i))

    def s2b(j, i):
        block = gathered.at[x, core, chunk(j), y, :, second]
        return copy(block, block, s2b_sem, j, at(dx=i))

    def s3a(j, i):
        block = gathered.at[x, core, chunk(j), :, :, first]
        return copy(block, block, s3a_sem, j, at(dx=i))

    def s3b(j, i):
        block = gathered.at[:, core, chunk(j), y, :, second]
        return copy(block, block, s3b_sem, j, at(dy=i))

    def c(j):
        block = gathered.at[:, core, chunk(j)]
        return copy(block, block, c_sem, j, at(dc=1))

    def hidden_of(b, k):
        return gathered[b // 2, b % 2, k].reshape(CH, CS)

    def score(k):
        here = pl.ds(pl.multiple_of(k * CH, CH), CH)
        wide = jnp.concatenate([hidden_of(b, k) for b in range(NV)], axis=1)
        value = jnp.dot(wide, weights[...], preferred_element_type=F32) / TEMPERATURE
        scores[here, :] = value
        top = jnp.max(value, axis=1, keepdims=True)
        total = jnp.sum(jnp.exp(value - top), axis=1, keepdims=True)
        group = lax.broadcasted_iota(jnp.int32, (8, LANES), 0) // nb == mod(k, per_tile)

        def put(column, tile):
            parts = [to_lanes(column[j * q : (j + 1) * q], eye) for j in range(nb)]
            value = jnp.concatenate(parts * per_tile, axis=0)
            stat_voc[voc, tile] = jnp.where(group, value, stat_voc[voc, tile])

        put(top, k // per_tile)
        put(total, tiles + k // per_tile)

    def gather(j):
        @pl.when(j == 0)
        def _():
            own_columns.wait()
            load_mentor.wait()

        @pl.when((j > 0) & (j < Z))
        def _():
            s1(away(j)).wait()

        @pl.when(j < Z)
        def _():
            each(Y, lambda i: s2a(j, i).start(), 1)
            each(X, lambda i: s2b(j, i).start(), 1)

        @pl.when((j >= 1) & (j < Z + 1))
        def _():
            join(gathered.at[x, core, chunk(j - 1), pl.ds(0, Y - 1), :, first], s2a_sem, j - 1)
            each(X, lambda i: s3a(j - 1, i).start(), 1)
            join(gathered.at[pl.ds(0, X - 1), core, chunk(j - 1), y, :, second], s2b_sem, j - 1)
            each(Y, lambda i: s3b(j - 1, i).start(), 1)

        @pl.when((j >= 2) & (j < Z + 2))
        def _():
            join(gathered.at[pl.ds(0, X - 1), core, chunk(j - 2), :, :, first], s3a_sem, j - 2)
            join(gathered.at[:, core, chunk(j - 2), pl.ds(0, Y - 1), :, second], s3b_sem, j - 2)
            c(j - 2).start()

        @pl.when(j < Z)
        def _():
            mentor_part(j)
            fill_picks(j)

        @pl.when(j == Z - 1)
        def _():
            mentor_done()

        @pl.when(j == Z)
        def _():
            mentor_second()

        @pl.when(j == Z + 1)
        def _():
            mentor_third()

        @pl.when(j == 3)
        def _():
            load_weights.wait()

        @pl.when(j >= 3)
        def _():
            c(j - 3).wait()
            score(chunk(j - 3))

    each(Z + 3, gather)

    def combine(buf, n):
        tops = [buf[j, :tiles] for j in range(n)]
        sums = [buf[j, tiles:] for j in range(n)]
        top = functools.reduce(jnp.maximum, tops)
        total = functools.reduce(jnp.add, [s * jnp.exp(m - top) for s, m in zip(sums, tops)])
        return top, total

    stat_stages[0][0]()
    stat_stages[0][1]()
    top_s, sum_s = combine(stat_voc, NV)
    stat_y[y, :tiles] = top_s
    stat_y[y, tiles:] = sum_s
    stat_stages[1][0]()
    stat_stages[1][1]()
    top_s, sum_s = combine(stat_y, Y)
    stat_z[z, :tiles] = top_s
    stat_z[z, tiles:] = sum_s
    stat_stages[2][0]()
    mentor_stages[2][1]()
    table_top = jnp.concatenate(
        [mentor_z[i, j, 0:1] for i in range(Z) for j in range(Y)], axis=0
    ).astype(BF16)
    table_log = jnp.concatenate(
        [mentor_z[i, j, 1:2] for i in range(Z) for j in range(Y)], axis=0
    )
    log_hi = table_log.astype(BF16)
    rest = table_log - log_hi.astype(F32)
    log_mid = rest.astype(BF16)
    log_lo = (rest - log_mid.astype(F32)).astype(BF16)
    stat_stages[2][1]()
    top_s, sum_s = combine(stat_z, Z)
    stat_voc[0, :tiles] = top_s
    stat_voc[0, tiles:] = jnp.log(jnp.where(sum_s > 0.0, sum_s, 1.0))

    ends = []
    total = jnp.int32(0)
    for j in range(lengths.shape[0]):
        total = total + lengths[j]
        ends.append(total - 1)

    own_block.wait()
    join(teacher.at[pl.ds(0, (NT - 1) * R), :], t_sem)

    def mate(k):
        return copy(mate_send.at[k], mate_recv.at[k], mate_sem, k, at(dc=1))

    def r1a(k, i):
        return copy(
            folded.at[k, :, mod(x + i, X), :, pl.ds(0, PA)],
            first_a.at[k, i - 1],
            r1a_sem,
            k,
            at(dx=i),
        )

    def r1b(k, i):
        return copy(
            folded.at[k, mod(y + i, Y), :, :, pl.ds(PA, PA)],
            first_b.at[k, i - 1],
            r1b_sem,
            k,
            at(dy=i),
        )

    def r1c(k):
        return copy(
            folded.at[k, :, :, :, pl.ds(2 * PA, PC)], first_c.at[k], r1c_sem, 0, at(dz=k + 1)
        )

    loss_voc[voc] = jnp.zeros((8, LANES), F32)

    def gradient(k):
        zc = mod(z + 1 + k, Z)
        here = pl.ds(pl.multiple_of(zc * CH, CH), CH)
        wanted = wanted_rows[here, :]
        block = wanted // R
        pick = (lax.broadcasted_iota(jnp.int32, (CH, NT), 1) == block).astype(F32).astype(BF16)
        lane = lax.broadcasted_iota(jnp.int32, (CH, LANES), 1) == (wanted - block * R)

        def take(table):
            return jnp.dot(pick, table, preferred_element_type=F32)

        def one(value):
            return jnp.sum(jnp.where(lane, value, 0.0), axis=1, keepdims=True)

        teacher_top = one(take(table_top))
        teacher_log = one(take(log_hi) + take(log_mid) + take(log_lo))
        row_of = lax.broadcasted_iota(jnp.int32, (8, LANES), 0)

        def student(tile):
            value = stat_voc[0, tile + zc // per_tile]
            first_row = mod(zc, per_tile) * nb
            picked = [
                jnp.sum(jnp.where(row_of == first_row + j, value, 0.0), axis=0, keepdims=True)
                for j in range(nb)
            ]
            return jnp.concatenate([to_column(row) for row in picked], axis=0)

        student_top = student(0)
        student_log = student(tiles)
        place = lax.broadcasted_iota(jnp.int32, (CH, 1), 0) + zc * CH
        valid = jnp.ones((CH, 1), F32)
        for end in ends:
            valid = jnp.where(place == end, 0.0, valid)
        taken = jnp.dot(picks[here, :], teacher[...], preferred_element_type=F32) / TEMPERATURE
        log_teacher = (taken - teacher_top) - teacher_log
        log_student = (scores[here, :] - student_top) - student_log
        p_teacher = jnp.exp(log_teacher)
        p_student = jnp.exp(log_student)
        kl = jnp.sum(p_teacher * (log_teacher - log_student), axis=1, keepdims=True)
        grad = ((SCALE * TEMPERATURE) * valid * (p_student - p_teacher)).astype(BF16)
        slope[here, :] = grad

        def product(c):
            return lax.dot_general(
                grad,
                weights[pl.ds(pl.multiple_of(c * HALF, HALF), HALF), :],
                (((1,), (1,)), ((), ())),
                preferred_element_type=F32,
            )

        mate_send[k] = product(1 - core).astype(BF16)
        mate(k).start()
        own_half[mod(k, 2)] = product(core)
        loss_voc[voc] = loss_voc[voc] + jnp.sum(valid * kl, axis=0, keepdims=True)

    def fold_mate(k):
        mate(k).wait()
        value = own_half[mod(k, 2)] + mate_recv[k].astype(F32)
        folded[k] = value.astype(BF16).reshape(Y, X, 16, HALF)
        each(X, lambda i: r1a(k, i).start(), 1)
        each(Y, lambda i: r1b(k, i).start(), 1)

        @pl.when(k < Z - 1)
        def _():
            r1c(k).start()

    def weight_part(b):
        wide = gathered[b // 2, mod(b, 2)].reshape(N, CS)
        value = lax.dot_general(
            wide, slope[...], (((0,), (0,)), ((), ())), preferred_element_type=F32
        )
        grad_weight[pl.ds(pl.multiple_of(b * CS, CS), CS), :] = value.astype(BF16)

    def r2a(k, i):
        return copy(second_a.at[k, mod(y + i, Y)], got_a.at[k, i - 1], r2a_sem, k, at(dy=i))

    def r2b(k, i):
        return copy(second_b.at[k, mod(x + i, X)], got_b.at[k, i - 1], r2b_sem, k, at(dx=i))

    def add(value, others):
        for other in others:
            value = value + other.astype(F32)
        return value

    def fold_first(k):
        join(first_a.at[k], r1a_sem, k)
        value = folded[k, :, x, :, :PA].astype(F32)
        second_a[k] = add(value, [first_a[k, i] for i in range(X - 1)]).astype(BF16)
        each(Y, lambda i: r2a(k, i).start(), 1)
        join(first_b.at[k], r1b_sem, k)
        value = folded[k, y, :, :, PA : 2 * PA].astype(F32)
        second_b[k] = add(value, [first_b[k, i] for i in range(Y - 1)]).astype(BF16)
        each(X, lambda i: r2b(k, i).start(), 1)

    def fold_second(k):
        join(got_a.at[k], r2a_sem, k)
        join(got_b.at[k], r2b_sem, k)
        left = add(second_a[k, y].astype(F32), [got_a[k, i] for i in range(Y - 1)])
        right = add(second_b[k, x].astype(F32), [got_b[k, i] for i in range(X - 1)])
        last[0, k] = jnp.concatenate([left, right], axis=1).astype(BF16)

    def r2c(i):
        return copy(second_c.at[mod(y + i, Y)], got_c.at[i - 1], r2c_sem, 0, at(dy=i))

    def r3c(i):
        return copy(third_c.at[mod(x + i, X)], got_d.at[i - 1], r3c_sem, 0, at(dx=i))

    def fold_first_c():
        join(first_c, r1c_sem)
        value = folded[Z - 1, :, :, :, 2 * PA :].astype(F32)
        second_c[...] = add(value, [first_c[k] for k in range(Z - 1)]).astype(BF16)
        each(Y, lambda i: r2c(i).start(), 1)

    def fold_second_c():
        join(got_c, r2c_sem)
        value = second_c[y].astype(F32)
        third_c[...] = add(value, [got_c[i] for i in range(Y - 1)]).astype(BF16)
        each(X, lambda i: r3c(i).start(), 1)

    def r3(k):
        return copy(last.at[0, k], last.at[1, k], r3_sem, 0, at(dz=k + 1))

    LAG1, LAG2 = 3, 4

    def turn(j):
        @pl.when(j < Z)
        def _():
            gradient(j)

        @pl.when((j >= 1) & (j < Z + 1))
        def _():
            fold_mate(j - 1)

        @pl.when(j == Z)
        def _():
            loss_stages[0][0]()

        @pl.when(j == Z + 1)
        def _():
            loss_stages[0][1]()
            loss_y[y] = functools.reduce(jnp.add, [loss_voc[i] for i in range(NV)])
            loss_stages[1][0]()

        @pl.when(j == Z + 2)
        def _():
            fold_first_c()
            loss_stages[1][1]()
            loss_z[z] = functools.reduce(jnp.add, [loss_y[i] for i in range(Y)])
            loss_stages[2][0]()

        @pl.when((j >= Z) & (j < Z + NV // 2))
        def _():
            weight_part(2 * (j - Z))
            weight_part(2 * (j - Z) + 1)

        @pl.when((j >= LAG1) & (j < Z + LAG1))
        def _():
            fold_first(j - LAG1)

        @pl.when(j == Z + 3)
        def _():
            fold_second_c()

        @pl.when(j >= LAG2)
        def _():
            fold_second(j - LAG2)

        @pl.when((j >= LAG2) & (j < Z + LAG2 - 1))
        def _():
            r3(j - LAG2).start()

    each(Z + LAG2, turn)
    loss_stages[2][1]()
    loss = functools.reduce(jnp.add, [loss_z[j] for j in range(Z)])
    loss_out[0, 0] = jnp.max(TEMPERATURE * TEMPERATURE * loss / (N - lengths.shape[0]))
    join(last.at[1, pl.ds(0, Z - 1)], r3_sem)
    join(got_d, r3c_sem)
    value = add(last[0, Z - 1].astype(F32), [last[1, k] for k in range(Z - 1)])
    right = add(third_c[x].astype(F32), [got_d[i] for i in range(X - 1)])
    value = jnp.concatenate([value, right], axis=1)
    final[...] = value
    swap = copy(final.at[pl.ds(pl.multiple_of((1 - core) * 8, 8), 8), :], final_recv, final_sem, 0, at(dc=1))
    swap.start()
    mine = jnp.where(core == 0, value[:8], value[8:])
    swap.wait()
    theirs = final_recv[...]
    grad_hidden[:, :HALF] = jnp.where(core == 0, mine, theirs).astype(BF16)
    grad_hidden[:, HALF:] = jnp.where(core == 0, theirs, mine).astype(BF16)


def body(dims, hidden, weights, mentor, rows, lengths):
    Z, Y, X, R, V, D = dims
    NT, NV, CH = Z * Y, X * 2, Y * R
    N, HALF, CS = Z * CH, D // 2, D // NV
    PC = HALF // 4
    PA = (HALF - PC) // 2
    vmem = pl.BlockSpec(memory_space=pltpu.VMEM)
    anywhere = pl.BlockSpec(memory_space=pl.ANY)
    nb = max(1, CH // LANES)
    tiles = max(1, Z * nb // 8)
    dma = lambda n: pltpu.SemaphoreType.DMA((2, n))
    loss, grad_hidden, grad_weight = pl.pallas_call(
        functools.partial(kernel, dims),
        out_shape=(
            jax.ShapeDtypeStruct((1, 1), F32),
            jax.ShapeDtypeStruct((8, D), BF16),
            jax.ShapeDtypeStruct((D, V), BF16),
        ),
        in_specs=[anywhere, anywhere, anywhere, vmem, pl.BlockSpec(memory_space=pltpu.SMEM)],
        out_specs=(pl.BlockSpec(memory_space=pltpu.SMEM), vmem, vmem),
        scratch_shapes=[
            pltpu.VMEM((D, V), BF16),
            pltpu.VMEM((R, V * NT), BF16),
            pltpu.VMEM((N, 1), jnp.int32),
            pltpu.VMEM((R, LANES), F32),
            pltpu.VMEM((R, LANES), F32),
            pltpu.VMEM((X, 2, Z, Y, R, CS), BF16),
            pltpu.VMEM((N, V), BF16),
            pltpu.VMEM((N, N), BF16),
            pltpu.VMEM((N, V), F32),
            pltpu.VMEM((N, V), BF16),
            pltpu.VMEM((Z, CH, HALF), BF16),
            pltpu.VMEM((Z, CH, HALF), BF16),
            pltpu.VMEM((2, CH, HALF), F32),
            pltpu.VMEM((Z, Y, X, 16, HALF), BF16),
            pltpu.VMEM((Z, X - 1, Y, 16, PA), BF16),
            pltpu.VMEM((Z, Y - 1, X, 16, PA), BF16),
            pltpu.VMEM((Z, Y, 16, PA), BF16),
            pltpu.VMEM((Z, X, 16, PA), BF16),
            pltpu.VMEM((Z, Y - 1, 16, PA), BF16),
            pltpu.VMEM((Z, X - 1, 16, PA), BF16),
            pltpu.VMEM((Z - 1, Y, X, 16, PC), BF16),
            pltpu.VMEM((Y, X, 16, PC), BF16),
            pltpu.VMEM((Y - 1, X, 16, PC), BF16),
            pltpu.VMEM((X, 16, PC), BF16),
            pltpu.VMEM((X - 1, 16, PC), BF16),
            pltpu.VMEM((2, Z, 16, 2 * PA), BF16),
            pltpu.VMEM((16, HALF), F32),
            pltpu.VMEM((8, HALF), F32),
            pltpu.VMEM((NV, 2 * tiles, 8, LANES), F32),
            pltpu.VMEM((Y, 2 * tiles, 8, LANES), F32),
            pltpu.VMEM((Z, 2 * tiles, 8, LANES), F32),
            pltpu.VMEM((NV, 8, LANES), F32),
            pltpu.VMEM((Y, 8, LANES), F32),
            pltpu.VMEM((Z, Y, 8, LANES), F32),
            pltpu.VMEM((NV, 8, LANES), F32),
            pltpu.VMEM((Y, 8, LANES), F32),
            pltpu.VMEM((Z, 8, LANES), F32),
            pltpu.SemaphoreType.DMA((4,)),
            dma(Z),
            dma(1),
            dma(Z),
            dma(Z),
            dma(Z),
            dma(Z),
            dma(Z),
            dma(1),
            dma(1),
            dma(1),
            dma(1),
            dma(1),
            dma(1),
            dma(1),
            dma(1),
            dma(1),
            dma(Z),
            dma(Z),
            dma(Z),
            dma(Z),
            dma(Z),
            dma(1),
            dma(1),
            dma(1),
            dma(1),
            dma(1),
        ],
        compiler_params=pltpu.CompilerParams(
            collective_id=0, has_side_effects=True, vmem_limit_bytes=63 * 2**20
        ),
    )(hidden, weights, mentor, rows.reshape(Z * nb, CH // nb), lengths)
    return loss.reshape(()), grad_hidden, grad_weight


def solution(mesh):
    NT, NV = mesh.shape["tok"], mesh.shape["voc"]
    Y = 1 << ((NT.bit_length() - 1) // 2)
    Z, X = NT // Y, NV // 2

    def run(hidden, weights, mentor, rows, lengths):
        N, D = hidden.shape
        dims = (Z, Y, X, N // NT, weights.shape[1] // (NT * NV), D)
        return jax.shard_map(
            functools.partial(body, dims),
            mesh=mesh,
            in_specs=(P("tok", None), P(None, ("voc", "tok")), P("tok", "voc"), P(), P()),
            out_specs=(P(), P(("tok", "voc"), None), P(None, ("voc", "tok"))),
            check_vma=False,
        )(hidden, weights, mentor, rows, lengths)

    return run
```

```python
import functools

import jax
import jax.numpy as jnp
from jax import lax
from jax.experimental import pallas as pl
from jax.experimental.pallas import tpu as pltpu
from jax.sharding import PartitionSpec as P

MESH = pl.DeviceIdType.MESH
F32 = jnp.float32
BF16 = jnp.bfloat16
TEMPERATURE = 2.0
SCALE = 512.0
LANES = 128


def mod(a, n):
    return lax.rem(a, n)


def kernel(
    dims,
    hidden,
    weights_hbm,
    mentor_hbm,
    rows,
    lengths,
    loss_out,
    grad_hidden,
    grad_weight,
    weights,
    mentor,
    wanted_rows,
    run_top,
    run_sum,
    gathered,
    teacher,
    picks,
    scores,
    slope,
    mate_send,
    mate_recv,
    own_half,
    folded,
    first_a,
    first_b,
    second_a,
    second_b,
    got_a,
    got_b,
    first_c,
    second_c,
    got_c,
    third_c,
    got_d,
    last,
    final,
    final_recv,
    stat_voc,
    stat_y,
    stat_z,
    mentor_voc,
    mentor_y,
    mentor_z,
    loss_voc,
    loss_y,
    loss_z,
    local_sem,
    s1_sem,
    t_sem,
    s2a_sem,
    s2b_sem,
    s3a_sem,
    s3b_sem,
    c_sem,
    stat_voc_sem,
    stat_y_sem,
    stat_z_sem,
    mentor_voc_sem,
    mentor_y_sem,
    mentor_z_sem,
    loss_voc_sem,
    loss_y_sem,
    loss_z_sem,
    mate_sem,
    r1a_sem,
    r1b_sem,
    r2a_sem,
    r2b_sem,
    r1c_sem,
    r2c_sem,
    r3c_sem,
    r3_sem,
    final_sem,
):
    Z, Y, X, R, V, D = dims
    tok, voc = lax.axis_index("tok"), lax.axis_index("voc")
    z, y = tok // Y, mod(tok, Y)
    x, core = voc // 2, mod(voc, 2)
    NT, NV = Z * Y, X * 2
    CH = Y * R
    N = Z * CH
    HALF = D // 2
    PC = HALF // 4
    PA = (HALF - PC) // 2
    CS = D // NV
    RA = (3 * R // 4) // 16 * 16
    nb = max(1, CH // LANES)
    q = CH // nb
    per_tile = 8 // nb
    tiles = max(1, Z // per_tile)

    def at(dz=0, dy=0, dx=0, dc=0):
        return (
            mod(z + dz, Z) * Y + mod(y + dy, Y),
            mod(x + dx, X) * 2 + mod(core + dc, 2),
        )

    def copy(src, dst, sems, index, device):
        return pltpu.make_async_remote_copy(
            src_ref=src,
            dst_ref=dst,
            send_sem=sems.at[0, index],
            recv_sem=sems.at[1, index],
            device_id=device,
            device_id_type=MESH,
        )

    def join(block, sems, index=0):
        copy(block, block, sems, index, at(dc=1)).wait()

    def each(n, body, start=0):
        def step(i, carry):
            body(i)
            return carry

        lax.fori_loop(start, n, step, 0)

    load_mentor = pltpu.make_async_copy(mentor_hbm, mentor, local_sem.at[2])
    load_weights = pltpu.make_async_copy(weights_hbm, weights, local_sem.at[3])
    load_mentor.start()
    load_weights.start()

    barrier = pltpu.get_barrier_semaphore()

    def greet_tok(i):
        pl.semaphore_signal(barrier, inc=1, device_id=at(dz=i // Y, dy=mod(i, Y)), device_id_type=MESH)

    def greet_voc(i):
        pl.semaphore_signal(barrier, inc=1, device_id=at(dx=i // 2, dc=mod(i, 2)), device_id_type=MESH)

    each(NT, greet_tok, 1)
    each(NV, greet_voc, 1)
    pl.semaphore_wait(barrier, NT - 1 + NV - 1)

    def s1(i):
        return copy(
            hidden.at[:, pl.ds(pl.multiple_of(voc * CS, CS), CS)],
            gathered.at[x, core, z, y],
            s1_sem,
            i,
            at(dz=i),
        )

    each(Z, lambda i: s1(i).start(), 1)
    own_columns = pltpu.make_async_copy(
        hidden.at[:, pl.ds(pl.multiple_of(voc * CS, CS), CS)],
        gathered.at[x, core, z, y],
        local_sem.at[0],
    )
    own_columns.start()

    def t_copy(i):
        device = at(dz=i // Y, dy=mod(i, Y))
        return copy(
            mentor_hbm.at[:, pl.ds(pl.multiple_of(device[0] * V, V), V)],
            teacher.at[pl.ds(pl.multiple_of(tok * R, R), R), :],
            t_sem,
            0,
            device,
        )

    each(NT, lambda i: t_copy(i).start(), 1)
    own_block = pltpu.make_async_copy(
        mentor_hbm.at[:, pl.ds(pl.multiple_of(tok * V, V), V)],
        teacher.at[pl.ds(pl.multiple_of(tok * R, R), R), :],
        local_sem.at[1],
    )
    own_block.start()

    def stage(buf, sems, slot, n, target):
        def c(i):
            return copy(buf.at[slot], buf.at[slot], sems, 0, target(i))

        def start():
            each(n, lambda i: c(i).start(), 1)

        def wait():
            join(buf.at[pl.ds(0, n - 1)], sems)

        return start, wait

    def three(voc_buf, y_buf, z_buf, voc_sem, y_sem, z_sem):
        return (
            stage(voc_buf, voc_sem, voc, NV, lambda i: at(dx=i // 2, dc=mod(i, 2))),
            stage(y_buf, y_sem, y, Y, lambda i: at(dy=i)),
            stage(z_buf, z_sem, z, Z, lambda i: at(dz=i)),
        )

    stat_stages = three(stat_voc, stat_y, stat_z, stat_voc_sem, stat_y_sem, stat_z_sem)
    mentor_stages = three(
        mentor_voc, mentor_y, mentor_z, mentor_voc_sem, mentor_y_sem, mentor_z_sem
    )
    loss_stages = three(loss_voc, loss_y, loss_z, loss_voc_sem, loss_y_sem, loss_z_sem)

    eye = lax.broadcasted_iota(jnp.int32, (q, LANES), 0) == lax.broadcasted_iota(
        jnp.int32, (q, LANES), 1
    )
    eye_rows = lax.broadcasted_iota(jnp.int32, (R, LANES), 0) == lax.broadcasted_iota(
        jnp.int32, (R, LANES), 1
    )

    def columns_of(i):
        return mentor[:, pl.ds(pl.multiple_of(i * V, V), V)].astype(F32) / TEMPERATURE

    def fold(op, value):
        total = value[:, :LANES]
        for j in range(1, V // LANES):
            total = op(total, value[:, j * LANES : (j + 1) * LANES])
        return total

    def to_lanes(column, mask):
        return jnp.sum(jnp.where(mask, column, 0.0), axis=0, keepdims=True)

    run_top[...] = jnp.full((R, LANES), -jnp.inf, F32)
    run_sum[...] = jnp.zeros((R, LANES), F32)

    def mentor_part(j):
        old = run_top[...]
        top = lax.fori_loop(
            j * Y, (j + 1) * Y, lambda i, m: jnp.maximum(m, fold(jnp.maximum, columns_of(i))), old
        )
        wide = jnp.concatenate([top] * (V // LANES), axis=1)
        run_sum[...] = lax.fori_loop(
            j * Y,
            (j + 1) * Y,
            lambda i, s: s + fold(jnp.add, jnp.exp(columns_of(i) - wide)),
            run_sum[...] * jnp.exp(old - top),
        )
        run_top[...] = top

    def mentor_done():
        top_t = jnp.max(run_top[...], axis=1, keepdims=True)
        sum_t = jnp.sum(run_sum[...] * jnp.exp(run_top[...] - top_t), axis=1, keepdims=True)
        mentor_voc[voc] = jnp.concatenate(
            [to_lanes(top_t, eye_rows), to_lanes(sum_t, eye_rows), jnp.zeros((6, LANES), F32)],
            axis=0,
        )
        mentor_stages[0][0]()

    def to_column(row):
        return jnp.sum(jnp.where(eye[:, : row.shape[1]], row, 0.0), axis=1, keepdims=True)

    def fill_picks(k):
        here = pl.ds(pl.multiple_of(k * CH, CH), CH)
        parts = [to_column(rows[pl.ds(k * nb + j, 1), :].astype(F32)) for j in range(nb)]
        wanted = jnp.concatenate(parts, axis=0).astype(jnp.int32)
        wanted_rows[here, :] = wanted
        places = lax.broadcasted_iota(jnp.int32, (CH, N), 1)
        picks[here, :] = jnp.where(places == wanted, 1.0, 0.0).astype(BF16)

    def mentor_second():
        mentor_stages[0][1]()
        tops = [mentor_voc[j, 0:1] for j in range(NV)]
        sums = [mentor_voc[j, 1:2] for j in range(NV)]
        top_t = functools.reduce(jnp.maximum, tops)
        sum_t = functools.reduce(jnp.add, [s * jnp.exp(m - top_t) for s, m in zip(sums, tops)])
        used = lax.broadcasted_iota(jnp.int32, (1, LANES), 1) < R
        sum_t = jnp.where(used, sum_t, 1.0)
        mentor_y[y] = jnp.concatenate([top_t, jnp.log(sum_t), jnp.zeros((6, LANES), F32)], axis=0)
        mentor_stages[1][0]()

    def mentor_third():
        mentor_stages[1][1]()
        for j in range(Y):
            mentor_z[z, j] = mentor_y[j]
        mentor_stages[2][0]()

    first, second = pl.ds(0, RA), pl.ds(RA, R - RA)
    stat_voc[voc] = jnp.zeros((2 * tiles, 8, LANES), F32)

    def away(j):
        return mod(jnp.where(mod(j, 2) == 1, (j + 1) // 2, Z - j // 2), Z)

    def chunk(j):
        return mod(z + Z - away(j), Z)

    def s2a(j, i):
        block = gathered.at[x, core, chunk(j), y, first]
        return copy(block, block, s2a_sem, j, at(dy=i))

    def s2b(j, i):
        block = gathered.at[x, core, chunk(j), y, second]
        return copy(block, block, s2b_sem, j, at(dx=i))

    def s3a(j, i):
        block = gathered.at[x, core, chunk(j), :, first]
        return copy(block, block, s3a_sem, j, at(dx=i))

    def s3b(j, i):
        block = gathered.at[:, core, chunk(j), y, second]
        return copy(block, block, s3b_sem, j, at(dy=i))

    def c(j):
        block = gathered.at[:, core, chunk(j)]
        return copy(block, block, c_sem, j, at(dc=1))

    def hidden_of(b, k):
        return gathered[b // 2, b % 2, k].reshape(CH, CS)

    def score(k):
        here = pl.ds(pl.multiple_of(k * CH, CH), CH)
        wide = jnp.concatenate([hidden_of(b, k) for b in range(NV)], axis=1)
        value = jnp.dot(wide, weights[...], preferred_element_type=F32) / TEMPERATURE
        scores[here, :] = value
        top = jnp.max(value, axis=1, keepdims=True)
        total = jnp.sum(jnp.exp(value - top), axis=1, keepdims=True)
        group = lax.broadcasted_iota(jnp.int32, (8, LANES), 0) // nb == mod(k, per_tile)

        def put(column, tile):
            parts = [to_lanes(column[j * q : (j + 1) * q], eye) for j in range(nb)]
            value = jnp.concatenate(parts * per_tile, axis=0)
            stat_voc[voc, tile] = jnp.where(group, value, stat_voc[voc, tile])

        put(top, k // per_tile)
        put(total, tiles + k // per_tile)

    def second_step(j):
        each(Y, lambda i: s2a(j, i).start(), 1)
        each(X, lambda i: s2b(j, i).start(), 1)

    def third_step(j):
        join(gathered.at[x, core, chunk(j), pl.ds(0, Y - 1), first], s2a_sem, j)
        each(X, lambda i: s3a(j, i).start(), 1)
        join(gathered.at[pl.ds(0, X - 1), core, chunk(j), y, second], s2b_sem, j)
        each(Y, lambda i: s3b(j, i).start(), 1)

    def fourth_step(j):
        join(gathered.at[pl.ds(0, X - 1), core, chunk(j), :, first], s3a_sem, j)
        join(gathered.at[:, core, chunk(j), pl.ds(0, Y - 1), second], s3b_sem, j)
        c(j).start()

    def last_step(j):
        c(j).wait()
        score(chunk(j))

    own_columns.wait()
    second_step(0)
    load_mentor.wait()
    each(Z // 2, mentor_part)
    third_step(0)
    each(Z, mentor_part, Z // 2)
    mentor_done()

    def on_first(j):
        s1(away(j)).wait()
        second_step(j)

    each(Z, on_first, 1)
    each(Z, third_step, 1)
    mentor_second()
    each(Z, fill_picks)
    mentor_third()
    load_weights.wait()
    fourth_step(0)

    def on_third(j):
        fourth_step(j)
        last_step(j - 1)

    each(Z, on_third, 1)
    last_step(Z - 1)

    def combine(buf, n):
        tops = [buf[j, :tiles] for j in range(n)]
        sums = [buf[j, tiles:] for j in range(n)]
        top = functools.reduce(jnp.maximum, tops)
        total = functools.reduce(jnp.add, [s * jnp.exp(m - top) for s, m in zip(sums, tops)])
        return top, total

    stat_stages[0][0]()
    stat_stages[0][1]()
    top_s, sum_s = combine(stat_voc, NV)
    stat_y[y, :tiles] = top_s
    stat_y[y, tiles:] = sum_s
    stat_stages[1][0]()
    stat_stages[1][1]()
    top_s, sum_s = combine(stat_y, Y)
    stat_z[z, :tiles] = top_s
    stat_z[z, tiles:] = sum_s
    stat_stages[2][0]()
    mentor_stages[2][1]()
    table_top = jnp.concatenate(
        [mentor_z[i, j, 0:1] for i in range(Z) for j in range(Y)], axis=0
    ).astype(BF16)
    table_log = jnp.concatenate(
        [mentor_z[i, j, 1:2] for i in range(Z) for j in range(Y)], axis=0
    )
    log_hi = table_log.astype(BF16)
    rest = table_log - log_hi.astype(F32)
    log_mid = rest.astype(BF16)
    log_lo = (rest - log_mid.astype(F32)).astype(BF16)
    stat_stages[2][1]()
    top_s, sum_s = combine(stat_z, Z)
    stat_voc[0, :tiles] = top_s
    stat_voc[0, tiles:] = jnp.log(jnp.where(sum_s > 0.0, sum_s, 1.0))

    ends = []
    total = jnp.int32(0)
    for j in range(lengths.shape[0]):
        total = total + lengths[j]
        ends.append(total - 1)

    own_block.wait()
    join(teacher.at[pl.ds(0, (NT - 1) * R), :], t_sem)

    def mate(k):
        return copy(mate_send.at[k], mate_recv.at[k], mate_sem, k, at(dc=1))

    def r1a(k, i):
        return copy(
            folded.at[k, :, mod(x + i, X), :, pl.ds(0, PA)],
            first_a.at[k, i - 1],
            r1a_sem,
            k,
            at(dx=i),
        )

    def r1b(k, i):
        return copy(
            folded.at[k, mod(y + i, Y), :, :, pl.ds(PA, PA)],
            first_b.at[k, i - 1],
            r1b_sem,
            k,
            at(dy=i),
        )

    def r1c(k):
        return copy(
            folded.at[k, :, :, :, pl.ds(2 * PA, PC)], first_c.at[k], r1c_sem, 0, at(dz=k + 1)
        )

    loss_voc[voc] = jnp.zeros((8, LANES), F32)

    def gradient(k):
        zc = mod(z + 1 + k, Z)
        here = pl.ds(pl.multiple_of(zc * CH, CH), CH)
        wanted = wanted_rows[here, :]
        block = wanted // R
        pick = (lax.broadcasted_iota(jnp.int32, (CH, NT), 1) == block).astype(F32).astype(BF16)
        lane = lax.broadcasted_iota(jnp.int32, (CH, LANES), 1) == (wanted - block * R)

        def take(table):
            return jnp.dot(pick, table, preferred_element_type=F32)

        def one(value):
            return jnp.sum(jnp.where(lane, value, 0.0), axis=1, keepdims=True)

        teacher_top = one(take(table_top))
        teacher_log = one(take(log_hi) + take(log_mid) + take(log_lo))
        row_of = lax.broadcasted_iota(jnp.int32, (8, LANES), 0)

        def student(tile):
            value = stat_voc[0, tile + zc // per_tile]
            first_row = mod(zc, per_tile) * nb
            picked = [
                jnp.sum(jnp.where(row_of == first_row + j, value, 0.0), axis=0, keepdims=True)
                for j in range(nb)
            ]
            return jnp.concatenate([to_column(row) for row in picked], axis=0)

        student_top = student(0)
        student_log = student(tiles)
        place = lax.broadcasted_iota(jnp.int32, (CH, 1), 0) + zc * CH
        valid = jnp.ones((CH, 1), F32)
        for end in ends:
            valid = jnp.where(place == end, 0.0, valid)
        taken = jnp.dot(picks[here, :], teacher[...], preferred_element_type=F32) / TEMPERATURE
        log_teacher = (taken - teacher_top) - teacher_log
        log_student = (scores[here, :] - student_top) - student_log
        p_teacher = jnp.exp(log_teacher)
        p_student = jnp.exp(log_student)
        kl = jnp.sum(p_teacher * (log_teacher - log_student), axis=1, keepdims=True)
        grad = ((SCALE * TEMPERATURE) * valid * (p_student - p_teacher)).astype(BF16)
        slope[here, :] = grad

        def product(c):
            return lax.dot_general(
                grad,
                weights[pl.ds(pl.multiple_of(c * HALF, HALF), HALF), :],
                (((1,), (1,)), ((), ())),
                preferred_element_type=F32,
            )

        mate_send[k] = product(1 - core).astype(BF16)
        mate(k).start()
        own_half[mod(k, 2)] = product(core)
        loss_voc[voc] = loss_voc[voc] + jnp.sum(valid * kl, axis=0, keepdims=True)

    def fold_mate(k):
        mate(k).wait()
        value = own_half[mod(k, 2)] + mate_recv[k].astype(F32)
        folded[k] = value.astype(BF16).reshape(Y, X, 16, HALF)
        each(X, lambda i: r1a(k, i).start(), 1)
        each(Y, lambda i: r1b(k, i).start(), 1)

        @pl.when(k < Z - 1)
        def _():
            r1c(k).start()

    def weight_part(b):
        wide = gathered[b // 2, mod(b, 2)].reshape(N, CS)
        value = lax.dot_general(
            wide, slope[...], (((0,), (0,)), ((), ())), preferred_element_type=F32
        )
        grad_weight[pl.ds(pl.multiple_of(b * CS, CS), CS), :] = value.astype(BF16)

    def r2a(k, i):
        return copy(second_a.at[k, mod(y + i, Y)], got_a.at[k, i - 1], r2a_sem, k, at(dy=i))

    def r2b(k, i):
        return copy(second_b.at[k, mod(x + i, X)], got_b.at[k, i - 1], r2b_sem, k, at(dx=i))

    def add(value, others):
        for other in others:
            value = value + other.astype(F32)
        return value

    def fold_first(k):
        join(first_a.at[k], r1a_sem, k)
        value = folded[k, :, x, :, :PA].astype(F32)
        second_a[k] = add(value, [first_a[k, i] for i in range(X - 1)]).astype(BF16)
        each(Y, lambda i: r2a(k, i).start(), 1)
        join(first_b.at[k], r1b_sem, k)
        value = folded[k, y, :, :, PA : 2 * PA].astype(F32)
        second_b[k] = add(value, [first_b[k, i] for i in range(Y - 1)]).astype(BF16)
        each(X, lambda i: r2b(k, i).start(), 1)

    def fold_second(k):
        join(got_a.at[k], r2a_sem, k)
        join(got_b.at[k], r2b_sem, k)
        left = add(second_a[k, y].astype(F32), [got_a[k, i] for i in range(Y - 1)])
        right = add(second_b[k, x].astype(F32), [got_b[k, i] for i in range(X - 1)])
        last[0, k] = jnp.concatenate([left, right], axis=1).astype(BF16)

    def r2c(i):
        return copy(second_c.at[mod(y + i, Y)], got_c.at[i - 1], r2c_sem, 0, at(dy=i))

    def r3c(i):
        return copy(third_c.at[mod(x + i, X)], got_d.at[i - 1], r3c_sem, 0, at(dx=i))

    def fold_first_c():
        join(first_c, r1c_sem)
        value = folded[Z - 1, :, :, :, 2 * PA :].astype(F32)
        second_c[...] = add(value, [first_c[k] for k in range(Z - 1)]).astype(BF16)
        each(Y, lambda i: r2c(i).start(), 1)

    def fold_second_c():
        join(got_c, r2c_sem)
        value = second_c[y].astype(F32)
        third_c[...] = add(value, [got_c[i] for i in range(Y - 1)]).astype(BF16)
        each(X, lambda i: r3c(i).start(), 1)

    def r3(k):
        return copy(last.at[0, k], last.at[1, k], r3_sem, 0, at(dz=k + 1))

    def forward(j):
        @pl.when(j < Z)
        def _():
            gradient(j)

        @pl.when(j >= 1)
        def _():
            fold_mate(j - 1)

    each(Z + 1, forward)
    loss_stages[0][0]()
    PER = NV // Z if NV > Z else 1
    LAG = 2

    def backward(j):
        @pl.when(j < Z)
        def _():
            fold_first(j)
            for i in range(PER):
                weight_part(j * PER + i)

        @pl.when(j == 1)
        def _():
            loss_stages[0][1]()
            loss_y[y] = functools.reduce(jnp.add, [loss_voc[i] for i in range(NV)])
            loss_stages[1][0]()

        @pl.when(j == Z - 3)
        def _():
            loss_stages[1][1]()
            loss_z[z] = functools.reduce(jnp.add, [loss_y[i] for i in range(Y)])
            loss_stages[2][0]()

        @pl.when(j == Z - 1)
        def _():
            fold_first_c()

        @pl.when(j == Z)
        def _():
            fold_second_c()

        @pl.when(j >= LAG)
        def _():
            fold_second(j - LAG)

        @pl.when((j >= LAG) & (j < Z + LAG - 1))
        def _():
            r3(j - LAG).start()

    each(Z + LAG, backward)
    loss_stages[2][1]()
    loss = functools.reduce(jnp.add, [loss_z[j] for j in range(Z)])
    loss_out[0, 0] = jnp.max(TEMPERATURE * TEMPERATURE * loss / (N - lengths.shape[0]))
    join(last.at[1, pl.ds(0, Z - 1)], r3_sem)
    join(got_d, r3c_sem)
    value = add(last[0, Z - 1].astype(F32), [last[1, k] for k in range(Z - 1)])
    right = add(third_c[x].astype(F32), [got_d[i] for i in range(X - 1)])
    value = jnp.concatenate([value, right], axis=1)
    final[...] = value
    swap = copy(final.at[pl.ds(pl.multiple_of((1 - core) * 8, 8), 8), :], final_recv, final_sem, 0, at(dc=1))
    swap.start()
    mine = jnp.where(core == 0, value[:8], value[8:])
    swap.wait()
    theirs = final_recv[...]
    grad_hidden[:, :HALF] = jnp.where(core == 0, mine, theirs).astype(BF16)
    grad_hidden[:, HALF:] = jnp.where(core == 0, theirs, mine).astype(BF16)


def body(dims, hidden, weights, mentor, rows, lengths):
    Z, Y, X, R, V, D = dims
    NT, NV, CH = Z * Y, X * 2, Y * R
    N, HALF, CS = Z * CH, D // 2, D // NV
    PC = HALF // 4
    PA = (HALF - PC) // 2
    vmem = pl.BlockSpec(memory_space=pltpu.VMEM)
    anywhere = pl.BlockSpec(memory_space=pl.ANY)
    nb = max(1, CH // LANES)
    tiles = max(1, Z * nb // 8)
    dma = lambda n: pltpu.SemaphoreType.DMA((2, n))
    loss, grad_hidden, grad_weight = pl.pallas_call(
        functools.partial(kernel, dims),
        out_shape=(
            jax.ShapeDtypeStruct((1, 1), F32),
            jax.ShapeDtypeStruct((8, D), BF16),
            jax.ShapeDtypeStruct((D, V), BF16),
        ),
        in_specs=[anywhere, anywhere, anywhere, vmem, pl.BlockSpec(memory_space=pltpu.SMEM)],
        out_specs=(pl.BlockSpec(memory_space=pltpu.SMEM), vmem, vmem),
        scratch_shapes=[
            pltpu.VMEM((D, V), BF16),
            pltpu.VMEM((R, V * NT), BF16),
            pltpu.VMEM((N, 1), jnp.int32),
            pltpu.VMEM((R, LANES), F32),
            pltpu.VMEM((R, LANES), F32),
            pltpu.VMEM((X, 2, Z, Y, R, CS), BF16),
            pltpu.VMEM((N, V), BF16),
            pltpu.VMEM((N, N), BF16),
            pltpu.VMEM((N, V), F32),
            pltpu.VMEM((N, V), BF16),
            pltpu.VMEM((Z, CH, HALF), BF16),
            pltpu.VMEM((Z, CH, HALF), BF16),
            pltpu.VMEM((2, CH, HALF), F32),
            pltpu.VMEM((Z, Y, X, 16, HALF), BF16),
            pltpu.VMEM((Z, X - 1, Y, 16, PA), BF16),
            pltpu.VMEM((Z, Y - 1, X, 16, PA), BF16),
            pltpu.VMEM((Z, Y, 16, PA), BF16),
            pltpu.VMEM((Z, X, 16, PA), BF16),
            pltpu.VMEM((Z, Y - 1, 16, PA), BF16),
            pltpu.VMEM((Z, X - 1, 16, PA), BF16),
            pltpu.VMEM((Z - 1, Y, X, 16, PC), BF16),
            pltpu.VMEM((Y, X, 16, PC), BF16),
            pltpu.VMEM((Y - 1, X, 16, PC), BF16),
            pltpu.VMEM((X, 16, PC), BF16),
            pltpu.VMEM((X - 1, 16, PC), BF16),
            pltpu.VMEM((2, Z, 16, 2 * PA), BF16),
            pltpu.VMEM((16, HALF), F32),
            pltpu.VMEM((8, HALF), F32),
            pltpu.VMEM((NV, 2 * tiles, 8, LANES), F32),
            pltpu.VMEM((Y, 2 * tiles, 8, LANES), F32),
            pltpu.VMEM((Z, 2 * tiles, 8, LANES), F32),
            pltpu.VMEM((NV, 8, LANES), F32),
            pltpu.VMEM((Y, 8, LANES), F32),
            pltpu.VMEM((Z, Y, 8, LANES), F32),
            pltpu.VMEM((NV, 8, LANES), F32),
            pltpu.VMEM((Y, 8, LANES), F32),
            pltpu.VMEM((Z, 8, LANES), F32),
            pltpu.SemaphoreType.DMA((4,)),
            dma(Z),
            dma(1),
            dma(Z),
            dma(Z),
            dma(Z),
            dma(Z),
            dma(Z),
            dma(1),
            dma(1),
            dma(1),
            dma(1),
            dma(1),
            dma(1),
            dma(1),
            dma(1),
            dma(1),
            dma(Z),
            dma(Z),
            dma(Z),
            dma(Z),
            dma(Z),
            dma(1),
            dma(1),
            dma(1),
            dma(1),
            dma(1),
        ],
        compiler_params=pltpu.CompilerParams(
            collective_id=0, has_side_effects=True, vmem_limit_bytes=63 * 2**20
        ),
    )(hidden, weights, mentor, rows.reshape(Z * nb, CH // nb), lengths)
    return loss.reshape(()), grad_hidden, grad_weight


def solution(mesh):
    NT, NV = mesh.shape["tok"], mesh.shape["voc"]
    Y = 1 << ((NT.bit_length() - 1) // 2)
    Z, X = NT // Y, NV // 2

    def run(hidden, weights, mentor, rows, lengths):
        N, D = hidden.shape
        dims = (Z, Y, X, N // NT, weights.shape[1] // (NT * NV), D)
        return jax.shard_map(
            functools.partial(body, dims),
            mesh=mesh,
            in_specs=(P("tok", None), P(None, ("voc", "tok")), P("tok", "voc"), P(), P()),
            out_specs=(P(), P(("tok", "voc"), None), P(None, ("voc", "tok"))),
            check_vma=False,
        )(hidden, weights, mentor, rows, lengths)

    return run
```

```python
import functools

import jax
import jax.numpy as jnp
from jax import lax
from jax.experimental import pallas as pl
from jax.experimental.pallas import tpu as pltpu
from jax.sharding import PartitionSpec as P

MESH = pl.DeviceIdType.MESH
F32 = jnp.float32
BF16 = jnp.bfloat16
TEMPERATURE = 2.0
SCALE = 512.0
LANES = 128


def mod(a, n):
    return lax.rem(a, n)


def kernel(
    dims,
    hidden,
    weights_hbm,
    mentor_hbm,
    rows,
    lengths,
    loss_out,
    grad_hidden,
    grad_weight,
    weights,
    mentor,
    wanted_rows,
    run_top,
    run_sum,
    gathered,
    teacher,
    picks,
    scores,
    slope,
    mate_send,
    mate_recv,
    own_half,
    folded,
    first_a,
    first_b,
    second_a,
    second_b,
    got_a,
    got_b,
    first_c,
    second_c,
    got_c,
    third_c,
    got_d,
    last,
    final,
    final_recv,
    stat_voc,
    stat_y,
    stat_z,
    mentor_voc,
    mentor_y,
    mentor_z,
    loss_voc,
    loss_y,
    loss_z,
    local_sem,
    s1_sem,
    t_sem,
    s2a_sem,
    s2b_sem,
    s3a_sem,
    s3b_sem,
    c_sem,
    stat_voc_sem,
    stat_y_sem,
    stat_z_sem,
    mentor_voc_sem,
    mentor_y_sem,
    mentor_z_sem,
    loss_voc_sem,
    loss_y_sem,
    loss_z_sem,
    mate_sem,
    r1a_sem,
    r1b_sem,
    r2a_sem,
    r2b_sem,
    r1c_sem,
    r2c_sem,
    r3c_sem,
    r3_sem,
    final_sem,
):
    Z, Y, X, R, V, D = dims
    tok, voc = lax.axis_index("tok"), lax.axis_index("voc")
    z, y = tok // Y, mod(tok, Y)
    x, core = voc // 2, mod(voc, 2)
    NT, NV = Z * Y, X * 2
    CH = Y * R
    N = Z * CH
    HALF = D // 2
    PC = HALF // 4
    PA = (HALF - PC) // 2
    CS = D // NV
    RA = (3 * R // 4) // 16 * 16
    nb = max(1, CH // LANES)
    q = CH // nb
    per_tile = 8 // nb
    tiles = max(1, Z // per_tile)

    def at(dz=0, dy=0, dx=0, dc=0):
        return (
            mod(z + dz, Z) * Y + mod(y + dy, Y),
            mod(x + dx, X) * 2 + mod(core + dc, 2),
        )

    def copy(src, dst, sems, index, device):
        return pltpu.make_async_remote_copy(
            src_ref=src,
            dst_ref=dst,
            send_sem=sems.at[0, index],
            recv_sem=sems.at[1, index],
            device_id=device,
            device_id_type=MESH,
        )

    def join(block, sems, index=0):
        copy(block, block, sems, index, at(dc=1)).wait()

    def each(n, body, start=0):
        def step(i, carry):
            body(i)
            return carry

        lax.fori_loop(start, n, step, 0)

    load_mentor = pltpu.make_async_copy(mentor_hbm, mentor, local_sem.at[2])
    load_weights = pltpu.make_async_copy(weights_hbm, weights, local_sem.at[3])
    load_mentor.start()
    load_weights.start()

    def turns(i, n):
        return jnp.where(mod(i, 2) == 1, n // 2 - (i + 1) // 2, n // 2 + i // 2)

    barrier = pltpu.get_barrier_semaphore()

    def greet_tok(i):
        pl.semaphore_signal(barrier, inc=1, device_id=at(dz=i // Y, dy=mod(i, Y)), device_id_type=MESH)

    def greet_voc(i):
        pl.semaphore_signal(barrier, inc=1, device_id=at(dx=i // 2, dc=mod(i, 2)), device_id_type=MESH)

    each(NT, greet_tok, 1)
    each(NV, greet_voc, 1)
    pl.semaphore_wait(barrier, NT - 1 + NV - 1)

    def s1(i):
        return copy(
            hidden.at[:, pl.ds(pl.multiple_of(voc * CS, CS), CS)],
            gathered.at[x, core, z, y],
            s1_sem,
            i,
            at(dz=i),
        )

    each(Z - 1, lambda i: s1(turns(i, Z)).start())
    own_columns = pltpu.make_async_copy(
        hidden.at[:, pl.ds(pl.multiple_of(voc * CS, CS), CS)],
        gathered.at[x, core, z, y],
        local_sem.at[0],
    )
    own_columns.start()

    def t_copy(i):
        device = at(dz=turns(i // Y, Z), dy=turns(mod(i, Y), Y))
        return copy(
            mentor_hbm.at[:, pl.ds(pl.multiple_of(device[0] * V, V), V)],
            teacher.at[pl.ds(pl.multiple_of(tok * R, R), R), :],
            t_sem,
            0,
            device,
        )

    each(NT - 1, lambda i: t_copy(i).start())
    own_block = pltpu.make_async_copy(
        mentor_hbm.at[:, pl.ds(pl.multiple_of(tok * V, V), V)],
        teacher.at[pl.ds(pl.multiple_of(tok * R, R), R), :],
        local_sem.at[1],
    )
    own_block.start()

    def stage(buf, sems, slot, n, target):
        def c(i):
            return copy(buf.at[slot], buf.at[slot], sems, 0, target(i))

        def start():
            each(n, lambda i: c(i).start(), 1)

        def wait():
            join(buf.at[pl.ds(0, n - 1)], sems)

        return start, wait

    def three(voc_buf, y_buf, z_buf, voc_sem, y_sem, z_sem):
        return (
            stage(voc_buf, voc_sem, voc, NV, lambda i: at(dx=i // 2, dc=mod(i, 2))),
            stage(y_buf, y_sem, y, Y, lambda i: at(dy=i)),
            stage(z_buf, z_sem, z, Z, lambda i: at(dz=i)),
        )

    stat_stages = three(stat_voc, stat_y, stat_z, stat_voc_sem, stat_y_sem, stat_z_sem)
    mentor_stages = three(
        mentor_voc, mentor_y, mentor_z, mentor_voc_sem, mentor_y_sem, mentor_z_sem
    )
    loss_stages = three(loss_voc, loss_y, loss_z, loss_voc_sem, loss_y_sem, loss_z_sem)

    eye = lax.broadcasted_iota(jnp.int32, (q, LANES), 0) == lax.broadcasted_iota(
        jnp.int32, (q, LANES), 1
    )
    eye_rows = lax.broadcasted_iota(jnp.int32, (R, LANES), 0) == lax.broadcasted_iota(
        jnp.int32, (R, LANES), 1
    )

    def columns_of(i):
        return mentor[:, pl.ds(pl.multiple_of(i * V, V), V)].astype(F32) / TEMPERATURE

    def fold(op, value):
        total = value[:, :LANES]
        for j in range(1, V // LANES):
            total = op(total, value[:, j * LANES : (j + 1) * LANES])
        return total

    def to_lanes(column, mask):
        return jnp.sum(jnp.where(mask, column, 0.0), axis=0, keepdims=True)

    run_top[...] = jnp.full((R, LANES), -jnp.inf, F32)
    run_sum[...] = jnp.zeros((R, LANES), F32)

    def mentor_part(j):
        old = run_top[...]
        top = lax.fori_loop(
            j * Y, (j + 1) * Y, lambda i, m: jnp.maximum(m, fold(jnp.maximum, columns_of(i))), old
        )
        wide = jnp.concatenate([top] * (V // LANES), axis=1)
        run_sum[...] = lax.fori_loop(
            j * Y,
            (j + 1) * Y,
            lambda i, s: s + fold(jnp.add, jnp.exp(columns_of(i) - wide)),
            run_sum[...] * jnp.exp(old - top),
        )
        run_top[...] = top

    def mentor_done():
        top_t = jnp.max(run_top[...], axis=1, keepdims=True)
        sum_t = jnp.sum(run_sum[...] * jnp.exp(run_top[...] - top_t), axis=1, keepdims=True)
        mentor_voc[voc] = jnp.concatenate(
            [to_lanes(top_t, eye_rows), to_lanes(sum_t, eye_rows), jnp.zeros((6, LANES), F32)],
            axis=0,
        )
        mentor_stages[0][0]()

    def to_column(row):
        return jnp.sum(jnp.where(eye[:, : row.shape[1]], row, 0.0), axis=1, keepdims=True)

    def fill_picks(k):
        here = pl.ds(pl.multiple_of(k * CH, CH), CH)
        parts = [to_column(rows[pl.ds(k * nb + j, 1), :].astype(F32)) for j in range(nb)]
        wanted = jnp.concatenate(parts, axis=0).astype(jnp.int32)
        wanted_rows[here, :] = wanted
        places = lax.broadcasted_iota(jnp.int32, (CH, N), 1)
        picks[here, :] = jnp.where(places == wanted, 1.0, 0.0).astype(BF16)

    def mentor_second():
        mentor_stages[0][1]()
        tops = [mentor_voc[j, 0:1] for j in range(NV)]
        sums = [mentor_voc[j, 1:2] for j in range(NV)]
        top_t = functools.reduce(jnp.maximum, tops)
        sum_t = functools.reduce(jnp.add, [s * jnp.exp(m - top_t) for s, m in zip(sums, tops)])
        used = lax.broadcasted_iota(jnp.int32, (1, LANES), 1) < R
        sum_t = jnp.where(used, sum_t, 1.0)
        mentor_y[y] = jnp.concatenate([top_t, jnp.log(sum_t), jnp.zeros((6, LANES), F32)], axis=0)
        mentor_stages[1][0]()

    def mentor_third():
        mentor_stages[1][1]()
        for j in range(Y):
            mentor_z[z, j] = mentor_y[j]
        mentor_stages[2][0]()

    first, second = pl.ds(0, RA), pl.ds(RA, R - RA)
    stat_voc[voc] = jnp.zeros((2 * tiles, 8, LANES), F32)

    def away(j):
        return turns(mod(j + Z - 1, Z), Z)

    def chunk(j):
        return mod(z + Z - away(j), Z)

    def s2a(j, i):
        block = gathered.at[x, core, chunk(j), y, first]
        return copy(block, block, s2a_sem, j, at(dy=i))

    def s2b(j, i):
        block = gathered.at[x, core, chunk(j), y, second]
        return copy(block, block, s2b_sem, j, at(dx=i))

    def s3a(j, i):
        block = gathered.at[x, core, chunk(j), :, first]
        return copy(block, block, s3a_sem, j, at(dx=i))

    def s3b(j, i):
        block = gathered.at[:, core, chunk(j), y, second]
        return copy(block, block, s3b_sem, j, at(dy=i))

    def c(j):
        block = gathered.at[:, core, chunk(j)]
        return copy(block, block, c_sem, j, at(dc=1))

    def hidden_of(b, k):
        return gathered[b // 2, b % 2, k].reshape(CH, CS)

    def score(k):
        here = pl.ds(pl.multiple_of(k * CH, CH), CH)
        wide = jnp.concatenate([hidden_of(b, k) for b in range(NV)], axis=1)
        value = jnp.dot(wide, weights[...], preferred_element_type=F32) / TEMPERATURE
        scores[here, :] = value
        top = jnp.max(value, axis=1, keepdims=True)
        total = jnp.sum(jnp.exp(value - top), axis=1, keepdims=True)
        group = lax.broadcasted_iota(jnp.int32, (8, LANES), 0) // nb == mod(k, per_tile)

        def put(column, tile):
            parts = [to_lanes(column[j * q : (j + 1) * q], eye) for j in range(nb)]
            value = jnp.concatenate(parts * per_tile, axis=0)
            stat_voc[voc, tile] = jnp.where(group, value, stat_voc[voc, tile])

        put(top, k // per_tile)
        put(total, tiles + k // per_tile)

    def second_step(j):
        each(Y, lambda i: s2a(j, i).start(), 1)
        each(X, lambda i: s2b(j, i).start(), 1)

    def third_step(j):
        join(gathered.at[x, core, chunk(j), pl.ds(0, Y - 1), first], s2a_sem, j)
        each(X, lambda i: s3a(j, i).start(), 1)
        join(gathered.at[pl.ds(0, X - 1), core, chunk(j), y, second], s2b_sem, j)
        each(Y, lambda i: s3b(j, i).start(), 1)

    def fourth_step(j):
        join(gathered.at[pl.ds(0, X - 1), core, chunk(j), :, first], s3a_sem, j)
        join(gathered.at[:, core, chunk(j), pl.ds(0, Y - 1), second], s3b_sem, j)
        c(j).start()

    def last_step(j):
        c(j).wait()
        score(chunk(j))

    own_columns.wait()
    second_step(0)
    load_mentor.wait()
    each(Z // 2, mentor_part)
    third_step(0)
    each(Z, mentor_part, Z // 2)
    mentor_done()

    def on_first(j):
        s1(away(j)).wait()
        second_step(j)

    each(Z, on_first, 1)
    each(Z, third_step, 1)
    mentor_second()
    each(Z, fill_picks)
    mentor_third()
    load_weights.wait()
    fourth_step(0)

    def on_third(j):
        fourth_step(j)
        last_step(j - 1)

    each(Z, on_third, 1)
    last_step(Z - 1)

    def combine(buf, n):
        tops = [buf[j, :tiles] for j in range(n)]
        sums = [buf[j, tiles:] for j in range(n)]
        top = functools.reduce(jnp.maximum, tops)
        total = functools.reduce(jnp.add, [s * jnp.exp(m - top) for s, m in zip(sums, tops)])
        return top, total

    stat_stages[0][0]()
    stat_stages[0][1]()
    top_s, sum_s = combine(stat_voc, NV)
    stat_y[y, :tiles] = top_s
    stat_y[y, tiles:] = sum_s
    stat_stages[1][0]()
    stat_stages[1][1]()
    top_s, sum_s = combine(stat_y, Y)
    stat_z[z, :tiles] = top_s
    stat_z[z, tiles:] = sum_s
    stat_stages[2][0]()
    mentor_stages[2][1]()
    table_top = jnp.concatenate(
        [mentor_z[i, j, 0:1] for i in range(Z) for j in range(Y)], axis=0
    ).astype(BF16)
    table_log = jnp.concatenate(
        [mentor_z[i, j, 1:2] for i in range(Z) for j in range(Y)], axis=0
    )
    log_hi = table_log.astype(BF16)
    rest = table_log - log_hi.astype(F32)
    log_mid = rest.astype(BF16)
    log_lo = (rest - log_mid.astype(F32)).astype(BF16)
    stat_stages[2][1]()
    top_s, sum_s = combine(stat_z, Z)
    stat_voc[0, :tiles] = top_s
    stat_voc[0, tiles:] = jnp.log(jnp.where(sum_s > 0.0, sum_s, 1.0))

    ends = []
    total = jnp.int32(0)
    for j in range(lengths.shape[0]):
        total = total + lengths[j]
        ends.append(total - 1)

    own_block.wait()
    join(teacher.at[pl.ds(0, (NT - 1) * R), :], t_sem)

    def mate(k):
        return copy(mate_send.at[k], mate_recv.at[k], mate_sem, k, at(dc=1))

    def r1a(k, i):
        return copy(
            folded.at[k, :, mod(x + i, X), :, pl.ds(0, PA)],
            first_a.at[k, i - 1],
            r1a_sem,
            k,
            at(dx=i),
        )

    def r1b(k, i):
        return copy(
            folded.at[k, mod(y + i, Y), :, :, pl.ds(PA, PA)],
            first_b.at[k, i - 1],
            r1b_sem,
            k,
            at(dy=i),
        )

    def r1c(k):
        return copy(
            folded.at[k, :, :, :, pl.ds(2 * PA, PC)], first_c.at[k], r1c_sem, 0, at(dz=turns(k, Z))
        )

    loss_voc[voc] = jnp.zeros((8, LANES), F32)

    def gradient(k):
        zc = mod(z + turns(k, Z), Z)
        here = pl.ds(pl.multiple_of(zc * CH, CH), CH)
        wanted = wanted_rows[here, :]
        block = wanted // R
        pick = (lax.broadcasted_iota(jnp.int32, (CH, NT), 1) == block).astype(F32).astype(BF16)
        lane = lax.broadcasted_iota(jnp.int32, (CH, LANES), 1) == (wanted - block * R)

        def take(table):
            return jnp.dot(pick, table, preferred_element_type=F32)

        def one(value):
            return jnp.sum(jnp.where(lane, value, 0.0), axis=1, keepdims=True)

        teacher_top = one(take(table_top))
        teacher_log = one(take(log_hi) + take(log_mid) + take(log_lo))
        row_of = lax.broadcasted_iota(jnp.int32, (8, LANES), 0)

        def student(tile):
            value = stat_voc[0, tile + zc // per_tile]
            first_row = mod(zc, per_tile) * nb
            picked = [
                jnp.sum(jnp.where(row_of == first_row + j, value, 0.0), axis=0, keepdims=True)
                for j in range(nb)
            ]
            return jnp.concatenate([to_column(row) for row in picked], axis=0)

        student_top = student(0)
        student_log = student(tiles)
        place = lax.broadcasted_iota(jnp.int32, (CH, 1), 0) + zc * CH
        valid = jnp.ones((CH, 1), F32)
        for end in ends:
            valid = jnp.where(place == end, 0.0, valid)
        taken = jnp.dot(picks[here, :], teacher[...], preferred_element_type=F32) / TEMPERATURE
        log_teacher = (taken - teacher_top) - teacher_log
        log_student = (scores[here, :] - student_top) - student_log
        p_teacher = jnp.exp(log_teacher)
        p_student = jnp.exp(log_student)
        kl = jnp.sum(p_teacher * (log_teacher - log_student), axis=1, keepdims=True)
        grad = ((SCALE * TEMPERATURE) * valid * (p_student - p_teacher)).astype(BF16)
        slope[here, :] = grad

        def product(c):
            return lax.dot_general(
                grad,
                weights[pl.ds(pl.multiple_of(c * HALF, HALF), HALF), :],
                (((1,), (1,)), ((), ())),
                preferred_element_type=F32,
            )

        mate_send[k] = product(1 - core).astype(BF16)
        mate(k).start()
        own_half[mod(k, 2)] = product(core)
        loss_voc[voc] = loss_voc[voc] + jnp.sum(valid * kl, axis=0, keepdims=True)

    def fold_mate(k):
        mate(k).wait()
        value = own_half[mod(k, 2)] + mate_recv[k].astype(F32)
        folded[k] = value.astype(BF16).reshape(Y, X, 16, HALF)
        each(X, lambda i: r1a(k, i).start(), 1)
        each(Y, lambda i: r1b(k, i).start(), 1)

        @pl.when(k < Z - 1)
        def _():
            r1c(k).start()

    def weight_part(b):
        wide = gathered[b // 2, mod(b, 2)].reshape(N, CS)
        value = lax.dot_general(
            wide, slope[...], (((0,), (0,)), ((), ())), preferred_element_type=F32
        )
        grad_weight[pl.ds(pl.multiple_of(b * CS, CS), CS), :] = value.astype(BF16)

    def r2a(k, i):
        return copy(second_a.at[k, mod(y + i, Y)], got_a.at[k, i - 1], r2a_sem, k, at(dy=i))

    def r2b(k, i):
        return copy(second_b.at[k, mod(x + i, X)], got_b.at[k, i - 1], r2b_sem, k, at(dx=i))

    def add(value, others):
        for other in others:
            value = value + other.astype(F32)
        return value

    def fold_first(k):
        join(first_a.at[k], r1a_sem, k)
        value = folded[k, :, x, :, :PA].astype(F32)
        second_a[k] = add(value, [first_a[k, i] for i in range(X - 1)]).astype(BF16)
        each(Y, lambda i: r2a(k, i).start(), 1)
        join(first_b.at[k], r1b_sem, k)
        value = folded[k, y, :, :, PA : 2 * PA].astype(F32)
        second_b[k] = add(value, [first_b[k, i] for i in range(Y - 1)]).astype(BF16)
        each(X, lambda i: r2b(k, i).start(), 1)

    def fold_second(k):
        join(got_a.at[k], r2a_sem, k)
        join(got_b.at[k], r2b_sem, k)
        left = add(second_a[k, y].astype(F32), [got_a[k, i] for i in range(Y - 1)])
        right = add(second_b[k, x].astype(F32), [got_b[k, i] for i in range(X - 1)])
        last[0, k] = jnp.concatenate([left, right], axis=1).astype(BF16)

    def r2c(i):
        return copy(second_c.at[mod(y + i, Y)], got_c.at[i - 1], r2c_sem, 0, at(dy=i))

    def r3c(i):
        return copy(third_c.at[mod(x + i, X)], got_d.at[i - 1], r3c_sem, 0, at(dx=i))

    def fold_first_c():
        join(first_c, r1c_sem)
        value = folded[Z - 1, :, :, :, 2 * PA :].astype(F32)
        second_c[...] = add(value, [first_c[k] for k in range(Z - 1)]).astype(BF16)
        each(Y, lambda i: r2c(i).start(), 1)

    def fold_second_c():
        join(got_c, r2c_sem)
        value = second_c[y].astype(F32)
        third_c[...] = add(value, [got_c[i] for i in range(Y - 1)]).astype(BF16)
        each(X, lambda i: r3c(i).start(), 1)

    def r3(k):
        return copy(last.at[0, k], last.at[1, k], r3_sem, 0, at(dz=turns(k, Z)))

    def forward(j):
        @pl.when(j < Z)
        def _():
            gradient(j)

        @pl.when(j >= 1)
        def _():
            fold_mate(j - 1)

    each(Z + 1, forward)
    loss_stages[0][0]()
    PER = NV // Z if NV > Z else 1
    LAG = 2

    def backward(j):
        @pl.when(j < Z)
        def _():
            fold_first(j)
            for i in range(PER):
                weight_part(j * PER + i)

        @pl.when(j == 1)
        def _():
            loss_stages[0][1]()
            loss_y[y] = functools.reduce(jnp.add, [loss_voc[i] for i in range(NV)])
            loss_stages[1][0]()

        @pl.when(j == Z - 3)
        def _():
            loss_stages[1][1]()
            loss_z[z] = functools.reduce(jnp.add, [loss_y[i] for i in range(Y)])
            loss_stages[2][0]()

        @pl.when(j == Z - 1)
        def _():
            fold_first_c()

        @pl.when(j == Z)
        def _():
            fold_second_c()

        @pl.when(j >= LAG)
        def _():
            fold_second(j - LAG)

        @pl.when((j >= LAG) & (j < Z + LAG - 1))
        def _():
            r3(j - LAG).start()

    each(Z + LAG, backward)
    loss_stages[2][1]()
    loss = functools.reduce(jnp.add, [loss_z[j] for j in range(Z)])
    loss_out[0, 0] = jnp.max(TEMPERATURE * TEMPERATURE * loss / (N - lengths.shape[0]))
    join(last.at[1, pl.ds(0, Z - 1)], r3_sem)
    join(got_d, r3c_sem)
    value = add(last[0, Z - 1].astype(F32), [last[1, k] for k in range(Z - 1)])
    right = add(third_c[x].astype(F32), [got_d[i] for i in range(X - 1)])
    value = jnp.concatenate([value, right], axis=1)
    final[...] = value
    swap = copy(final.at[pl.ds(pl.multiple_of((1 - core) * 8, 8), 8), :], final_recv, final_sem, 0, at(dc=1))
    swap.start()
    mine = jnp.where(core == 0, value[:8], value[8:])
    swap.wait()
    theirs = final_recv[...]
    grad_hidden[:, :HALF] = jnp.where(core == 0, mine, theirs).astype(BF16)
    grad_hidden[:, HALF:] = jnp.where(core == 0, theirs, mine).astype(BF16)


def body(dims, hidden, weights, mentor, rows, lengths):
    Z, Y, X, R, V, D = dims
    NT, NV, CH = Z * Y, X * 2, Y * R
    N, HALF, CS = Z * CH, D // 2, D // NV
    PC = HALF // 4
    PA = (HALF - PC) // 2
    vmem = pl.BlockSpec(memory_space=pltpu.VMEM)
    anywhere = pl.BlockSpec(memory_space=pl.ANY)
    nb = max(1, CH // LANES)
    tiles = max(1, Z * nb // 8)
    dma = lambda n: pltpu.SemaphoreType.DMA((2, n))
    loss, grad_hidden, grad_weight = pl.pallas_call(
        functools.partial(kernel, dims),
        out_shape=(
            jax.ShapeDtypeStruct((1, 1), F32),
            jax.ShapeDtypeStruct((8, D), BF16),
            jax.ShapeDtypeStruct((D, V), BF16),
        ),
        in_specs=[anywhere, anywhere, anywhere, vmem, pl.BlockSpec(memory_space=pltpu.SMEM)],
        out_specs=(pl.BlockSpec(memory_space=pltpu.SMEM), vmem, vmem),
        scratch_shapes=[
            pltpu.VMEM((D, V), BF16),
            pltpu.VMEM((R, V * NT), BF16),
            pltpu.VMEM((N, 1), jnp.int32),
            pltpu.VMEM((R, LANES), F32),
            pltpu.VMEM((R, LANES), F32),
            pltpu.VMEM((X, 2, Z, Y, R, CS), BF16),
            pltpu.VMEM((N, V), BF16),
            pltpu.VMEM((N, N), BF16),
            pltpu.VMEM((N, V), F32),
            pltpu.VMEM((N, V), BF16),
            pltpu.VMEM((Z, CH, HALF), BF16),
            pltpu.VMEM((Z, CH, HALF), BF16),
            pltpu.VMEM((2, CH, HALF), F32),
            pltpu.VMEM((Z, Y, X, 16, HALF), BF16),
            pltpu.VMEM((Z, X - 1, Y, 16, PA), BF16),
            pltpu.VMEM((Z, Y - 1, X, 16, PA), BF16),
            pltpu.VMEM((Z, Y, 16, PA), BF16),
            pltpu.VMEM((Z, X, 16, PA), BF16),
            pltpu.VMEM((Z, Y - 1, 16, PA), BF16),
            pltpu.VMEM((Z, X - 1, 16, PA), BF16),
            pltpu.VMEM((Z - 1, Y, X, 16, PC), BF16),
            pltpu.VMEM((Y, X, 16, PC), BF16),
            pltpu.VMEM((Y - 1, X, 16, PC), BF16),
            pltpu.VMEM((X, 16, PC), BF16),
            pltpu.VMEM((X - 1, 16, PC), BF16),
            pltpu.VMEM((2, Z, 16, 2 * PA), BF16),
            pltpu.VMEM((16, HALF), F32),
            pltpu.VMEM((8, HALF), F32),
            pltpu.VMEM((NV, 2 * tiles, 8, LANES), F32),
            pltpu.VMEM((Y, 2 * tiles, 8, LANES), F32),
            pltpu.VMEM((Z, 2 * tiles, 8, LANES), F32),
            pltpu.VMEM((NV, 8, LANES), F32),
            pltpu.VMEM((Y, 8, LANES), F32),
            pltpu.VMEM((Z, Y, 8, LANES), F32),
            pltpu.VMEM((NV, 8, LANES), F32),
            pltpu.VMEM((Y, 8, LANES), F32),
            pltpu.VMEM((Z, 8, LANES), F32),
            pltpu.SemaphoreType.DMA((4,)),
            dma(Z),
            dma(1),
            dma(Z),
            dma(Z),
            dma(Z),
            dma(Z),
            dma(Z),
            dma(1),
            dma(1),
            dma(1),
            dma(1),
            dma(1),
            dma(1),
            dma(1),
            dma(1),
            dma(1),
            dma(Z),
            dma(Z),
            dma(Z),
            dma(Z),
            dma(Z),
            dma(1),
            dma(1),
            dma(1),
            dma(1),
            dma(1),
        ],
        compiler_params=pltpu.CompilerParams(
            collective_id=0, has_side_effects=True, vmem_limit_bytes=63 * 2**20
        ),
    )(hidden, weights, mentor, rows.reshape(Z * nb, CH // nb), lengths)
    return loss.reshape(()), grad_hidden, grad_weight


def solution(mesh):
    NT, NV = mesh.shape["tok"], mesh.shape["voc"]
    Y = 1 << ((NT.bit_length() - 1) // 2)
    Z, X = NT // Y, NV // 2

    def run(hidden, weights, mentor, rows, lengths):
        N, D = hidden.shape
        dims = (Z, Y, X, N // NT, weights.shape[1] // (NT * NV), D)
        return jax.shard_map(
            functools.partial(body, dims),
            mesh=mesh,
            in_specs=(P("tok", None), P(None, ("voc", "tok")), P("tok", "voc"), P(), P()),
            out_specs=(P(), P(("tok", "voc"), None), P(None, ("voc", "tok"))),
            check_vma=False,
        )(hidden, weights, mentor, rows, lengths)

    return run
```

```python
import functools

import jax
import jax.numpy as jnp
from jax import lax
from jax.experimental import pallas as pl
from jax.experimental.pallas import tpu as pltpu
from jax.sharding import PartitionSpec as P

MESH = pl.DeviceIdType.MESH
F32 = jnp.float32
BF16 = jnp.bfloat16
TEMPERATURE = 2.0
SCALE = 512.0
LANES = 128


def mod(a, n):
    return lax.rem(a, n)


def kernel(
    dims,
    hidden,
    weights_hbm,
    mentor_hbm,
    rows,
    lengths,
    loss_out,
    grad_hidden,
    grad_weight_hbm,
    grad_weight,
    weights,
    mentor,
    wanted_rows,
    run_top,
    run_sum,
    gathered,
    teacher,
    picks,
    scores,
    slope,
    mate_send,
    mate_recv,
    own_half,
    folded,
    first_a,
    first_b,
    second_a,
    second_b,
    got_a,
    got_b,
    first_c,
    second_c,
    got_c,
    third_c,
    got_d,
    last,
    arrived,
    stat_voc,
    stat_y,
    stat_z,
    mentor_voc,
    mentor_y,
    mentor_z,
    loss_voc,
    loss_y,
    loss_z,
    local_sem,
    s1_sem,
    t_sem,
    s2a_sem,
    s2b_sem,
    s3a_sem,
    s3b_sem,
    c_sem,
    stat_voc_sem,
    stat_y_sem,
    stat_z_sem,
    mentor_voc_sem,
    mentor_y_sem,
    mentor_z_sem,
    loss_voc_sem,
    loss_y_sem,
    loss_z_sem,
    mate_sem,
    r1a_sem,
    r1b_sem,
    r2a_sem,
    r2b_sem,
    r1c_sem,
    r2c_sem,
    r3c_sem,
    r3_sem,
):
    Z, Y, X, R, V, D = dims
    tok, voc = lax.axis_index("tok"), lax.axis_index("voc")
    z, y = tok // Y, mod(tok, Y)
    x, core = voc // 2, mod(voc, 2)
    NT, NV = Z * Y, X * 2
    CH = Y * R
    N = Z * CH
    HALF = D // 2
    PC = HALF // 4
    PA = (HALF - PC) // 2
    CS = D // NV
    RA = (3 * R // 4) // 16 * 16
    nb = max(1, CH // LANES)
    q = CH // nb
    per_tile = 8 // nb
    tiles = max(1, Z // per_tile)

    def at(dz=0, dy=0, dx=0, dc=0):
        return (
            mod(z + dz, Z) * Y + mod(y + dy, Y),
            mod(x + dx, X) * 2 + mod(core + dc, 2),
        )

    def copy(src, dst, sems, index, device):
        return pltpu.make_async_remote_copy(
            src_ref=src,
            dst_ref=dst,
            send_sem=sems.at[0, index],
            recv_sem=sems.at[1, index],
            device_id=device,
            device_id_type=MESH,
        )

    def join(block, sems, index=0):
        copy(block, block, sems, index, at(dc=1)).wait()

    def each(n, body, start=0):
        def step(i, carry):
            body(i)
            return carry

        lax.fori_loop(start, n, step, 0)

    load_mentor = pltpu.make_async_copy(mentor_hbm, mentor, local_sem.at[2])
    load_weights = pltpu.make_async_copy(weights_hbm, weights, local_sem.at[3])
    load_mentor.start()
    load_weights.start()

    def turns(i, n):
        return jnp.where(mod(i, 2) == 1, n // 2 - (i + 1) // 2, n // 2 + i // 2)

    barrier = pltpu.get_barrier_semaphore()

    def greet_tok(i):
        pl.semaphore_signal(barrier, inc=1, device_id=at(dz=i // Y, dy=mod(i, Y)), device_id_type=MESH)

    def greet_voc(i):
        pl.semaphore_signal(barrier, inc=1, device_id=at(dx=i // 2, dc=mod(i, 2)), device_id_type=MESH)

    def greet_cross(i):
        pl.semaphore_signal(barrier, inc=1, device_id=at(dz=i, dc=1), device_id_type=MESH)

    each(NT, greet_tok, 1)
    each(NV, greet_voc, 1)
    each(Z, greet_cross, 1)
    pl.semaphore_wait(barrier, NT - 1 + NV - 1 + Z - 1)

    def s1(i):
        return copy(
            hidden.at[:, pl.ds(pl.multiple_of(voc * CS, CS), CS)],
            gathered.at[x, core, z, y],
            s1_sem,
            i,
            at(dz=i),
        )

    each(Z - 1, lambda i: s1(turns(i, Z)).start())
    own_columns = pltpu.make_async_copy(
        hidden.at[:, pl.ds(pl.multiple_of(voc * CS, CS), CS)],
        gathered.at[x, core, z, y],
        local_sem.at[0],
    )
    own_columns.start()

    def t_copy(i):
        device = at(dz=turns(i // Y, Z), dy=turns(mod(i, Y), Y))
        return copy(
            mentor_hbm.at[:, pl.ds(pl.multiple_of(device[0] * V, V), V)],
            teacher.at[pl.ds(pl.multiple_of(tok * R, R), R), :],
            t_sem,
            0,
            device,
        )

    own_block = pltpu.make_async_copy(
        mentor_hbm.at[:, pl.ds(pl.multiple_of(tok * V, V), V)],
        teacher.at[pl.ds(pl.multiple_of(tok * R, R), R), :],
        local_sem.at[1],
    )
    own_block.start()

    def stage(buf, sems, slot, n, target):
        def c(i):
            return copy(buf.at[slot], buf.at[slot], sems, 0, target(i))

        def start():
            each(n, lambda i: c(i).start(), 1)

        def wait():
            join(buf.at[pl.ds(0, n - 1)], sems)

        return start, wait

    def three(voc_buf, y_buf, z_buf, voc_sem, y_sem, z_sem):
        return (
            stage(voc_buf, voc_sem, voc, NV, lambda i: at(dx=i // 2, dc=mod(i, 2))),
            stage(y_buf, y_sem, y, Y, lambda i: at(dy=i)),
            stage(z_buf, z_sem, z, Z, lambda i: at(dz=i)),
        )

    stat_stages = three(stat_voc, stat_y, stat_z, stat_voc_sem, stat_y_sem, stat_z_sem)
    mentor_stages = three(
        mentor_voc, mentor_y, mentor_z, mentor_voc_sem, mentor_y_sem, mentor_z_sem
    )
    loss_stages = three(loss_voc, loss_y, loss_z, loss_voc_sem, loss_y_sem, loss_z_sem)

    eye = lax.broadcasted_iota(jnp.int32, (q, LANES), 0) == lax.broadcasted_iota(
        jnp.int32, (q, LANES), 1
    )
    eye_rows = lax.broadcasted_iota(jnp.int32, (R, LANES), 0) == lax.broadcasted_iota(
        jnp.int32, (R, LANES), 1
    )

    def columns_of(i):
        return mentor[:, pl.ds(pl.multiple_of(i * V, V), V)].astype(F32) / TEMPERATURE

    def fold(op, value):
        total = value[:, :LANES]
        for j in range(1, V // LANES):
            total = op(total, value[:, j * LANES : (j + 1) * LANES])
        return total

    def to_lanes(column, mask):
        return jnp.sum(jnp.where(mask, column, 0.0), axis=0, keepdims=True)

    run_top[...] = jnp.full((R, LANES), -jnp.inf, F32)
    run_sum[...] = jnp.zeros((R, LANES), F32)

    def mentor_part(j):
        old = run_top[...]
        top = lax.fori_loop(
            j * Y, (j + 1) * Y, lambda i, m: jnp.maximum(m, fold(jnp.maximum, columns_of(i))), old
        )
        wide = jnp.concatenate([top] * (V // LANES), axis=1)
        run_sum[...] = lax.fori_loop(
            j * Y,
            (j + 1) * Y,
            lambda i, s: s + fold(jnp.add, jnp.exp(columns_of(i) - wide)),
            run_sum[...] * jnp.exp(old - top),
        )
        run_top[...] = top

    def mentor_done():
        top_t = jnp.max(run_top[...], axis=1, keepdims=True)
        sum_t = jnp.sum(run_sum[...] * jnp.exp(run_top[...] - top_t), axis=1, keepdims=True)
        mentor_voc[voc] = jnp.concatenate(
            [to_lanes(top_t, eye_rows), to_lanes(sum_t, eye_rows), jnp.zeros((6, LANES), F32)],
            axis=0,
        )
        mentor_stages[0][0]()

    def to_column(row):
        return jnp.sum(jnp.where(eye[:, : row.shape[1]], row, 0.0), axis=1, keepdims=True)

    def fill_picks(k):
        here = pl.ds(pl.multiple_of(k * CH, CH), CH)
        parts = [to_column(rows[pl.ds(k * nb + j, 1), :].astype(F32)) for j in range(nb)]
        wanted = jnp.concatenate(parts, axis=0).astype(jnp.int32)
        wanted_rows[here, :] = wanted
        places = lax.broadcasted_iota(jnp.int32, (CH, N), 1)
        picks[here, :] = jnp.where(places == wanted, 1.0, 0.0).astype(BF16)

    def mentor_second():
        mentor_stages[0][1]()
        tops = [mentor_voc[j, 0:1] for j in range(NV)]
        sums = [mentor_voc[j, 1:2] for j in range(NV)]
        top_t = functools.reduce(jnp.maximum, tops)
        sum_t = functools.reduce(jnp.add, [s * jnp.exp(m - top_t) for s, m in zip(sums, tops)])
        used = lax.broadcasted_iota(jnp.int32, (1, LANES), 1) < R
        sum_t = jnp.where(used, sum_t, 1.0)
        mentor_y[y] = jnp.concatenate([top_t, jnp.log(sum_t), jnp.zeros((6, LANES), F32)], axis=0)
        mentor_stages[1][0]()

    def mentor_third():
        mentor_stages[1][1]()
        for j in range(Y):
            mentor_z[z, j] = mentor_y[j]
        mentor_stages[2][0]()

    first, second = pl.ds(0, RA), pl.ds(RA, R - RA)
    stat_voc[voc] = jnp.zeros((2 * tiles, 8, LANES), F32)

    def away(j):
        return turns(mod(j + Z - 1, Z), Z)

    def chunk(j):
        return mod(z + Z - away(j), Z)

    def s2a(j, i):
        block = gathered.at[x, core, chunk(j), y, first]
        return copy(block, block, s2a_sem, j, at(dy=i))

    def s2b(j, i):
        block = gathered.at[x, core, chunk(j), y, second]
        return copy(block, block, s2b_sem, j, at(dx=i))

    def s3a(j, i):
        block = gathered.at[x, core, chunk(j), :, first]
        return copy(block, block, s3a_sem, j, at(dx=i))

    def s3b(j, i):
        block = gathered.at[:, core, chunk(j), y, second]
        return copy(block, block, s3b_sem, j, at(dy=i))

    def c(j):
        block = gathered.at[:, core, chunk(j)]
        return copy(block, block, c_sem, j, at(dc=1))

    def hidden_of(b, k):
        return gathered[b // 2, b % 2, k].reshape(CH, CS)

    def score(k):
        here = pl.ds(pl.multiple_of(k * CH, CH), CH)
        wide = jnp.concatenate([hidden_of(b, k) for b in range(NV)], axis=1)
        value = jnp.dot(wide, weights[...], preferred_element_type=F32) / TEMPERATURE
        scores[here, :] = value
        top = jnp.max(value, axis=1, keepdims=True)
        total = jnp.sum(jnp.exp(value - top), axis=1, keepdims=True)
        group = lax.broadcasted_iota(jnp.int32, (8, LANES), 0) // nb == mod(k, per_tile)

        def put(column, tile):
            parts = [to_lanes(column[j * q : (j + 1) * q], eye) for j in range(nb)]
            value = jnp.concatenate(parts * per_tile, axis=0)
            stat_voc[voc, tile] = jnp.where(group, value, stat_voc[voc, tile])

        put(top, k // per_tile)
        put(total, tiles + k // per_tile)

    def second_step(j):
        each(Y, lambda i: s2a(j, i).start(), 1)
        each(X, lambda i: s2b(j, i).start(), 1)

    def third_step(j):
        join(gathered.at[x, core, chunk(j), pl.ds(0, Y - 1), first], s2a_sem, j)
        each(X, lambda i: s3a(j, i).start(), 1)
        join(gathered.at[pl.ds(0, X - 1), core, chunk(j), y, second], s2b_sem, j)
        each(Y, lambda i: s3b(j, i).start(), 1)

    def fourth_step(j):
        join(gathered.at[pl.ds(0, X - 1), core, chunk(j), :, first], s3a_sem, j)
        join(gathered.at[:, core, chunk(j), pl.ds(0, Y - 1), second], s3b_sem, j)
        c(j).start()

    def last_step(j):
        c(j).wait()
        score(chunk(j))

    own_columns.wait()
    second_step(0)
    each(NT - 1, lambda i: t_copy(i).start())
    load_mentor.wait()
    each(Z // 2, mentor_part)
    third_step(0)
    each(Z, mentor_part, Z // 2)
    mentor_done()

    def on_first(j):
        s1(away(j)).wait()
        second_step(j)

    each(Z, on_first, 1)
    each(Z, third_step, 1)
    mentor_second()
    each(Z, fill_picks)
    mentor_third()
    load_weights.wait()
    fourth_step(0)

    def on_third(j):
        fourth_step(j)
        last_step(j - 1)

    each(Z, on_third, 1)
    last_step(Z - 1)

    def combine(buf, n):
        tops = [buf[j, :tiles] for j in range(n)]
        sums = [buf[j, tiles:] for j in range(n)]
        top = functools.reduce(jnp.maximum, tops)
        total = functools.reduce(jnp.add, [s * jnp.exp(m - top) for s, m in zip(sums, tops)])
        return top, total

    stat_stages[0][0]()
    stat_stages[0][1]()
    top_s, sum_s = combine(stat_voc, NV)
    stat_y[y, :tiles] = top_s
    stat_y[y, tiles:] = sum_s
    stat_stages[1][0]()
    stat_stages[1][1]()
    top_s, sum_s = combine(stat_y, Y)
    stat_z[z, :tiles] = top_s
    stat_z[z, tiles:] = sum_s
    stat_stages[2][0]()
    mentor_stages[2][1]()
    table_top = jnp.concatenate(
        [mentor_z[i, j, 0:1] for i in range(Z) for j in range(Y)], axis=0
    ).astype(BF16)
    table_log = jnp.concatenate(
        [mentor_z[i, j, 1:2] for i in range(Z) for j in range(Y)], axis=0
    )
    log_hi = table_log.astype(BF16)
    rest = table_log - log_hi.astype(F32)
    log_mid = rest.astype(BF16)
    log_lo = (rest - log_mid.astype(F32)).astype(BF16)
    stat_stages[2][1]()
    top_s, sum_s = combine(stat_z, Z)
    stat_voc[0, :tiles] = top_s
    stat_voc[0, tiles:] = jnp.log(jnp.where(sum_s > 0.0, sum_s, 1.0))

    ends = []
    total = jnp.int32(0)
    for j in range(lengths.shape[0]):
        total = total + lengths[j]
        ends.append(total - 1)

    own_block.wait()
    join(teacher.at[pl.ds(0, (NT - 1) * R), :], t_sem)

    def mate(k):
        return copy(mate_send.at[k], mate_recv.at[k], mate_sem, k, at(dc=1))

    def r1a(k, i):
        return copy(
            folded.at[k, :, mod(x + i, X), :, pl.ds(0, PA)],
            first_a.at[k, i - 1],
            r1a_sem,
            k,
            at(dx=i),
        )

    def r1b(k, i):
        return copy(
            folded.at[k, mod(y + i, Y), :, :, pl.ds(PA, PA)],
            first_b.at[k, i - 1],
            r1b_sem,
            k,
            at(dy=i),
        )

    def r1c(k):
        return copy(
            folded.at[k, :, :, :, pl.ds(2 * PA, PC)], first_c.at[k], r1c_sem, 0, at(dz=turns(k, Z))
        )

    loss_voc[voc] = jnp.zeros((8, LANES), F32)

    def gradient(k):
        zc = mod(z + turns(k, Z), Z)
        here = pl.ds(pl.multiple_of(zc * CH, CH), CH)
        wanted = wanted_rows[here, :]
        block = wanted // R
        pick = (lax.broadcasted_iota(jnp.int32, (CH, NT), 1) == block).astype(F32).astype(BF16)
        lane = lax.broadcasted_iota(jnp.int32, (CH, LANES), 1) == (wanted - block * R)

        def take(table):
            return jnp.dot(pick, table, preferred_element_type=F32)

        def one(value):
            return jnp.sum(jnp.where(lane, value, 0.0), axis=1, keepdims=True)

        teacher_top = one(take(table_top))
        teacher_log = one(take(log_hi) + take(log_mid) + take(log_lo))
        row_of = lax.broadcasted_iota(jnp.int32, (8, LANES), 0)

        def student(tile):
            value = stat_voc[0, tile + zc // per_tile]
            first_row = mod(zc, per_tile) * nb
            picked = [
                jnp.sum(jnp.where(row_of == first_row + j, value, 0.0), axis=0, keepdims=True)
                for j in range(nb)
            ]
            return jnp.concatenate([to_column(row) for row in picked], axis=0)

        student_top = student(0)
        student_log = student(tiles)
        place = lax.broadcasted_iota(jnp.int32, (CH, 1), 0) + zc * CH
        valid = jnp.ones((CH, 1), F32)
        for end in ends:
            valid = jnp.where(place == end, 0.0, valid)
        taken = jnp.dot(picks[here, :], teacher[...], preferred_element_type=F32) / TEMPERATURE
        log_teacher = (taken - teacher_top) - teacher_log
        log_student = (scores[here, :] - student_top) - student_log
        p_teacher = jnp.exp(log_teacher)
        p_student = jnp.exp(log_student)
        kl = jnp.sum(p_teacher * (log_teacher - log_student), axis=1, keepdims=True)
        grad = ((SCALE * TEMPERATURE) * valid * (p_student - p_teacher)).astype(BF16)
        slope[here, :] = grad

        def product(c):
            return lax.dot_general(
                grad,
                weights[pl.ds(pl.multiple_of(c * HALF, HALF), HALF), :],
                (((1,), (1,)), ((), ())),
                preferred_element_type=F32,
            )

        mate_send[k] = product(1 - core).astype(BF16)
        mate(k).start()
        own_half[mod(k, 2)] = product(core)
        loss_voc[voc] = loss_voc[voc] + jnp.sum(valid * kl, axis=0, keepdims=True)

    def fold_mate(k):
        mate(k).wait()
        value = own_half[mod(k, 2)] + mate_recv[k].astype(F32)
        folded[k] = value.astype(BF16).reshape(Y, X, 16, HALF)
        each(X, lambda i: r1a(k, i).start(), 1)
        each(Y, lambda i: r1b(k, i).start(), 1)

        @pl.when(k < Z - 1)
        def _():
            r1c(k).start()

    def weight_part(b):
        wide = gathered[b // 2, mod(b, 2)].reshape(N, CS)
        value = lax.dot_general(
            wide, slope[...], (((0,), (0,)), ((), ())), preferred_element_type=F32
        )
        grad_weight[pl.ds(pl.multiple_of(b * CS, CS), CS), :] = value.astype(BF16)

    def r2a(k, i):
        return copy(second_a.at[k, mod(y + i, Y)], got_a.at[k, i - 1], r2a_sem, k, at(dy=i))

    def r2b(k, i):
        return copy(second_b.at[k, mod(x + i, X)], got_b.at[k, i - 1], r2b_sem, k, at(dx=i))

    def add(value, others):
        for other in others:
            value = value + other.astype(F32)
        return value

    def fold_first(k):
        join(first_a.at[k], r1a_sem, k)
        value = folded[k, :, x, :, :PA].astype(F32)
        second_a[k] = add(value, [first_a[k, i] for i in range(X - 1)]).astype(BF16)
        each(Y, lambda i: r2a(k, i).start(), 1)
        join(first_b.at[k], r1b_sem, k)
        value = folded[k, y, :, :, PA : 2 * PA].astype(F32)
        second_b[k] = add(value, [first_b[k, i] for i in range(Y - 1)]).astype(BF16)
        each(X, lambda i: r2b(k, i).start(), 1)

    def fold_second(k):
        join(got_a.at[k], r2a_sem, k)
        join(got_b.at[k], r2b_sem, k)
        left = add(second_a[k, y].astype(F32), [got_a[k, i] for i in range(Y - 1)])
        right = add(second_b[k, x].astype(F32), [got_b[k, i] for i in range(X - 1)])
        for d in range(2):
            rows8 = slice(8 * d, 8 * d + 8)
            last[k, d] = jnp.concatenate([left[rows8], right[rows8]], axis=0).astype(BF16)

    def r2c(i):
        return copy(second_c.at[mod(y + i, Y)], got_c.at[i - 1], r2c_sem, 0, at(dy=i))

    def r3c(i):
        dx, dc = i // 2, mod(i, 2)
        return copy(
            third_c.at[mod(x + dx, X), mod(core + dc, 2)],
            got_d.at[2 * dx + core],
            r3c_sem,
            0,
            at(dx=dx, dc=dc),
        )

    def fold_first_c():
        join(first_c, r1c_sem)
        value = folded[Z - 1, :, :, :, 2 * PA :].astype(F32)
        second_c[...] = add(value, [first_c[k] for k in range(Z - 1)]).astype(BF16)
        each(Y, lambda i: r2c(i).start(), 1)

    def fold_second_c():
        join(got_c, r2c_sem)
        value = second_c[y].astype(F32)
        value = add(value, [got_c[i] for i in range(Y - 1)])
        for i in range(X):
            for d in range(2):
                part = value[i, 8 * d : 8 * d + 8]
                part = jnp.concatenate([part[:, : PC // 2], part[:, PC // 2 :]], axis=0)
                third_c[i, d] = part.astype(BF16)
        each(NV, lambda i: r3c(i).start(), 1)
        got_d[core] = third_c[x, core]

    def r3(k, dc):
        return copy(
            last.at[k, mod(core + dc, 2)],
            arrived.at[2 * k + core],
            r3_sem,
            0,
            at(dz=turns(k, Z), dc=dc),
        )

    def forward(j):
        @pl.when(j < Z)
        def _():
            gradient(j)

        @pl.when(j >= 1)
        def _():
            fold_mate(j - 1)

    each(Z + 1, forward)
    loss_stages[0][0]()
    PER = NV // (Z // 2)
    LAG = 2

    def backward(j):
        fold_first(j)

        @pl.when(j < Z // 2)
        def _():
            for i in range(PER):
                weight_part(j * PER + i)

        @pl.when(j == Z // 2 - 1)
        def _():
            loss_stages[0][1]()
            loss_y[y] = functools.reduce(jnp.add, [loss_voc[i] for i in range(NV)])
            loss_stages[1][0]()

        @pl.when(j == Z - 2)
        def _():
            loss_stages[1][1]()
            loss_z[z] = functools.reduce(jnp.add, [loss_y[i] for i in range(Y)])
            loss_stages[2][0]()

        @pl.when(j >= LAG)
        def _():
            fold_second(j - LAG)
            r3(j - LAG, 0).start()
            r3(j - LAG, 1).start()

    each(Z, backward)
    fold_first_c()
    store_weight = pltpu.make_async_copy(grad_weight, grad_weight_hbm, local_sem.at[0])
    store_weight.start()
    fold_second(Z - 2)
    r3(Z - 2, 0).start()
    r3(Z - 2, 1).start()
    fold_second(Z - 1)
    r3(Z - 1, 1).start()
    arrived[2 * (Z - 1) + core] = last[Z - 1, core]
    fold_second_c()
    loss_stages[2][1]()
    loss = functools.reduce(jnp.add, [loss_z[j] for j in range(Z)])
    loss_out[0, 0] = jnp.max(TEMPERATURE * TEMPERATURE * loss / (N - lengths.shape[0]))
    join(arrived.at[pl.ds(0, 2 * Z - 1)], r3_sem)
    join(got_d.at[pl.ds(0, NV - 1)], r3c_sem)
    for d in range(2):
        value = add(arrived[d].astype(F32), [arrived[2 * k + d] for k in range(1, Z)])
        right = add(got_d[d].astype(F32), [got_d[2 * i + d] for i in range(1, X)])
        parts = [value[:8], value[8:], right[:8], right[8:]]
        grad_hidden[:, d * HALF : (d + 1) * HALF] = jnp.concatenate(parts, axis=1).astype(BF16)
    store_weight.wait()


def body(dims, hidden, weights, mentor, rows, lengths):
    Z, Y, X, R, V, D = dims
    NT, NV, CH = Z * Y, X * 2, Y * R
    N, HALF, CS = Z * CH, D // 2, D // NV
    PC = HALF // 4
    PA = (HALF - PC) // 2
    vmem = pl.BlockSpec(memory_space=pltpu.VMEM)
    anywhere = pl.BlockSpec(memory_space=pl.ANY)
    nb = max(1, CH // LANES)
    tiles = max(1, Z * nb // 8)
    dma = lambda n: pltpu.SemaphoreType.DMA((2, n))
    loss, grad_hidden, grad_weight = pl.pallas_call(
        functools.partial(kernel, dims),
        out_shape=(
            jax.ShapeDtypeStruct((1, 1), F32),
            jax.ShapeDtypeStruct((8, D), BF16),
            jax.ShapeDtypeStruct((D, V), BF16),
        ),
        in_specs=[anywhere, anywhere, anywhere, vmem, pl.BlockSpec(memory_space=pltpu.SMEM)],
        out_specs=(pl.BlockSpec(memory_space=pltpu.SMEM), vmem, anywhere),
        scratch_shapes=[
            pltpu.VMEM((D, V), BF16),
            pltpu.VMEM((D, V), BF16),
            pltpu.VMEM((R, V * NT), BF16),
            pltpu.VMEM((N, 1), jnp.int32),
            pltpu.VMEM((R, LANES), F32),
            pltpu.VMEM((R, LANES), F32),
            pltpu.VMEM((X, 2, Z, Y, R, CS), BF16),
            pltpu.VMEM((N, V), BF16),
            pltpu.VMEM((N, N), BF16),
            pltpu.VMEM((N, V), F32),
            pltpu.VMEM((N, V), BF16),
            pltpu.VMEM((Z, CH, HALF), BF16),
            pltpu.VMEM((Z, CH, HALF), BF16),
            pltpu.VMEM((2, CH, HALF), F32),
            pltpu.VMEM((Z, Y, X, 16, HALF), BF16),
            pltpu.VMEM((Z, X - 1, Y, 16, PA), BF16),
            pltpu.VMEM((Z, Y - 1, X, 16, PA), BF16),
            pltpu.VMEM((Z, Y, 16, PA), BF16),
            pltpu.VMEM((Z, X, 16, PA), BF16),
            pltpu.VMEM((Z, Y - 1, 16, PA), BF16),
            pltpu.VMEM((Z, X - 1, 16, PA), BF16),
            pltpu.VMEM((Z - 1, Y, X, 16, PC), BF16),
            pltpu.VMEM((Y, X, 16, PC), BF16),
            pltpu.VMEM((Y - 1, X, 16, PC), BF16),
            pltpu.VMEM((X, 2, 16, PC // 2), BF16),
            pltpu.VMEM((NV, 16, PC // 2), BF16),
            pltpu.VMEM((Z, 2, 16, PA), BF16),
            pltpu.VMEM((2 * Z, 16, PA), BF16),
            pltpu.VMEM((NV, 2 * tiles, 8, LANES), F32),
            pltpu.VMEM((Y, 2 * tiles, 8, LANES), F32),
            pltpu.VMEM((Z, 2 * tiles, 8, LANES), F32),
            pltpu.VMEM((NV, 8, LANES), F32),
            pltpu.VMEM((Y, 8, LANES), F32),
            pltpu.VMEM((Z, Y, 8, LANES), F32),
            pltpu.VMEM((NV, 8, LANES), F32),
            pltpu.VMEM((Y, 8, LANES), F32),
            pltpu.VMEM((Z, 8, LANES), F32),
            pltpu.SemaphoreType.DMA((4,)),
            dma(Z),
            dma(1),
            dma(Z),
            dma(Z),
            dma(Z),
            dma(Z),
            dma(Z),
            dma(1),
            dma(1),
            dma(1),
            dma(1),
            dma(1),
            dma(1),
            dma(1),
            dma(1),
            dma(1),
            dma(Z),
            dma(Z),
            dma(Z),
            dma(Z),
            dma(Z),
            dma(1),
            dma(1),
            dma(1),
            dma(1),
        ],
        compiler_params=pltpu.CompilerParams(
            collective_id=0, has_side_effects=True, vmem_limit_bytes=63 * 2**20
        ),
    )(hidden, weights, mentor, rows.reshape(Z * nb, CH // nb), lengths)
    return loss.reshape(()), grad_hidden, grad_weight


def solution(mesh):
    NT, NV = mesh.shape["tok"], mesh.shape["voc"]
    Y = 1 << ((NT.bit_length() - 1) // 2)
    Z, X = NT // Y, NV // 2

    def run(hidden, weights, mentor, rows, lengths):
        N, D = hidden.shape
        dims = (Z, Y, X, N // NT, weights.shape[1] // (NT * NV), D)
        return jax.shard_map(
            functools.partial(body, dims),
            mesh=mesh,
            in_specs=(P("tok", None), P(None, ("voc", "tok")), P("tok", "voc"), P(), P()),
            out_specs=(P(), P(("tok", "voc"), None), P(None, ("voc", "tok"))),
            check_vma=False,
        )(hidden, weights, mentor, rows, lengths)

    return run
```

```python
import functools

import jax
import jax.numpy as jnp
from jax import lax
from jax.experimental import pallas as pl
from jax.experimental.pallas import tpu as pltpu
from jax.sharding import PartitionSpec as P

MESH = pl.DeviceIdType.MESH
F32 = jnp.float32
BF16 = jnp.bfloat16
TEMPERATURE = 2.0
SCALE = 512.0
LANES = 128


def mod(a, n):
    return lax.rem(a, n)


def kernel(
    dims,
    hidden,
    weights_hbm,
    mentor_hbm,
    rows,
    lengths,
    loss_out,
    grad_hidden,
    grad_weight,
    weights,
    mentor,
    wanted_rows,
    run_top,
    run_sum,
    gathered,
    teacher,
    picks,
    scores,
    mentor_top,
    mentor_log,
    weight_of,
    slope,
    mate_send,
    mate_recv,
    own_half,
    folded,
    first_a,
    first_b,
    second_a,
    second_b,
    got_a,
    got_b,
    first_c,
    second_c,
    got_c,
    third_c,
    got_d,
    last,
    arrived,
    stat_voc,
    stat_y,
    stat_z,
    mentor_voc,
    mentor_y,
    mentor_z,
    loss_voc,
    loss_y,
    loss_z,
    local_sem,
    s1_sem,
    t_sem,
    s2a_sem,
    s2b_sem,
    s3a_sem,
    s3b_sem,
    c_sem,
    stat_voc_sem,
    stat_y_sem,
    stat_z_sem,
    mentor_voc_sem,
    mentor_y_sem,
    mentor_z_sem,
    loss_voc_sem,
    loss_y_sem,
    loss_z_sem,
    mate_sem,
    r1a_sem,
    r1b_sem,
    r2a_sem,
    r2b_sem,
    r1c_sem,
    r2c_sem,
    r3c_sem,
    r3_sem,
):
    Z, Y, X, R, V, D = dims
    tok, voc = lax.axis_index("tok"), lax.axis_index("voc")
    z, y = tok // Y, mod(tok, Y)
    x, core = voc // 2, mod(voc, 2)
    NT, NV = Z * Y, X * 2
    CH = Y * R
    N = Z * CH
    HALF = D // 2
    PC = HALF // 4
    PA = (HALF - PC) // 2
    CS = D // NV
    RA = (3 * R // 4) // 16 * 16
    nb = max(1, CH // LANES)
    q = CH // nb
    per_tile = 8 // nb
    tiles = max(1, Z // per_tile)

    def at(dz=0, dy=0, dx=0, dc=0):
        return (
            mod(z + dz, Z) * Y + mod(y + dy, Y),
            mod(x + dx, X) * 2 + mod(core + dc, 2),
        )

    def copy(src, dst, sems, index, device):
        return pltpu.make_async_remote_copy(
            src_ref=src,
            dst_ref=dst,
            send_sem=sems.at[0, index],
            recv_sem=sems.at[1, index],
            device_id=device,
            device_id_type=MESH,
        )

    def join(block, sems, index=0):
        copy(block, block, sems, index, at(dc=1)).wait()

    def each(n, body, start=0):
        def step(i, carry):
            body(i)
            return carry

        lax.fori_loop(start, n, step, 0)

    load_mentor = pltpu.make_async_copy(mentor_hbm, mentor, local_sem.at[2])
    load_weights = pltpu.make_async_copy(weights_hbm, weights, local_sem.at[3])
    load_mentor.start()
    load_weights.start()

    def turns(i, n):
        return jnp.where(mod(i, 2) == 1, n // 2 - (i + 1) // 2, n // 2 + i // 2)

    barrier = pltpu.get_barrier_semaphore()

    def greet_tok(i):
        pl.semaphore_signal(barrier, inc=1, device_id=at(dz=i // Y, dy=mod(i, Y)), device_id_type=MESH)

    def greet_voc(i):
        pl.semaphore_signal(barrier, inc=1, device_id=at(dx=i // 2, dc=mod(i, 2)), device_id_type=MESH)

    def greet_cross(i):
        pl.semaphore_signal(barrier, inc=1, device_id=at(dz=i, dc=1), device_id_type=MESH)

    each(NT, greet_tok, 1)
    each(NV, greet_voc, 1)
    each(Z, greet_cross, 1)
    pl.semaphore_wait(barrier, NT - 1 + NV - 1 + Z - 1)

    def s1(i):
        return copy(
            hidden.at[:, pl.ds(pl.multiple_of(voc * CS, CS), CS)],
            gathered.at[x, core, z, y],
            s1_sem,
            i,
            at(dz=i),
        )

    each(Z - 1, lambda i: s1(turns(i, Z)).start())
    own_columns = pltpu.make_async_copy(
        hidden.at[:, pl.ds(pl.multiple_of(voc * CS, CS), CS)],
        gathered.at[x, core, z, y],
        local_sem.at[0],
    )
    own_columns.start()

    def t_copy(i):
        device = at(dz=turns(i // Y, Z), dy=turns(mod(i, Y), Y))
        return copy(
            mentor_hbm.at[:, pl.ds(pl.multiple_of(device[0] * V, V), V)],
            teacher.at[pl.ds(pl.multiple_of(tok * R, R), R), :],
            t_sem,
            0,
            device,
        )

    own_block = pltpu.make_async_copy(
        mentor_hbm.at[:, pl.ds(pl.multiple_of(tok * V, V), V)],
        teacher.at[pl.ds(pl.multiple_of(tok * R, R), R), :],
        local_sem.at[1],
    )
    own_block.start()

    def stage(buf, sems, slot, n, target):
        def c(i):
            return copy(buf.at[slot], buf.at[slot], sems, 0, target(i))

        def start():
            each(n, lambda i: c(i).start(), 1)

        def wait():
            join(buf.at[pl.ds(0, n - 1)], sems)

        return start, wait

    def three(voc_buf, y_buf, z_buf, voc_sem, y_sem, z_sem):
        return (
            stage(voc_buf, voc_sem, voc, NV, lambda i: at(dx=i // 2, dc=mod(i, 2))),
            stage(y_buf, y_sem, y, Y, lambda i: at(dy=i)),
            stage(z_buf, z_sem, z, Z, lambda i: at(dz=i)),
        )

    stat_stages = three(stat_voc, stat_y, stat_z, stat_voc_sem, stat_y_sem, stat_z_sem)
    mentor_stages = three(
        mentor_voc, mentor_y, mentor_z, mentor_voc_sem, mentor_y_sem, mentor_z_sem
    )
    loss_stages = three(loss_voc, loss_y, loss_z, loss_voc_sem, loss_y_sem, loss_z_sem)

    eye = lax.broadcasted_iota(jnp.int32, (q, LANES), 0) == lax.broadcasted_iota(
        jnp.int32, (q, LANES), 1
    )
    eye_rows = lax.broadcasted_iota(jnp.int32, (R, LANES), 0) == lax.broadcasted_iota(
        jnp.int32, (R, LANES), 1
    )

    def columns_of(i):
        return mentor[:, pl.ds(pl.multiple_of(i * V, V), V)].astype(F32) / TEMPERATURE

    def fold(op, value):
        total = value[:, :LANES]
        for j in range(1, V // LANES):
            total = op(total, value[:, j * LANES : (j + 1) * LANES])
        return total

    def to_lanes(column, mask):
        return jnp.sum(jnp.where(mask, column, 0.0), axis=0, keepdims=True)

    run_top[...] = jnp.full((R, LANES), -jnp.inf, F32)
    run_sum[...] = jnp.zeros((R, LANES), F32)

    def mentor_part(j):
        old = run_top[...]
        top = lax.fori_loop(
            j * Y, (j + 1) * Y, lambda i, m: jnp.maximum(m, fold(jnp.maximum, columns_of(i))), old
        )
        wide = jnp.concatenate([top] * (V // LANES), axis=1)
        run_sum[...] = lax.fori_loop(
            j * Y,
            (j + 1) * Y,
            lambda i, s: s + fold(jnp.add, jnp.exp(columns_of(i) - wide)),
            run_sum[...] * jnp.exp(old - top),
        )
        run_top[...] = top

    def mentor_done():
        top_t = jnp.max(run_top[...], axis=1, keepdims=True)
        sum_t = jnp.sum(run_sum[...] * jnp.exp(run_top[...] - top_t), axis=1, keepdims=True)
        mentor_voc[voc] = jnp.concatenate(
            [to_lanes(top_t, eye_rows), to_lanes(sum_t, eye_rows), jnp.zeros((6, LANES), F32)],
            axis=0,
        )
        mentor_stages[0][0]()

    def to_column(row):
        return jnp.sum(jnp.where(eye[:, : row.shape[1]], row, 0.0), axis=1, keepdims=True)

    def fill_picks(k):
        here = pl.ds(pl.multiple_of(k * CH, CH), CH)
        parts = [to_column(rows[pl.ds(k * nb + j, 1), :].astype(F32)) for j in range(nb)]
        wanted = jnp.concatenate(parts, axis=0).astype(jnp.int32)
        wanted_rows[here, :] = wanted
        places = lax.broadcasted_iota(jnp.int32, (CH, N), 1)
        picks[here, :] = jnp.where(places == wanted, 1.0, 0.0).astype(BF16)

    def mentor_second():
        mentor_stages[0][1]()
        tops = [mentor_voc[j, 0:1] for j in range(NV)]
        sums = [mentor_voc[j, 1:2] for j in range(NV)]
        top_t = functools.reduce(jnp.maximum, tops)
        sum_t = functools.reduce(jnp.add, [s * jnp.exp(m - top_t) for s, m in zip(sums, tops)])
        used = lax.broadcasted_iota(jnp.int32, (1, LANES), 1) < R
        sum_t = jnp.where(used, sum_t, 1.0)
        mentor_y[y] = jnp.concatenate([top_t, jnp.log(sum_t), jnp.zeros((6, LANES), F32)], axis=0)
        mentor_stages[1][0]()

    def mentor_third():
        mentor_stages[1][1]()
        for j in range(Y):
            mentor_z[z, j] = mentor_y[j]
        mentor_stages[2][0]()

    first, second = pl.ds(0, RA), pl.ds(RA, R - RA)
    stat_voc[voc] = jnp.zeros((2 * tiles, 8, LANES), F32)

    def away(j):
        return turns(mod(j + Z - 1, Z), Z)

    def chunk(j):
        return mod(z + Z - away(j), Z)

    def s2a(j, i):
        block = gathered.at[x, core, chunk(j), y, first]
        return copy(block, block, s2a_sem, j, at(dy=i))

    def s2b(j, i):
        block = gathered.at[x, core, chunk(j), y, second]
        return copy(block, block, s2b_sem, j, at(dx=i))

    def s3a(j, i):
        block = gathered.at[x, core, chunk(j), :, first]
        return copy(block, block, s3a_sem, j, at(dx=i))

    def s3b(j, i):
        block = gathered.at[:, core, chunk(j), y, second]
        return copy(block, block, s3b_sem, j, at(dy=i))

    def c(j):
        block = gathered.at[:, core, chunk(j)]
        return copy(block, block, c_sem, j, at(dc=1))

    def hidden_of(b, k):
        return gathered[b // 2, b % 2, k].reshape(CH, CS)

    def score(k):
        here = pl.ds(pl.multiple_of(k * CH, CH), CH)
        wide = jnp.concatenate([hidden_of(b, k) for b in range(NV)], axis=1)
        value = jnp.dot(wide, weights[...], preferred_element_type=F32) / TEMPERATURE
        scores[here, :] = value
        top = jnp.max(value, axis=1, keepdims=True)
        total = jnp.sum(jnp.exp(value - top), axis=1, keepdims=True)
        group = lax.broadcasted_iota(jnp.int32, (8, LANES), 0) // nb == mod(k, per_tile)

        def put(column, tile):
            parts = [to_lanes(column[j * q : (j + 1) * q], eye) for j in range(nb)]
            value = jnp.concatenate(parts * per_tile, axis=0)
            stat_voc[voc, tile] = jnp.where(group, value, stat_voc[voc, tile])

        put(top, k // per_tile)
        put(total, tiles + k // per_tile)

    def second_step(j):
        each(Y, lambda i: s2a(j, i).start(), 1)
        each(X, lambda i: s2b(j, i).start(), 1)

    def third_step(j):
        join(gathered.at[x, core, chunk(j), pl.ds(0, Y - 1), first], s2a_sem, j)
        each(X, lambda i: s3a(j, i).start(), 1)
        join(gathered.at[pl.ds(0, X - 1), core, chunk(j), y, second], s2b_sem, j)
        each(Y, lambda i: s3b(j, i).start(), 1)

    def fourth_step(j):
        join(gathered.at[pl.ds(0, X - 1), core, chunk(j), :, first], s3a_sem, j)
        join(gathered.at[:, core, chunk(j), pl.ds(0, Y - 1), second], s3b_sem, j)
        c(j).start()

    def last_step(j):
        c(j).wait()
        score(chunk(j))

    own_columns.wait()
    second_step(0)
    each(NT - 1, lambda i: t_copy(i).start())
    load_mentor.wait()
    each(Z // 2, mentor_part)
    third_step(0)
    each(Z, mentor_part, Z // 2)
    mentor_done()

    def on_first(j):
        s1(away(j)).wait()
        second_step(j)

    each(Z, on_first, 1)
    each(Z, third_step, 1)
    mentor_second()
    each(Z, fill_picks)
    mentor_third()
    load_weights.wait()
    fourth_step(0)

    def on_third(j):
        fourth_step(j)
        last_step(j - 1)

    each(Z, on_third, 1)
    last_step(Z - 1)

    def combine(buf, n):
        tops = [buf[j, :tiles] for j in range(n)]
        sums = [buf[j, tiles:] for j in range(n)]
        top = functools.reduce(jnp.maximum, tops)
        total = functools.reduce(jnp.add, [s * jnp.exp(m - top) for s, m in zip(sums, tops)])
        return top, total

    stat_stages[0][0]()
    stat_stages[0][1]()
    top_s, sum_s = combine(stat_voc, NV)
    stat_y[y, :tiles] = top_s
    stat_y[y, tiles:] = sum_s
    stat_stages[1][0]()
    stat_stages[1][1]()
    top_s, sum_s = combine(stat_y, Y)
    stat_z[z, :tiles] = top_s
    stat_z[z, tiles:] = sum_s
    stat_stages[2][0]()
    mentor_stages[2][1]()
    table_top = jnp.concatenate(
        [mentor_z[i, j, 0:1] for i in range(Z) for j in range(Y)], axis=0
    ).astype(BF16)
    table_log = jnp.concatenate(
        [mentor_z[i, j, 1:2] for i in range(Z) for j in range(Y)], axis=0
    )
    log_hi = table_log.astype(BF16)
    rest = table_log - log_hi.astype(F32)
    log_mid = rest.astype(BF16)
    log_lo = (rest - log_mid.astype(F32)).astype(BF16)

    ends = []
    total = jnp.int32(0)
    for j in range(lengths.shape[0]):
        total = total + lengths[j]
        ends.append(total - 1)

    def prepare(k):
        here = pl.ds(pl.multiple_of(k * CH, CH), CH)
        wanted = wanted_rows[here, :]
        block = wanted // R
        pick = (lax.broadcasted_iota(jnp.int32, (CH, NT), 1) == block).astype(F32).astype(BF16)
        lane = lax.broadcasted_iota(jnp.int32, (CH, LANES), 1) == (wanted - block * R)

        def take(table):
            return jnp.dot(pick, table, preferred_element_type=F32)

        def one(value):
            return jnp.sum(jnp.where(lane, value, 0.0), axis=1, keepdims=True)

        teacher_top = one(take(table_top))
        teacher_log = one(take(log_hi) + take(log_mid) + take(log_lo))
        place = lax.broadcasted_iota(jnp.int32, (CH, 1), 0) + k * CH
        valid = jnp.ones((CH, 1), F32)
        for end in ends:
            valid = jnp.where(place == end, 0.0, valid)
        mentor_top[here, :] = teacher_top
        mentor_log[here, :] = teacher_log
        weight_of[here, :] = valid

    each(Z, prepare)
    stat_stages[2][1]()
    top_s, sum_s = combine(stat_z, Z)
    stat_voc[0, :tiles] = top_s
    stat_voc[0, tiles:] = jnp.log(jnp.where(sum_s > 0.0, sum_s, 1.0))

    own_block.wait()
    join(teacher.at[pl.ds(0, (NT - 1) * R), :], t_sem)

    def mate(k):
        return copy(mate_send.at[k], mate_recv.at[k], mate_sem, k, at(dc=1))

    def r1a(k, i):
        return copy(
            folded.at[k, :, mod(x + i, X), :, pl.ds(0, PA)],
            first_a.at[k, i - 1],
            r1a_sem,
            k,
            at(dx=i),
        )

    def r1b(k, i):
        return copy(
            folded.at[k, mod(y + i, Y), :, :, pl.ds(PA, PA)],
            first_b.at[k, i - 1],
            r1b_sem,
            k,
            at(dy=i),
        )

    def r1c(k):
        return copy(
            folded.at[k, :, :, :, pl.ds(2 * PA, PC)], first_c.at[k], r1c_sem, 0, at(dz=turns(k, Z))
        )

    loss_voc[voc] = jnp.zeros((8, LANES), F32)

    def gradient(k):
        zc = mod(z + turns(k, Z), Z)
        here = pl.ds(pl.multiple_of(zc * CH, CH), CH)
        row_of = lax.broadcasted_iota(jnp.int32, (8, LANES), 0)

        def student(tile):
            value = stat_voc[0, tile + zc // per_tile]
            first_row = mod(zc, per_tile) * nb
            picked = [
                jnp.sum(jnp.where(row_of == first_row + j, value, 0.0), axis=0, keepdims=True)
                for j in range(nb)
            ]
            return jnp.concatenate([to_column(row) for row in picked], axis=0)

        student_top = student(0)
        student_log = student(tiles)
        valid = weight_of[here, :]
        taken = jnp.dot(picks[here, :], teacher[...], preferred_element_type=F32) / TEMPERATURE
        log_teacher = (taken - mentor_top[here, :]) - mentor_log[here, :]
        log_student = (scores[here, :] - student_top) - student_log
        p_teacher = jnp.exp(log_teacher)
        p_student = jnp.exp(log_student)
        kl = jnp.sum(p_teacher * (log_teacher - log_student), axis=1, keepdims=True)
        grad = ((SCALE * TEMPERATURE) * valid * (p_student - p_teacher)).astype(BF16)
        slope[here, :] = grad

        def product(c):
            return lax.dot_general(
                grad,
                weights[pl.ds(pl.multiple_of(c * HALF, HALF), HALF), :],
                (((1,), (1,)), ((), ())),
                preferred_element_type=F32,
            )

        mate_send[k] = product(1 - core).astype(BF16)
        mate(k).start()
        own_half[mod(k, 2)] = product(core)
        loss_voc[voc] = loss_voc[voc] + jnp.sum(valid * kl, axis=0, keepdims=True)

    def fold_mate(k):
        mate(k).wait()
        value = own_half[mod(k, 2)] + mate_recv[k].astype(F32)
        folded[k] = value.astype(BF16).reshape(Y, X, 16, HALF)
        @pl.when(k < Z - 1)
        def _():
            r1c(k).start()

        each(X, lambda i: r1a(k, i).start(), 1)
        each(Y, lambda i: r1b(k, i).start(), 1)

    def weight_part(b):
        wide = gathered[b // 2, mod(b, 2)].reshape(N, CS)
        value = lax.dot_general(
            wide, slope[...], (((0,), (0,)), ((), ())), preferred_element_type=F32
        )
        here = pl.ds(pl.multiple_of(b * CS, CS), CS)
        grad_weight[here, :] = value.astype(BF16)

    def r2a(k, i):
        return copy(second_a.at[k, mod(y + i, Y)], got_a.at[k, i - 1], r2a_sem, k, at(dy=i))

    def r2b(k, i):
        return copy(second_b.at[k, mod(x + i, X)], got_b.at[k, i - 1], r2b_sem, k, at(dx=i))

    def add(value, others):
        for other in others:
            value = value + other.astype(F32)
        return value

    def fold_first(k):
        join(first_a.at[k], r1a_sem, k)
        value = folded[k, :, x, :, :PA].astype(F32)
        second_a[k] = add(value, [first_a[k, i] for i in range(X - 1)]).astype(BF16)
        each(Y, lambda i: r2a(k, i).start(), 1)
        join(first_b.at[k], r1b_sem, k)
        value = folded[k, y, :, :, PA : 2 * PA].astype(F32)
        second_b[k] = add(value, [first_b[k, i] for i in range(Y - 1)]).astype(BF16)
        each(X, lambda i: r2b(k, i).start(), 1)

    def fold_second(k):
        join(got_a.at[k], r2a_sem, k)
        join(got_b.at[k], r2b_sem, k)
        left = add(second_a[k, y].astype(F32), [got_a[k, i] for i in range(Y - 1)])
        right = add(second_b[k, x].astype(F32), [got_b[k, i] for i in range(X - 1)])
        for d in range(2):
            rows8 = slice(8 * d, 8 * d + 8)
            last[k, d] = jnp.concatenate([left[rows8], right[rows8]], axis=0).astype(BF16)

    def r2c(i):
        return copy(second_c.at[mod(y + i, Y)], got_c.at[i - 1], r2c_sem, 0, at(dy=i))

    def r3c(i):
        dx, dc = i // 2, mod(i, 2)
        return copy(
            third_c.at[mod(x + dx, X), mod(core + dc, 2)],
            got_d.at[2 * dx + core],
            r3c_sem,
            0,
            at(dx=dx, dc=dc),
        )

    def fold_first_c():
        join(first_c, r1c_sem)
        value = folded[Z - 1, :, :, :, 2 * PA :].astype(F32)
        second_c[...] = add(value, [first_c[k] for k in range(Z - 1)]).astype(BF16)
        each(Y, lambda i: r2c(i).start(), 1)

    def fold_second_c():
        join(got_c, r2c_sem)
        value = second_c[y].astype(F32)
        value = add(value, [got_c[i] for i in range(Y - 1)])
        for i in range(X):
            for d in range(2):
                part = value[i, 8 * d : 8 * d + 8]
                part = jnp.concatenate([part[:, : PC // 2], part[:, PC // 2 :]], axis=0)
                third_c[i, d] = part.astype(BF16)
        each(NV, lambda i: r3c(i).start(), 1)
        got_d[core] = third_c[x, core]

    def r3(k, dc):
        return copy(
            last.at[k, mod(core + dc, 2)],
            arrived.at[2 * k + core],
            r3_sem,
            0,
            at(dz=turns(k, Z), dc=dc),
        )

    def forward(j):
        @pl.when(j < Z)
        def _():
            gradient(j)

        @pl.when(j >= 1)
        def _():
            fold_mate(j - 1)

    each(Z + 1, forward)
    loss_stages[0][0]()
    PER = NV // Z
    LAG = 2

    def backward(j):
        fold_first(j)

        @pl.when(j < Z // 2)
        def _():
            for i in range(PER):
                weight_part(j * PER + i)

        @pl.when(j == Z // 2 - 1)
        def _():
            loss_stages[0][1]()
            loss_y[y] = functools.reduce(jnp.add, [loss_voc[i] for i in range(NV)])
            loss_stages[1][0]()

        @pl.when(j == Z - 2)
        def _():
            loss_stages[1][1]()
            loss_z[z] = functools.reduce(jnp.add, [loss_y[i] for i in range(Y)])
            loss_stages[2][0]()

        @pl.when(j >= LAG)
        def _():
            fold_second(j - LAG)
            r3(j - LAG, 0).start()
            r3(j - LAG, 1).start()

    each(Z, backward)
    fold_first_c()
    each(3 * NV // 4, weight_part, NV // 2)
    fold_second(Z - 2)
    r3(Z - 2, 0).start()
    r3(Z - 2, 1).start()
    fold_second(Z - 1)
    r3(Z - 1, 1).start()
    arrived[2 * (Z - 1) + core] = last[Z - 1, core]
    fold_second_c()
    each(NV, weight_part, 3 * NV // 4)
    loss_stages[2][1]()
    loss = functools.reduce(jnp.add, [loss_z[j] for j in range(Z)])
    loss_out[0, 0] = jnp.max(TEMPERATURE * TEMPERATURE * loss / (N - lengths.shape[0]))
    join(arrived.at[pl.ds(0, 2 * Z - 1)], r3_sem)
    join(got_d.at[pl.ds(0, NV - 1)], r3c_sem)
    for d in range(2):
        value = add(arrived[d].astype(F32), [arrived[2 * k + d] for k in range(1, Z)])
        right = add(got_d[d].astype(F32), [got_d[2 * i + d] for i in range(1, X)])
        parts = [value[:8], value[8:], right[:8], right[8:]]
        grad_hidden[:, d * HALF : (d + 1) * HALF] = jnp.concatenate(parts, axis=1).astype(BF16)


def body(dims, hidden, weights, mentor, rows, lengths):
    Z, Y, X, R, V, D = dims
    NT, NV, CH = Z * Y, X * 2, Y * R
    N, HALF, CS = Z * CH, D // 2, D // NV
    PC = HALF // 4
    PA = (HALF - PC) // 2
    vmem = pl.BlockSpec(memory_space=pltpu.VMEM)
    anywhere = pl.BlockSpec(memory_space=pl.ANY)
    nb = max(1, CH // LANES)
    tiles = max(1, Z * nb // 8)
    dma = lambda n: pltpu.SemaphoreType.DMA((2, n))
    loss, grad_hidden, grad_weight = pl.pallas_call(
        functools.partial(kernel, dims),
        out_shape=(
            jax.ShapeDtypeStruct((1, 1), F32),
            pltpu.VMEM((8, D), BF16),
            pltpu.VMEM((D, V), BF16),
        ),
        in_specs=[anywhere, anywhere, anywhere, vmem, pl.BlockSpec(memory_space=pltpu.SMEM)],
        out_specs=(pl.BlockSpec(memory_space=pltpu.SMEM), vmem, vmem),
        scratch_shapes=[
            pltpu.VMEM((D, V), BF16),
            pltpu.VMEM((R, V * NT), BF16),
            pltpu.VMEM((N, 1), jnp.int32),
            pltpu.VMEM((R, LANES), F32),
            pltpu.VMEM((R, LANES), F32),
            pltpu.VMEM((X, 2, Z, Y, R, CS), BF16),
            pltpu.VMEM((N, V), BF16),
            pltpu.VMEM((N, N), BF16),
            pltpu.VMEM((N, V), F32),
            pltpu.VMEM((N, 1), F32),
            pltpu.VMEM((N, 1), F32),
            pltpu.VMEM((N, 1), F32),
            pltpu.VMEM((N, V), BF16),
            pltpu.VMEM((Z, CH, HALF), BF16),
            pltpu.VMEM((Z, CH, HALF), BF16),
            pltpu.VMEM((2, CH, HALF), F32),
            pltpu.VMEM((Z, Y, X, 16, HALF), BF16),
            pltpu.VMEM((Z, X - 1, Y, 16, PA), BF16),
            pltpu.VMEM((Z, Y - 1, X, 16, PA), BF16),
            pltpu.VMEM((Z, Y, 16, PA), BF16),
            pltpu.VMEM((Z, X, 16, PA), BF16),
            pltpu.VMEM((Z, Y - 1, 16, PA), BF16),
            pltpu.VMEM((Z, X - 1, 16, PA), BF16),
            pltpu.VMEM((Z - 1, Y, X, 16, PC), BF16),
            pltpu.VMEM((Y, X, 16, PC), BF16),
            pltpu.VMEM((Y - 1, X, 16, PC), BF16),
            pltpu.VMEM((X, 2, 16, PC // 2), BF16),
            pltpu.VMEM((NV, 16, PC // 2), BF16),
            pltpu.VMEM((Z, 2, 16, PA), BF16),
            pltpu.VMEM((2 * Z, 16, PA), BF16),
            pltpu.VMEM((NV, 2 * tiles, 8, LANES), F32),
            pltpu.VMEM((Y, 2 * tiles, 8, LANES), F32),
            pltpu.VMEM((Z, 2 * tiles, 8, LANES), F32),
            pltpu.VMEM((NV, 8, LANES), F32),
            pltpu.VMEM((Y, 8, LANES), F32),
            pltpu.VMEM((Z, Y, 8, LANES), F32),
            pltpu.VMEM((NV, 8, LANES), F32),
            pltpu.VMEM((Y, 8, LANES), F32),
            pltpu.VMEM((Z, 8, LANES), F32),
            pltpu.SemaphoreType.DMA((4,)),
            dma(Z),
            dma(1),
            dma(Z),
            dma(Z),
            dma(Z),
            dma(Z),
            dma(Z),
            dma(1),
            dma(1),
            dma(1),
            dma(1),
            dma(1),
            dma(1),
            dma(1),
            dma(1),
            dma(1),
            dma(Z),
            dma(Z),
            dma(Z),
            dma(Z),
            dma(Z),
            dma(1),
            dma(1),
            dma(1),
            dma(1),
        ],
        compiler_params=pltpu.CompilerParams(
            collective_id=0, has_side_effects=True, vmem_limit_bytes=57 * 2**20
        ),
    )(hidden, weights, mentor, rows.reshape(Z * nb, CH // nb), lengths)
    return loss.reshape(()), grad_hidden, grad_weight


def solution(mesh):
    NT, NV = mesh.shape["tok"], mesh.shape["voc"]
    Y = 1 << ((NT.bit_length() - 1) // 2)
    Z, X = NT // Y, NV // 2

    def run(hidden, weights, mentor, rows, lengths):
        N, D = hidden.shape
        dims = (Z, Y, X, N // NT, weights.shape[1] // (NT * NV), D)
        return jax.shard_map(
            functools.partial(body, dims),
            mesh=mesh,
            in_specs=(P("tok", None), P(None, ("voc", "tok")), P("tok", "voc"), P(), P()),
            out_specs=(P(), P(("tok", "voc"), None), P(None, ("voc", "tok"))),
            check_vma=False,
        )(hidden, weights, mentor, rows, lengths)

    return run
```

```python
import functools

import jax
import jax.numpy as jnp
from jax import lax
from jax.experimental import pallas as pl
from jax.experimental.pallas import tpu as pltpu
from jax.sharding import PartitionSpec as P

MESH = pl.DeviceIdType.MESH
F32 = jnp.float32
BF16 = jnp.bfloat16
TEMPERATURE = 2.0
SCALE = 512.0
LANES = 128


def mod(a, n):
    return lax.rem(a, n)


def kernel(
    dims,
    hidden,
    weights_hbm,
    mentor_hbm,
    rows,
    lengths,
    loss_out,
    grad_hidden,
    grad_weight,
    weights,
    mentor,
    wanted_rows,
    run_top,
    run_sum,
    gathered,
    teacher,
    picks,
    scores,
    mentor_top,
    mentor_log,
    weight_of,
    slope,
    mate_send,
    mate_recv,
    own_half,
    folded,
    first_a,
    first_b,
    second_a,
    second_b,
    got_a,
    got_b,
    first_c,
    second_c,
    got_c,
    third_c,
    got_d,
    last,
    arrived,
    stat_voc,
    stat_y,
    stat_z,
    mentor_voc,
    mentor_y,
    mentor_z,
    loss_voc,
    loss_y,
    loss_z,
    local_sem,
    s1_sem,
    t_sem,
    s2a_sem,
    s2b_sem,
    s3a_sem,
    s3b_sem,
    c_sem,
    stat_voc_sem,
    stat_y_sem,
    stat_z_sem,
    mentor_voc_sem,
    mentor_y_sem,
    mentor_z_sem,
    loss_voc_sem,
    loss_y_sem,
    loss_z_sem,
    mate_sem,
    r1a_sem,
    r1b_sem,
    r2a_sem,
    r2b_sem,
    r1c_sem,
    r2c_sem,
    r3c_sem,
    r3_sem,
):
    Z, Y, X, R, V, D = dims
    tok, voc = lax.axis_index("tok"), lax.axis_index("voc")
    z, y = tok // Y, mod(tok, Y)
    x, core = voc // 2, mod(voc, 2)
    NT, NV = Z * Y, X * 2
    CH = Y * R
    N = Z * CH
    HALF = D // 2
    PC = HALF // 4
    PA = (HALF - PC) // 2
    CS = D // NV
    RA = (3 * R // 4) // 16 * 16
    nb = max(1, CH // LANES)
    q = CH // nb
    per_tile = 8 // nb
    tiles = max(1, Z // per_tile)

    def at(dz=0, dy=0, dx=0, dc=0):
        return (
            mod(z + dz, Z) * Y + mod(y + dy, Y),
            mod(x + dx, X) * 2 + mod(core + dc, 2),
        )

    def copy(src, dst, sems, index, device):
        return pltpu.make_async_remote_copy(
            src_ref=src,
            dst_ref=dst,
            send_sem=sems.at[0, index],
            recv_sem=sems.at[1, index],
            device_id=device,
            device_id_type=MESH,
        )

    def join(block, sems, index=0):
        copy(block, block, sems, index, at(dc=1)).wait()

    def each(n, body, start=0):
        def step(i, carry):
            body(i)
            return carry

        lax.fori_loop(start, n, step, 0)

    load_mentor = pltpu.make_async_copy(mentor_hbm, mentor, local_sem.at[2])
    load_weights = pltpu.make_async_copy(weights_hbm, weights, local_sem.at[3])
    load_mentor.start()
    load_weights.start()

    def turns(i, n):
        return jnp.where(mod(i, 2) == 1, n // 2 - (i + 1) // 2, n // 2 + i // 2)

    barrier = pltpu.get_barrier_semaphore()

    def greet_tok(i):
        pl.semaphore_signal(barrier, inc=1, device_id=at(dz=i // Y, dy=mod(i, Y)), device_id_type=MESH)

    def greet_voc(i):
        pl.semaphore_signal(barrier, inc=1, device_id=at(dx=i // 2, dc=mod(i, 2)), device_id_type=MESH)

    def greet_cross(i):
        pl.semaphore_signal(barrier, inc=1, device_id=at(dz=i, dc=1), device_id_type=MESH)

    each(NT, greet_tok, 1)
    each(NV, greet_voc, 1)
    each(Z, greet_cross, 1)
    pl.semaphore_wait(barrier, NT - 1 + NV - 1 + Z - 1)

    def s1(i):
        return copy(
            hidden.at[:, pl.ds(pl.multiple_of(voc * CS, CS), CS)],
            gathered.at[x, core, z, y],
            s1_sem,
            i,
            at(dz=i),
        )

    each(Z - 1, lambda i: s1(turns(i, Z)).start())
    own_columns = pltpu.make_async_copy(
        hidden.at[:, pl.ds(pl.multiple_of(voc * CS, CS), CS)],
        gathered.at[x, core, z, y],
        local_sem.at[0],
    )
    own_columns.start()

    def t_copy(i):
        device = at(dz=turns(i // Y, Z), dy=turns(mod(i, Y), Y))
        return copy(
            mentor_hbm.at[:, pl.ds(pl.multiple_of(device[0] * V, V), V)],
            teacher.at[pl.ds(pl.multiple_of(tok * R, R), R), :],
            t_sem,
            0,
            device,
        )

    own_block = pltpu.make_async_copy(
        mentor_hbm.at[:, pl.ds(pl.multiple_of(tok * V, V), V)],
        teacher.at[pl.ds(pl.multiple_of(tok * R, R), R), :],
        local_sem.at[1],
    )
    own_block.start()

    def stage(buf, sems, slot, n, target):
        def c(i):
            return copy(buf.at[slot], buf.at[slot], sems, 0, target(i))

        def start():
            each(n, lambda i: c(i).start(), 1)

        def wait():
            join(buf.at[pl.ds(0, n - 1)], sems)

        return start, wait

    def three(voc_buf, y_buf, z_buf, voc_sem, y_sem, z_sem):
        return (
            stage(voc_buf, voc_sem, voc, NV, lambda i: at(dx=i // 2, dc=mod(i, 2))),
            stage(y_buf, y_sem, y, Y, lambda i: at(dy=i)),
            stage(z_buf, z_sem, z, Z, lambda i: at(dz=turns(i - 1, Z))),
        )

    stat_stages = three(stat_voc, stat_y, stat_z, stat_voc_sem, stat_y_sem, stat_z_sem)
    mentor_stages = three(
        mentor_voc, mentor_y, mentor_z, mentor_voc_sem, mentor_y_sem, mentor_z_sem
    )
    loss_stages = three(loss_voc, loss_y, loss_z, loss_voc_sem, loss_y_sem, loss_z_sem)

    eye = lax.broadcasted_iota(jnp.int32, (q, LANES), 0) == lax.broadcasted_iota(
        jnp.int32, (q, LANES), 1
    )
    eye_rows = lax.broadcasted_iota(jnp.int32, (R, LANES), 0) == lax.broadcasted_iota(
        jnp.int32, (R, LANES), 1
    )

    def columns_of(i):
        return mentor[:, pl.ds(pl.multiple_of(i * V, V), V)].astype(F32) / TEMPERATURE

    def fold(op, value):
        total = value[:, :LANES]
        for j in range(1, V // LANES):
            total = op(total, value[:, j * LANES : (j + 1) * LANES])
        return total

    def to_lanes(column, mask):
        return jnp.sum(jnp.where(mask, column, 0.0), axis=0, keepdims=True)

    run_top[...] = jnp.full((R, LANES), -jnp.inf, F32)
    run_sum[...] = jnp.zeros((R, LANES), F32)

    def mentor_part(j):
        old = run_top[...]
        top = lax.fori_loop(
            j * Y, (j + 1) * Y, lambda i, m: jnp.maximum(m, fold(jnp.maximum, columns_of(i))), old
        )
        wide = jnp.concatenate([top] * (V // LANES), axis=1)
        run_sum[...] = lax.fori_loop(
            j * Y,
            (j + 1) * Y,
            lambda i, s: s + fold(jnp.add, jnp.exp(columns_of(i) - wide)),
            run_sum[...] * jnp.exp(old - top),
        )
        run_top[...] = top

    def mentor_done():
        top_t = jnp.max(run_top[...], axis=1, keepdims=True)
        sum_t = jnp.sum(run_sum[...] * jnp.exp(run_top[...] - top_t), axis=1, keepdims=True)
        mentor_voc[voc] = jnp.concatenate(
            [to_lanes(top_t, eye_rows), to_lanes(sum_t, eye_rows), jnp.zeros((6, LANES), F32)],
            axis=0,
        )
        mentor_stages[0][0]()

    def to_column(row):
        return jnp.sum(jnp.where(eye[:, : row.shape[1]], row, 0.0), axis=1, keepdims=True)

    def fill_picks(k):
        here = pl.ds(pl.multiple_of(k * CH, CH), CH)
        parts = [to_column(rows[pl.ds(k * nb + j, 1), :].astype(F32)) for j in range(nb)]
        wanted = jnp.concatenate(parts, axis=0).astype(jnp.int32)
        wanted_rows[here, :] = wanted
        places = lax.broadcasted_iota(jnp.int32, (CH, N), 1)
        picks[here, :] = jnp.where(places == wanted, 1.0, 0.0).astype(BF16)

    def mentor_second():
        mentor_stages[0][1]()
        tops = [mentor_voc[j, 0:1] for j in range(NV)]
        sums = [mentor_voc[j, 1:2] for j in range(NV)]
        top_t = functools.reduce(jnp.maximum, tops)
        sum_t = functools.reduce(jnp.add, [s * jnp.exp(m - top_t) for s, m in zip(sums, tops)])
        used = lax.broadcasted_iota(jnp.int32, (1, LANES), 1) < R
        sum_t = jnp.where(used, sum_t, 1.0)
        mentor_y[y] = jnp.concatenate([top_t, jnp.log(sum_t), jnp.zeros((6, LANES), F32)], axis=0)
        mentor_stages[1][0]()

    def mentor_third():
        mentor_stages[1][1]()
        for j in range(Y):
            mentor_z[z, j] = mentor_y[j]
        mentor_stages[2][0]()

    first, second = pl.ds(0, RA), pl.ds(RA, R - RA)
    stat_voc[voc] = jnp.zeros((2 * tiles, 8, LANES), F32)

    def away(j):
        return turns(mod(j + Z - 1, Z), Z)

    def chunk(j):
        return mod(z + Z - away(j), Z)

    def s2a(j, i):
        block = gathered.at[x, core, chunk(j), y, first]
        return copy(block, block, s2a_sem, j, at(dy=i))

    def s2b(j, i):
        block = gathered.at[x, core, chunk(j), y, second]
        return copy(block, block, s2b_sem, j, at(dx=i))

    def s3a(j, i):
        block = gathered.at[x, core, chunk(j), :, first]
        return copy(block, block, s3a_sem, j, at(dx=i))

    def s3b(j, i):
        block = gathered.at[:, core, chunk(j), y, second]
        return copy(block, block, s3b_sem, j, at(dy=i))

    def c(j):
        block = gathered.at[:, core, chunk(j)]
        return copy(block, block, c_sem, j, at(dc=1))

    def hidden_of(b, k):
        return gathered[b // 2, b % 2, k].reshape(CH, CS)

    def score(k):
        here = pl.ds(pl.multiple_of(k * CH, CH), CH)
        wide = jnp.concatenate([hidden_of(b, k) for b in range(NV)], axis=1)
        value = jnp.dot(wide, weights[...], preferred_element_type=F32) / TEMPERATURE
        scores[here, :] = value
        top = jnp.max(value, axis=1, keepdims=True)
        total = jnp.sum(jnp.exp(value - top), axis=1, keepdims=True)
        group = lax.broadcasted_iota(jnp.int32, (8, LANES), 0) // nb == mod(k, per_tile)

        def put(column, tile):
            parts = [to_lanes(column[j * q : (j + 1) * q], eye) for j in range(nb)]
            value = jnp.concatenate(parts * per_tile, axis=0)
            stat_voc[voc, tile] = jnp.where(group, value, stat_voc[voc, tile])

        put(top, k // per_tile)
        put(total, tiles + k // per_tile)

    def second_step(j):
        each(Y, lambda i: s2a(j, i).start(), 1)
        each(X, lambda i: s2b(j, i).start(), 1)

    def third_step(j):
        join(gathered.at[x, core, chunk(j), pl.ds(0, Y - 1), first], s2a_sem, j)
        each(X, lambda i: s3a(j, i).start(), 1)
        join(gathered.at[pl.ds(0, X - 1), core, chunk(j), y, second], s2b_sem, j)
        each(Y, lambda i: s3b(j, i).start(), 1)

    def fourth_step(j):
        join(gathered.at[pl.ds(0, X - 1), core, chunk(j), :, first], s3a_sem, j)
        join(gathered.at[:, core, chunk(j), pl.ds(0, Y - 1), second], s3b_sem, j)
        c(j).start()

    def last_step(j):
        c(j).wait()
        score(chunk(j))

    own_columns.wait()
    second_step(0)
    each(NT - 1, lambda i: t_copy(i).start())
    load_mentor.wait()
    each(Z // 2, mentor_part)
    third_step(0)
    each(Z, mentor_part, Z // 2)
    mentor_done()

    def on_first(j):
        s1(away(j)).wait()
        second_step(j)

    each(Z, on_first, 1)
    each(Z, third_step, 1)
    mentor_second()
    each(Z, fill_picks)
    mentor_third()
    load_weights.wait()
    fourth_step(0)

    def on_third(j):
        fourth_step(j)
        last_step(j - 1)

    each(Z, on_third, 1)
    last_step(Z - 1)

    def combine(buf, n):
        tops = [buf[j, :tiles] for j in range(n)]
        sums = [buf[j, tiles:] for j in range(n)]
        top = functools.reduce(jnp.maximum, tops)
        total = functools.reduce(jnp.add, [s * jnp.exp(m - top) for s, m in zip(sums, tops)])
        return top, total

    stat_stages[0][0]()
    stat_stages[0][1]()
    top_s, sum_s = combine(stat_voc, NV)
    stat_y[y, :tiles] = top_s
    stat_y[y, tiles:] = sum_s
    stat_stages[1][0]()
    stat_stages[1][1]()
    top_s, sum_s = combine(stat_y, Y)
    stat_z[z, :tiles] = top_s
    stat_z[z, tiles:] = sum_s
    stat_stages[2][0]()
    mentor_stages[2][1]()
    table_top = jnp.concatenate(
        [mentor_z[i, j, 0:1] for i in range(Z) for j in range(Y)], axis=0
    ).astype(BF16)
    table_log = jnp.concatenate(
        [mentor_z[i, j, 1:2] for i in range(Z) for j in range(Y)], axis=0
    )
    log_hi = table_log.astype(BF16)
    rest = table_log - log_hi.astype(F32)
    log_mid = rest.astype(BF16)
    log_lo = (rest - log_mid.astype(F32)).astype(BF16)

    ends = []
    total = jnp.int32(0)
    for j in range(lengths.shape[0]):
        total = total + lengths[j]
        ends.append(total - 1)

    def prepare(k):
        here = pl.ds(pl.multiple_of(k * CH, CH), CH)
        wanted = wanted_rows[here, :]
        block = wanted // R
        pick = (lax.broadcasted_iota(jnp.int32, (CH, NT), 1) == block).astype(F32).astype(BF16)
        lane = lax.broadcasted_iota(jnp.int32, (CH, LANES), 1) == (wanted - block * R)

        def take(table):
            return jnp.dot(pick, table, preferred_element_type=F32)

        def one(value):
            return jnp.sum(jnp.where(lane, value, 0.0), axis=1, keepdims=True)

        teacher_top = one(take(table_top))
        teacher_log = one(take(log_hi) + take(log_mid) + take(log_lo))
        place = lax.broadcasted_iota(jnp.int32, (CH, 1), 0) + k * CH
        valid = jnp.ones((CH, 1), F32)
        for end in ends:
            valid = jnp.where(place == end, 0.0, valid)
        mentor_top[here, :] = teacher_top
        mentor_log[here, :] = teacher_log
        weight_of[here, :] = valid

    each(Z, prepare)
    stat_stages[2][1]()
    top_s, sum_s = combine(stat_z, Z)
    stat_voc[0, :tiles] = top_s
    stat_voc[0, tiles:] = jnp.log(jnp.where(sum_s > 0.0, sum_s, 1.0))

    own_block.wait()
    join(teacher.at[pl.ds(0, (NT - 1) * R), :], t_sem)

    def mate(k):
        return copy(mate_send.at[k], mate_recv.at[k], mate_sem, k, at(dc=1))

    def r1a(k, i):
        return copy(
            folded.at[k, :, mod(x + i, X), :, pl.ds(0, PA)],
            first_a.at[k, i - 1],
            r1a_sem,
            k,
            at(dx=i),
        )

    def r1b(k, i):
        return copy(
            folded.at[k, mod(y + i, Y), :, :, pl.ds(PA, PA)],
            first_b.at[k, i - 1],
            r1b_sem,
            k,
            at(dy=i),
        )

    def r1c(k):
        return copy(
            folded.at[k, :, :, :, pl.ds(2 * PA, PC)], first_c.at[k], r1c_sem, 0, at(dz=turns(k, Z))
        )

    loss_voc[voc] = jnp.zeros((8, LANES), F32)

    def gradient(k):
        zc = mod(z + turns(k, Z), Z)
        here = pl.ds(pl.multiple_of(zc * CH, CH), CH)
        row_of = lax.broadcasted_iota(jnp.int32, (8, LANES), 0)

        def student(tile):
            value = stat_voc[0, tile + zc // per_tile]
            first_row = mod(zc, per_tile) * nb
            picked = [
                jnp.sum(jnp.where(row_of == first_row + j, value, 0.0), axis=0, keepdims=True)
                for j in range(nb)
            ]
            return jnp.concatenate([to_column(row) for row in picked], axis=0)

        student_top = student(0)
        student_log = student(tiles)
        valid = weight_of[here, :]
        taken = jnp.dot(picks[here, :], teacher[...], preferred_element_type=F32) / TEMPERATURE
        log_teacher = (taken - mentor_top[here, :]) - mentor_log[here, :]
        log_student = (scores[here, :] - student_top) - student_log
        p_teacher = jnp.exp(log_teacher)
        p_student = jnp.exp(log_student)
        kl = jnp.sum(p_teacher * (log_teacher - log_student), axis=1, keepdims=True)
        grad = ((SCALE * TEMPERATURE) * valid * (p_student - p_teacher)).astype(BF16)
        slope[here, :] = grad

        def product(c):
            return lax.dot_general(
                grad,
                weights[pl.ds(pl.multiple_of(c * HALF, HALF), HALF), :],
                (((1,), (1,)), ((), ())),
                preferred_element_type=F32,
            )

        mate_send[k] = product(1 - core).astype(BF16)
        mate(k).start()
        own_half[mod(k, 2)] = product(core)
        loss_voc[voc] = loss_voc[voc] + jnp.sum(valid * kl, axis=0, keepdims=True)

    def fold_mate(k):
        mate(k).wait()
        value = own_half[mod(k, 2)] + mate_recv[k].astype(F32)
        folded[k] = value.astype(BF16).reshape(Y, X, 16, HALF)
        @pl.when(k < Z - 1)
        def _():
            r1c(k).start()

        each(X, lambda i: r1a(k, i).start(), 1)
        each(Y, lambda i: r1b(k, i).start(), 1)

    def weight_part(b):
        wide = gathered[b // 2, mod(b, 2)].reshape(N, CS)
        value = lax.dot_general(
            wide, slope[...], (((0,), (0,)), ((), ())), preferred_element_type=F32
        )
        here = pl.ds(pl.multiple_of(b * CS, CS), CS)
        grad_weight[here, :] = value.astype(BF16)

    def r2a(k, i):
        return copy(second_a.at[k, mod(y + i, Y)], got_a.at[k, i - 1], r2a_sem, k, at(dy=i))

    def r2b(k, i):
        return copy(second_b.at[k, mod(x + i, X)], got_b.at[k, i - 1], r2b_sem, k, at(dx=i))

    def add(value, others):
        for other in others:
            value = value + other.astype(F32)
        return value

    def fold_first(k):
        join(first_a.at[k], r1a_sem, k)
        value = folded[k, :, x, :, :PA].astype(F32)
        second_a[k] = add(value, [first_a[k, i] for i in range(X - 1)]).astype(BF16)
        each(Y, lambda i: r2a(k, i).start(), 1)
        join(first_b.at[k], r1b_sem, k)
        value = folded[k, y, :, :, PA : 2 * PA].astype(F32)
        second_b[k] = add(value, [first_b[k, i] for i in range(Y - 1)]).astype(BF16)
        each(X, lambda i: r2b(k, i).start(), 1)

    def fold_second(k):
        join(got_a.at[k], r2a_sem, k)
        join(got_b.at[k], r2b_sem, k)
        left = add(second_a[k, y].astype(F32), [got_a[k, i] for i in range(Y - 1)])
        right = add(second_b[k, x].astype(F32), [got_b[k, i] for i in range(X - 1)])
        for d in range(2):
            rows8 = slice(8 * d, 8 * d + 8)
            last[k, d] = jnp.concatenate([left[rows8], right[rows8]], axis=0).astype(BF16)

    def r2c(i):
        return copy(second_c.at[mod(y + i, Y)], got_c.at[i - 1], r2c_sem, 0, at(dy=i))

    def r3c(i):
        dx, dc = i // 2, mod(i, 2)
        return copy(
            third_c.at[mod(x + dx, X), mod(core + dc, 2)],
            got_d.at[2 * dx + core],
            r3c_sem,
            0,
            at(dx=dx, dc=dc),
        )

    def fold_first_c():
        join(first_c, r1c_sem)
        value = folded[Z - 1, :, :, :, 2 * PA :].astype(F32)
        second_c[...] = add(value, [first_c[k] for k in range(Z - 1)]).astype(BF16)
        each(Y, lambda i: r2c(i).start(), 1)

    def fold_second_c():
        join(got_c, r2c_sem)
        value = second_c[y].astype(F32)
        value = add(value, [got_c[i] for i in range(Y - 1)])
        for i in range(X):
            for d in range(2):
                part = value[i, 8 * d : 8 * d + 8]
                part = jnp.concatenate([part[:, : PC // 2], part[:, PC // 2 :]], axis=0)
                third_c[i, d] = part.astype(BF16)
        each(NV, lambda i: r3c(i).start(), 1)
        got_d[core] = third_c[x, core]

    def r3(k, dc):
        return copy(
            last.at[k, mod(core + dc, 2)],
            arrived.at[2 * k + core],
            r3_sem,
            0,
            at(dz=turns(k, Z), dc=dc),
        )

    def forward(j):
        @pl.when(j < Z)
        def _():
            gradient(j)

        @pl.when(j >= 1)
        def _():
            fold_mate(j - 1)

    each(Z + 1, forward)
    loss_stages[0][0]()
    PER = NV // Z
    LAG = 2

    def backward(j):
        fold_first(j)

        @pl.when(j < Z // 2)
        def _():
            for i in range(PER):
                weight_part(j * PER + i)

        @pl.when(j == Z // 2 - 1)
        def _():
            loss_stages[0][1]()
            loss_y[y] = functools.reduce(jnp.add, [loss_voc[i] for i in range(NV)])
            loss_stages[1][0]()

        @pl.when(j == Z - 2)
        def _():
            loss_stages[1][1]()
            loss_z[z] = functools.reduce(jnp.add, [loss_y[i] for i in range(Y)])
            loss_stages[2][0]()

        @pl.when(j >= LAG)
        def _():
            fold_second(j - LAG)
            r3(j - LAG, 0).start()
            r3(j - LAG, 1).start()

    each(Z, backward)
    fold_first_c()
    each(3 * NV // 4, weight_part, NV // 2)
    fold_second(Z - 2)
    r3(Z - 2, 0).start()
    r3(Z - 2, 1).start()
    fold_second(Z - 1)
    r3(Z - 1, 1).start()
    arrived[2 * (Z - 1) + core] = last[Z - 1, core]
    fold_second_c()
    each(NV, weight_part, 3 * NV // 4)
    loss_stages[2][1]()
    loss = functools.reduce(jnp.add, [loss_z[j] for j in range(Z)])
    loss_out[0, 0] = jnp.max(TEMPERATURE * TEMPERATURE * loss / (N - lengths.shape[0]))
    join(arrived.at[pl.ds(0, 2 * Z - 1)], r3_sem)
    join(got_d.at[pl.ds(0, NV - 1)], r3c_sem)
    for d in range(2):
        value = add(arrived[d].astype(F32), [arrived[2 * k + d] for k in range(1, Z)])
        right = add(got_d[d].astype(F32), [got_d[2 * i + d] for i in range(1, X)])
        parts = [value[:8], value[8:], right[:8], right[8:]]
        grad_hidden[:, d * HALF : (d + 1) * HALF] = jnp.concatenate(parts, axis=1).astype(BF16)


def body(dims, hidden, weights, mentor, rows, lengths):
    Z, Y, X, R, V, D = dims
    NT, NV, CH = Z * Y, X * 2, Y * R
    N, HALF, CS = Z * CH, D // 2, D // NV
    PC = HALF // 4
    PA = (HALF - PC) // 2
    vmem = pl.BlockSpec(memory_space=pltpu.VMEM)
    anywhere = pl.BlockSpec(memory_space=pl.ANY)
    nb = max(1, CH // LANES)
    tiles = max(1, Z * nb // 8)
    dma = lambda n: pltpu.SemaphoreType.DMA((2, n))
    loss, grad_hidden, grad_weight = pl.pallas_call(
        functools.partial(kernel, dims),
        out_shape=(
            jax.ShapeDtypeStruct((1, 1), F32),
            pltpu.VMEM((8, D), BF16),
            pltpu.VMEM((D, V), BF16),
        ),
        in_specs=[anywhere, anywhere, anywhere, vmem, pl.BlockSpec(memory_space=pltpu.SMEM)],
        out_specs=(pl.BlockSpec(memory_space=pltpu.SMEM), vmem, vmem),
        scratch_shapes=[
            pltpu.VMEM((D, V), BF16),
            pltpu.VMEM((R, V * NT), BF16),
            pltpu.VMEM((N, 1), jnp.int32),
            pltpu.VMEM((R, LANES), F32),
            pltpu.VMEM((R, LANES), F32),
            pltpu.VMEM((X, 2, Z, Y, R, CS), BF16),
            pltpu.VMEM((N, V), BF16),
            pltpu.VMEM((N, N), BF16),
            pltpu.VMEM((N, V), F32),
            pltpu.VMEM((N, 1), F32),
            pltpu.VMEM((N, 1), F32),
            pltpu.VMEM((N, 1), F32),
            pltpu.VMEM((N, V), BF16),
            pltpu.VMEM((Z, CH, HALF), BF16),
            pltpu.VMEM((Z, CH, HALF), BF16),
            pltpu.VMEM((2, CH, HALF), F32),
            pltpu.VMEM((Z, Y, X, 16, HALF), BF16),
            pltpu.VMEM((Z, X - 1, Y, 16, PA), BF16),
            pltpu.VMEM((Z, Y - 1, X, 16, PA), BF16),
            pltpu.VMEM((Z, Y, 16, PA), BF16),
            pltpu.VMEM((Z, X, 16, PA), BF16),
            pltpu.VMEM((Z, Y - 1, 16, PA), BF16),
            pltpu.VMEM((Z, X - 1, 16, PA), BF16),
            pltpu.VMEM((Z - 1, Y, X, 16, PC), BF16),
            pltpu.VMEM((Y, X, 16, PC), BF16),
            pltpu.VMEM((Y - 1, X, 16, PC), BF16),
            pltpu.VMEM((X, 2, 16, PC // 2), BF16),
            pltpu.VMEM((NV, 16, PC // 2), BF16),
            pltpu.VMEM((Z, 2, 16, PA), BF16),
            pltpu.VMEM((2 * Z, 16, PA), BF16),
            pltpu.VMEM((NV, 2 * tiles, 8, LANES), F32),
            pltpu.VMEM((Y, 2 * tiles, 8, LANES), F32),
            pltpu.VMEM((Z, 2 * tiles, 8, LANES), F32),
            pltpu.VMEM((NV, 8, LANES), F32),
            pltpu.VMEM((Y, 8, LANES), F32),
            pltpu.VMEM((Z, Y, 8, LANES), F32),
            pltpu.VMEM((NV, 8, LANES), F32),
            pltpu.VMEM((Y, 8, LANES), F32),
            pltpu.VMEM((Z, 8, LANES), F32),
            pltpu.SemaphoreType.DMA((4,)),
            dma(Z),
            dma(1),
            dma(Z),
            dma(Z),
            dma(Z),
            dma(Z),
            dma(Z),
            dma(1),
            dma(1),
            dma(1),
            dma(1),
            dma(1),
            dma(1),
            dma(1),
            dma(1),
            dma(1),
            dma(Z),
            dma(Z),
            dma(Z),
            dma(Z),
            dma(Z),
            dma(1),
            dma(1),
            dma(1),
            dma(1),
        ],
        compiler_params=pltpu.CompilerParams(
            collective_id=0, has_side_effects=True, vmem_limit_bytes=57 * 2**20
        ),
    )(hidden, weights, mentor, rows.reshape(Z * nb, CH // nb), lengths)
    return loss.reshape(()), grad_hidden, grad_weight


def solution(mesh):
    NT, NV = mesh.shape["tok"], mesh.shape["voc"]
    Y = 1 << ((NT.bit_length() - 1) // 2)
    Z, X = NT // Y, NV // 2

    def run(hidden, weights, mentor, rows, lengths):
        N, D = hidden.shape
        dims = (Z, Y, X, N // NT, weights.shape[1] // (NT * NV), D)
        return jax.shard_map(
            functools.partial(body, dims),
            mesh=mesh,
            in_specs=(P("tok", None), P(None, ("voc", "tok")), P("tok", "voc"), P(), P()),
            out_specs=(P(), P(("tok", "voc"), None), P(None, ("voc", "tok"))),
            check_vma=False,
        )(hidden, weights, mentor, rows, lengths)

    return run
```
